32 devices in a mesh: dp: 2 (over y), seq: 16 (over z, x, core).
Axes of the slice: x: 2, y: 2, z: 4, core: 2. Of those that a mesh axis runs over, the one named last changes fastest.
Arguments:
- tokens: bfloat16 [2, 2, 1024, 1024], P(None, 'dp', 'seq'), may hold values from -6 to 6
- cotangent: bfloat16 [2, 2, 1024, 1024], P(None, 'dp', 'seq'), may hold values from -6 to 6
- w_query: bfloat16 [1024, 2048], replicated, may hold values from -0.1875 to 0.1875
- w_key: bfloat16 [1024, 1024], replicated, may hold values from -0.1875 to 0.1875
- w_value: bfloat16 [1024, 1024], replicated, may hold values from -0.1875 to 0.1875
- w_out: bfloat16 [2048, 1024], replicated, may hold values from -0.125 to 0.125
- q_gain: float32 [2048], replicated, may hold values from 0.25 to 1.75
- k_gain: float32 [1024], replicated, may hold values from 0.25 to 1.75
- attn_gain: float32 [1024], replicated, may hold values from 0.25 to 1.75
- w_gate: bfloat16 [1024, 3072], replicated, may hold values from -0.1875 to 0.1875
- w_up: bfloat16 [1024, 3072], replicated, may hold values from -0.1875 to 0.1875
- w_down: bfloat16 [3072, 1024], replicated, may hold values from -0.109375 to 0.109375
- mlp_gain: float32 [1024], replicated, may hold values from 0.25 to 1.75
- doc_lengths: int32 [2, 2, 2], P(None, 'dp'), may hold values from 0 to 1024, as said below
- block_order: int32 [16], replicated, may hold values from 0 to 15, each once
Outputs:
- layer_out: bfloat16 [2, 2, 1024, 1024], P(None, 'dp', 'seq')
- input_grad: float32 [2, 2, 1024, 1024], P(None, 'dp', 'seq')
- grad_w_query: float32 [1024, 2048], P(('dp', 'seq'))
- grad_w_key: float32 [1024, 1024], P(('dp', 'seq'))
- grad_w_value: float32 [1024, 1024], P(('dp', 'seq'))
- grad_w_out: float32 [2048, 1024], P(('dp', 'seq'))
- grad_q_gain: float32 [2048], P(('dp', 'seq'))
- grad_k_gain: float32 [1024], P(('dp', 'seq'))
- grad_attn_gain: float32 [1024], P(('dp', 'seq'))
- grad_w_gate: float32 [1024, 3072], P(('dp', 'seq'))
- grad_w_up: float32 [1024, 3072], P(('dp', 'seq'))
- grad_w_down: float32 [3072, 1024], P(('dp', 'seq'))
- grad_mlp_gain: float32 [1024], P(('dp', 'seq'))
The draws below stay inside these ranges and needn't reach their ends.
Inputs may be any that keep to these rules, and one draw needn't show every extreme that they name: Row r of micro-batch b holds two documents in order: positions 0 to doc_lengths[b, r, 0] - 1 and the rest; the two lengths sum to 1024. For every r exactly one micro-batch holds a single document of 1024 positions (second length 0); in the others the first length lies between 256 and 768. Layout positions j * 64 to (j + 1) * 64 - 1 of every row hold the positions block_order[j] * 64 onward, in order; each block appears once.
All inputs are finite; a program needn't handle non-finite values.
Results may differ from the reference program's by a relative error of at most 0.015.
Values may be sent and summed in bfloat16 or wider, within the bound.
A program may use at most 256 MiB of HBM per device.

```python
import jax
import jax.numpy as jnp
from jax import lax

D = 1024
HEADS = 16
KV_HEADS = 8
HD = 128
FF = 3072
QD = 2048
KVD = 1024
MICRO = 2
TOK_BLK = 64
BATCH = 2
BLOCKS = 16
SEQ = 1024


def draw_doc_lengths(key, part):
    key = jax.random.fold_in(key, 11)
    split_key, pick_key = jax.random.split(key)
    cut_points = jax.random.randint(split_key, (MICRO, BATCH), SEQ // 4, 3 * SEQ // 4 + 1)
    full_rows = jax.random.randint(pick_key, (BATCH,), 0, MICRO)
    first_length = jnp.where(jnp.arange(MICRO)[:, None] == full_rows[None, :], SEQ, cut_points)
    length_pair = jnp.stack([first_length, SEQ - first_length], axis=-1)
    return length_pair.astype(jnp.int32)


def block_levels(stream_key, dims, cuts, low, top_value):
    def one(dim, parts):
        steps = jax.random.uniform(jax.random.fold_in(jax.random.fold_in(stream_key, 6), dim), (parts,), jnp.float32, low / len(cuts), top_value / len(cuts))
        return jnp.repeat(jnp.exp(steps), dims[dim] // parts).reshape((-1,) + (1,) * (len(dims) - dim - 1))

    loudness = one(*cuts[0])
    for cut in cuts[1:]:
        loudness = loudness * one(*cut)
    return loudness


def centred(rng, extent, spread, reach, cuts=(), kind=jnp.bfloat16):
    entries = jax.random.normal(rng, extent, jnp.float32) * spread
    if len(cuts) > 0:
        entries = block_levels(rng, extent, cuts, -0.22, 0.18) * entries
    return jnp.clip(entries, min=-reach, max=reach).astype(kind)


def setup_inputs(seed: int = 0) -> dict:
    splits = jax.random.split(jax.random.key(seed), 16)
    tokens = centred(splits[0], (MICRO, BATCH, SEQ, D), 1.0, 6.0, ((1, 2), (2, 16)))
    cotangent = centred(splits[1], (MICRO, BATCH, SEQ, D), 1.0, 6.0, ((1, 2), (2, 16)))
    w_query = centred(splits[2], (D, QD), D ** -0.5, 0.1875)
    w_key = centred(splits[3], (D, KVD), D ** -0.5, 0.1875)
    w_value = centred(splits[4], (D, KVD), D ** -0.5, 0.1875)
    w_out = centred(splits[5], (QD, D), QD ** -0.5, 0.125)
    q_gain = jnp.clip(1.0 + 0.15 * jax.random.normal(splits[6], (QD,), jnp.float32), 0.25, 1.75)
    k_gain = jnp.clip(1.0 + 0.15 * jax.random.normal(splits[7], (KVD,), jnp.float32), 0.25, 1.75)
    attn_gain = jnp.clip(1.0 + 0.15 * jax.random.normal(splits[8], (D,), jnp.float32), 0.25, 1.75)
    w_gate = centred(splits[9], (D, FF), D ** -0.5, 0.1875)
    w_up = centred(splits[10], (D, FF), D ** -0.5, 0.1875)
    w_down = centred(splits[11], (FF, D), FF ** -0.5, 0.109375)
    mlp_gain = jnp.clip(1.0 + 0.15 * jax.random.normal(splits[12], (D,), jnp.float32), 0.25, 1.75)
    doc_lengths = draw_doc_lengths(jax.random.fold_in(splits[15], 71), 0)
    block_order = jax.random.permutation(splits[14], BLOCKS).astype(jnp.int32)
    return dict(tokens=tokens, cotangent=cotangent, w_query=w_query, w_key=w_key, w_value=w_value, w_out=w_out, q_gain=q_gain, k_gain=k_gain, attn_gain=attn_gain, w_gate=w_gate, w_up=w_up, w_down=w_down, mlp_gain=mlp_gain, doc_lengths=doc_lengths, block_order=block_order)


EPSILON = 1e-06
ROPE_BASE = 500000.0
MASK_FILL = -1e+30
HIGHEST_PRECISION = lax.Precision.HIGHEST

@jax.custom_vjp
def low(v):
    return lax.optimization_barrier(v.astype(jnp.bfloat16)).astype(jnp.float32)

@jax.custom_vjp
def low_back(v):
    return v

def low_keep(v):
    return (low(v), None)

def low_pass(kept, grad):
    return (grad,)

def back_keep(v):
    return (v, None)

def back_low(kept, grad):
    return (low(grad),)
low.defvjp(low_keep, low_pass)
low_back.defvjp(back_keep, back_low)

def matmul(left, right):
    return jnp.dot(left, right, precision=HIGHEST_PRECISION, preferred_element_type=jnp.float32)

def rms_norm(inputs, gain_vec):
    factor = lax.rsqrt(lax.optimization_barrier(jnp.mean(inputs * inputs, axis=-1, keepdims=True)) + EPSILON)
    return inputs * factor * gain_vec

def rope_tables(rot_places, head_size):
    frequency = jnp.power(ROPE_BASE, -jnp.arange(0, head_size, 2).astype(jnp.float32) / head_size)
    angles = rot_places.astype(jnp.float32)[:, None] * frequency[None, :]
    return (jnp.cos(angles), jnp.sin(angles))

def rotate(inputs, cos_table, sine_table, head_count, direction):
    row_count = inputs.shape[0]
    halves = inputs.reshape(row_count, head_count, 2, -1)
    first_half = halves[:, :, 0]
    second = halves[:, :, 1]
    cos_part = cos_table[:, None, :]
    sine_part = sine_table[:, None, :] * direction
    turned = jnp.stack([first_half * cos_part - second * sine_part, second * cos_part + first_half * sine_part], axis=2)
    return turned.reshape(row_count, -1)

def layer(weights_in, layer_in, key_places, segments, rot_places):
    w_query, w_key, w_value, w_out, q_gain, k_gain, attn_gain, w_gate, w_up, w_down, mlp_gain = weights_in
    row_count = layer_in.shape[0]
    cos_table, sine_table = rope_tables(rot_places, HD)
    q_pre = low_back(matmul(layer_in, w_query))
    k_pre = low_back(matmul(layer_in, w_key))
    v_pre = low_back(matmul(layer_in, w_value))
    queries = low(rotate(rms_norm(q_pre, q_gain), cos_table, sine_table, HEADS, 1.0))
    key_rows = low(rotate(rms_norm(k_pre, k_gain), cos_table, sine_table, KV_HEADS, 1.0))
    values = low(v_pre)
    q_heads = queries.reshape(row_count, KV_HEADS, HEADS // KV_HEADS, HD)
    k_heads = key_rows.reshape(row_count, KV_HEADS, HD)
    v_heads = values.reshape(row_count, KV_HEADS, HD)
    query_block = min(512, row_count)

    def attend(block_index):
        row_start = block_index * query_block
        q_part = lax.dynamic_slice_in_dim(q_heads, row_start, query_block, 0)
        q_places = lax.dynamic_slice_in_dim(key_places, row_start, query_block, 0)
        q_segments = lax.dynamic_slice_in_dim(segments, row_start, query_block, 0)
        raw_scores = jnp.einsum('tgrd,ugd->grtu', q_part, k_heads, precision=HIGHEST_PRECISION) * HD ** (-0.5)
        allowed = (q_segments[:, None] == segments[None, :]) & (key_places[None, :] <= q_places[:, None])
        masked = low_back(jnp.where(allowed[None, None], raw_scores, MASK_FILL))
        row_max = lax.optimization_barrier(jnp.max(masked, axis=-1, keepdims=True))
        exp_terms = jnp.exp(masked - row_max)
        attn_prob = low(exp_terms / lax.optimization_barrier(jnp.sum(exp_terms, axis=-1, keepdims=True)))
        attended = jnp.einsum('grtu,ugd->tgrd', attn_prob, v_heads, precision=HIGHEST_PRECISION)
        return attended.reshape(query_block, HEADS * HD)
    block_count = row_count // query_block
    attended = lax.map(jax.checkpoint(attend), jnp.arange(block_count, dtype=jnp.int32))
    attended = low(low_back(attended.reshape(row_count, HEADS * HD)))
    attn_proj = low_back(matmul(attended, w_out))
    hidden = layer_in + rms_norm(attn_proj, attn_gain)
    hidden_low = low(hidden)
    gate_pre = low_back(matmul(hidden_low, w_gate))
    up_pre = low_back(matmul(hidden_low, w_up))
    mixed = low(jax.nn.silu(gate_pre) * up_pre)
    down_pre = low_back(matmul(mixed, w_down))
    return hidden + rms_norm(down_pre, mlp_gain)

def reference(tokens, cotangent, w_query, w_key, w_value, w_out, q_gain, k_gain, attn_gain, w_gate, w_up, w_down, mlp_gain, doc_lengths, block_order):
    weights_in = tuple((weight.astype(jnp.float32) for weight in (w_query, w_key, w_value, w_out, q_gain, k_gain, attn_gain, w_gate, w_up, w_down, mlp_gain)))
    offsets = jnp.arange(TOK_BLK, dtype=jnp.int32)
    key_places = (block_order.astype(jnp.int32)[:, None] * TOK_BLK + offsets[None, :]).reshape(SEQ)
    row_inputs = tokens.reshape(MICRO * BATCH, SEQ, D).astype(jnp.float32)
    row_grads = cotangent.reshape(MICRO * BATCH, SEQ, D).astype(jnp.float32)
    first_lengths = doc_lengths.reshape(MICRO * BATCH, 2)[:, 0].astype(jnp.int32)

    def one_row(running, pieces):
        row_input, row_grad, first_length = pieces
        segments = (key_places >= first_length).astype(jnp.int32)
        rot_places = key_places - segments * first_length

        def forward(weights_now, layer_now):
            return layer(weights_now, layer_now, key_places, segments, rot_places)
        result, pullback = jax.vjp(forward, weights_in, row_input)
        weight_grads, input_grad = pullback(row_grad)
        running = jax.tree.map(jnp.add, running, weight_grads)
        return (running, (result.astype(jnp.bfloat16), input_grad))
    zero_grads = jax.tree.map(jnp.zeros_like, weights_in)
    totals, (results, input_grads) = lax.scan(one_row, zero_grads, (row_inputs, row_grads, first_lengths))
    layer_out = results.reshape(MICRO, BATCH, SEQ, D)
    input_grad = input_grads.reshape(MICRO, BATCH, SEQ, D)
    return (layer_out, input_grad, totals[0], totals[1], totals[2], totals[3], totals[4], totals[5], totals[6], totals[7], totals[8], totals[9], totals[10])
```

```python
import functools

import jax
import jax.numpy as jnp
import numpy as np
from jax import lax
from jax.experimental import pallas as pl
from jax.experimental.pallas import tpu as pltpu
from jax.sharding import PartitionSpec as P

HD = 128
EPSILON = 1e-06
ROPE_BASE = 500000.0
MASK_FILL = -1e30
MESH = pl.DeviceIdType.MESH
LOW = jnp.bfloat16
WIDE = jnp.float32
TILE = 128
CHUNK = 256


def remote(source, target, send_sem, recv_sem, place):
    return pltpu.make_async_remote_copy(
        src_ref=source,
        dst_ref=target,
        send_sem=send_sem,
        recv_sem=recv_sem,
        device_id=place,
        device_id_type=MESH,
    )


def dot(left, right):
    return jnp.dot(left, right, preferred_element_type=WIDE)


def dot_nt(left, right):
    return lax.dot_general(left, right, (((1,), (1,)), ((), ())), preferred_element_type=WIDE)


def dot_tn(left, right):
    return lax.dot_general(left, right, (((0,), (0,)), ((), ())), preferred_element_type=WIDE)


class Spot:
    def __init__(self):
        self.dp = lax.axis_index("dp")
        self.seq = lax.axis_index("seq")
        self.core = self.seq % 2
        self.chip = self.seq // 2
        self.x = self.chip % 2
        self.z = self.chip // 2
        self.sibling = self.seq + 1 - 2 * self.core
        self.flip_x = self.seq + 2 - 4 * self.x
        self.far_z = (
            self.z + 1 - 2 * (self.z % 2),
            self.z + 2 - 4 * (self.z // 2),
            3 - self.z,
        )


def greet_row(spot, devices):
    barrier = pltpu.get_barrier_semaphore()
    for step in range(1, devices):
        pl.semaphore_signal(
            barrier,
            inc=1,
            device_id=(spot.dp, (spot.seq + step) % devices),
            device_id_type=MESH,
        )
    pl.semaphore_wait(barrier, devices - 1)


class RowGather:
    def __init__(self, spot, own, held, local_sem, send_sems, recv_sems):
        self.spot, self.own, self.held = spot, own, held
        self.send_sems, self.recv_sems = send_sems, recv_sems
        self.sent = []
        self.local = pltpu.make_async_copy(own.at[spot.core], held.at[spot.seq], local_sem)

    def send(self, source, slots, recv_sem, target):
        copy = remote(
            source, slots, self.send_sems.at[len(self.sent)], recv_sem, (self.spot.dp, target)
        )
        copy.start()
        self.sent.append(copy)

    def start(self):
        spot = self.spot
        own_slot = self.held.at[spot.seq]
        own_sem = self.recv_sems.at[spot.seq]
        for far in spot.far_z:
            for micro in range(2):
                self.send(self.own.at[micro], own_slot, own_sem, far * 4 + spot.x * 2 + micro)
        for micro in range(2):
            self.send(
                self.own.at[micro], own_slot, own_sem, spot.z * 4 + (1 - spot.x) * 2 + micro
            )
        self.send(self.own.at[1 - spot.core], own_slot, own_sem, spot.sibling)
        self.local.start()

    def arrived(self, slots, recv_sem):
        remote(slots, slots, self.send_sems.at[0], recv_sem, (self.spot.dp, self.spot.sibling)).wait_recv()

    def forward(self):
        spot = self.spot
        for far in spot.far_z:
            first = far * 4 + spot.x * 2
            for core in range(2):
                self.arrived(self.held.at[first + core], self.recv_sems.at[first + core])
            pair = self.held.at[pl.ds(first, 2)]
            self.send(pair, pair, self.recv_sems.at[16 + far], spot.flip_x)

    def finish(self):
        spot = self.spot
        self.arrived(self.held.at[spot.sibling], self.recv_sems.at[spot.sibling])
        for core in range(2):
            slot = spot.z * 4 + (1 - spot.x) * 2 + core
            self.arrived(self.held.at[slot], self.recv_sems.at[slot])
        for far in spot.far_z:
            first = far * 4 + (1 - spot.x) * 2
            self.arrived(self.held.at[pl.ds(first, 2)], self.recv_sems.at[16 + far])
        self.local.wait()
        for copy in self.sent:
            copy.wait_send()


GATHER_SENDS = 12
GATHER_RECVS = 20


def rope_rows(table, block, first_length):
    start = block * 64
    inside = table[pl.ds(64 + start, 64), :]
    shifted = table[pl.ds(64 + jnp.maximum(start - first_length, -64), 64), :]
    places = start + lax.broadcasted_iota(jnp.int32, (64, HD), 0)
    return jnp.where(places < first_length, inside, shifted)


def swap_halves(head):
    return pltpu.roll(head, HD // 2, axis=1)


def columns_of(rows):
    return jnp.concatenate([rows] * 16, axis=0).T[:, :8]


def rows_of(first, second):
    lane = lax.broadcasted_iota(jnp.int32, (first.shape[0], HD), 1)
    return jnp.where(lane == 0, first, second).T[:8]


def allowed_places(tile, count, first_length):
    keys = lax.broadcasted_iota(jnp.int32, (count, 2 * TILE), 0)
    lanes = lax.broadcasted_iota(jnp.int32, (1, 2 * TILE), 1)
    queries = tile * TILE + lanes % TILE
    earliest = jnp.where(queries < first_length, 0, first_length)
    return (keys >= earliest) & (keys <= queries)


def forward_kernel(
    tok_ref, wq_hbm, wk_hbm, wv_hbm, qgain_ref, kgain_ref, cos_ref, sine_ref,
    order_ref, inverse_ref, first_ref,
    att_tok, tok_nat, q_pair, kv_nat, hat, factors, lse, att_nat,
    tok_all, w_own, stat_all, att_send, att_recv, kv_turned,
    local_sems, send_sems, recv_sems, stat_send, stat_recv, att_ssem, att_rsem,
):
    spot = Spot()
    devices = 16
    chips = 8
    chip = spot.chip
    loads = [
        pltpu.make_async_copy(wq_hbm.at[:, pl.ds(pl.multiple_of(chip * 256, 256), 256)], w_own.at[:, pl.ds(0, 256)], local_sems.at[1]),
        pltpu.make_async_copy(wk_hbm.at[:, pl.ds(pl.multiple_of(chip * 128, 128), 128)], w_own.at[:, pl.ds(256, 128)], local_sems.at[2]),
        pltpu.make_async_copy(wv_hbm.at[:, pl.ds(pl.multiple_of(chip * 128, 128), 128)], w_own.at[:, pl.ds(384, 128)], local_sems.at[3]),
    ]
    for load in loads:
        load.start()
    greet_row(spot, devices)
    gather = RowGather(spot, tok_ref, tok_all, local_sems.at[0], send_sems, recv_sems)
    gather.start()
    gather.forward()
    for load in loads:
        load.wait()
    gather.finish()

    first_length = first_ref[spot.core]
    for part in range(4):
        rows = pl.ds(part * CHUNK, CHUNK)
        chunk = jnp.concatenate([tok_all[inverse_ref[part * 4 + piece]] for piece in range(4)], axis=0)
        tok_nat[rows, :] = chunk
        pre = dot(chunk, w_own[...])
        hat[rows, :] = pre[:, :384]
        kv_nat[rows, 128:] = pre[:, 384:].astype(LOW)
        squares = pre[:, :384] * pre[:, :384]
        stat_all[pl.ds(chip, 1), :, rows] = rows_of(
            jnp.sum(squares[:, :256], axis=-1, keepdims=True),
            jnp.sum(squares[:, 256:], axis=-1, keepdims=True),
        )[None]
    stat_copies = []
    for step in range(1, chips):
        other = (chip + step) % chips
        copy = remote(
            stat_all.at[chip], stat_all.at[chip], stat_send.at[step - 1], stat_recv.at[chip],
            (spot.dp, other * 2 + spot.core),
        )
        copy.start()
        stat_copies.append(copy)
    for step in range(1, chips):
        other = (chip + step) % chips
        remote(
            stat_all.at[other], stat_all.at[other], stat_send.at[0], stat_recv.at[other],
            (spot.dp, spot.sibling),
        ).wait_recv()
    total = stat_all[0]
    for other in range(1, chips):
        total = total + stat_all[other]
    width = jnp.where(lax.broadcasted_iota(jnp.int32, total.shape, 0) == 0, 1.0 / 2048, 1.0 / 1024)
    factors[...] = lax.rsqrt(total * width + EPSILON)
    qgain = qgain_ref[pl.ds(chip * 2, 2), :]
    kgain = kgain_ref[pl.ds(chip, 1), :]
    for part in range(8):
        rows = pl.ds(part * TILE, TILE)
        scale = columns_of(factors[:, rows])
        cos = jnp.concatenate([rope_rows(cos_ref, part * 2 + piece, first_length) for piece in range(2)], axis=0)
        sine = jnp.concatenate([rope_rows(sine_ref, part * 2 + piece, first_length) for piece in range(2)], axis=0)
        for head in range(3):
            lanes = pl.ds(head * HD, HD)
            column = scale[:, 0:1] if head < 2 else scale[:, 1:2]
            gain = qgain[head : head + 1] if head < 2 else kgain
            normal = hat[rows, lanes] * column
            hat[rows, lanes] = normal
            normed = normal * gain
            turned = (normed * cos + swap_halves(normed) * sine).astype(LOW)
            if head < 2:
                q_pair[part, pl.ds(head * HD, HD), :] = turned
            else:
                kv_nat[rows, :HD] = turned
    kv_turned[...] = kv_nat[:, HD:].T
    for tile in range(8):
        count = (tile + 1) * TILE
        scores = dot_nt(kv_nat[:count, :HD], q_pair[tile]) * HD ** (-0.5)
        masked = jnp.where(allowed_places(tile, count, first_length), scores, MASK_FILL)
        top = jnp.max(masked, axis=0, keepdims=True)
        terms = jnp.exp(masked - top)
        weight = jnp.sum(terms, axis=0, keepdims=True)
        lse[pl.ds(tile, 1), :] = top + jnp.log(weight)
        turned = dot(kv_turned[:, :count], terms.astype(LOW)) / weight
        attended = turned.T.astype(LOW)
        att_nat[pl.ds(tile * 2, 2), :, :HD] = attended[:TILE].reshape(2, 64, HD)
        att_nat[pl.ds(tile * 2, 2), :, HD:] = attended[TILE:].reshape(2, 64, HD)
    own_part = (spot.core, slice(None), pl.ds(pl.multiple_of(chip * 256, 256), 256))
    att_recv[pl.ds(chip, 1), pl.ds(spot.core, 1)] = att_nat[order_ref[spot.seq]][None, None]
    sent = []
    for step in range(1, devices):
        other = (spot.seq + step) % devices
        att_send[step] = att_nat[order_ref[other]]
        copy = remote(
            att_send.at[step], att_recv.at[chip, spot.core], att_ssem.at[step],
            att_rsem.at[spot.seq], (spot.dp, other),
        )
        copy.start()
        sent.append(copy)
    for step in range(1, devices):
        other = (spot.seq + step) % devices
        slot = att_recv.at[other // 2, other % 2]
        remote(slot, slot, att_ssem.at[0], att_rsem.at[other], (spot.dp, spot.sibling)).wait_recv()
    for piece in range(chips):
        for micro in range(2):
            att_tok[micro, :, piece * 256 : (piece + 1) * 256] = att_recv[piece, micro]
    for copy in sent + stat_copies:
        copy.wait_send()


def rope_constants(length):
    frequency = np.power(np.float32(ROPE_BASE), -np.arange(0, HD, 2).astype(np.float32) / np.float32(HD)).astype(np.float32)
    angles = (np.arange(length, dtype=np.float32)[:, None] * frequency[None, :]).astype(np.float32).astype(np.float64)
    cos, sine = np.cos(angles), np.sin(angles)
    front = np.zeros((64, HD))
    cos = np.concatenate([front, np.concatenate([cos, cos], axis=1)], axis=0)
    sine = np.concatenate([front, np.concatenate([-sine, sine], axis=1)], axis=0)
    return jnp.asarray(cos, WIDE), jnp.asarray(sine, WIDE)


def row_forward(tokens, w_query, w_key, w_value, q_gain, k_gain, cos, sine, order, inverse, first):
    length = 1024
    width = tokens.shape[-1]
    any_spec = pl.BlockSpec(memory_space=pl.ANY)
    vmem = pl.BlockSpec(memory_space=pltpu.VMEM)
    smem = pl.BlockSpec(memory_space=pltpu.SMEM)
    shape = jax.ShapeDtypeStruct
    return pl.pallas_call(
        forward_kernel,
        out_shape=(
            shape((2, 64, 2048), LOW),
            shape((length, width), LOW),
            shape((8, 2 * TILE, HD), LOW),
            shape((length, 2 * HD), LOW),
            shape((length, 3 * HD), WIDE),
            shape((8, length), WIDE),
            shape((8, 2 * TILE), WIDE),
            shape((16, 64, 2 * HD), LOW),
        ),
        in_specs=[vmem, any_spec, any_spec, any_spec, vmem, vmem, vmem, vmem, smem, smem, smem],
        out_specs=(vmem,) * 8,
        scratch_shapes=[
            pltpu.VMEM((16, 64, width), LOW),
            pltpu.VMEM((width, 512), LOW),
            pltpu.VMEM((8, 8, length), WIDE),
            pltpu.VMEM((16, 64, 2 * HD), LOW),
            pltpu.VMEM((8, 2, 64, 2 * HD), LOW),
            pltpu.VMEM((HD, length), LOW),
            pltpu.SemaphoreType.DMA((4,)),
            pltpu.SemaphoreType.DMA((GATHER_SENDS,)),
            pltpu.SemaphoreType.DMA((GATHER_RECVS,)),
            pltpu.SemaphoreType.DMA((8,)),
            pltpu.SemaphoreType.DMA((8,)),
            pltpu.SemaphoreType.DMA((16,)),
            pltpu.SemaphoreType.DMA((16,)),
        ],
        compiler_params=pltpu.CompilerParams(
            collective_id=0, has_side_effects=True, vmem_limit_bytes=56 * 2**20
        ),
        name="row_forward",
    )(tokens, w_query, w_key, w_value, q_gain, k_gain, cos, sine, order, inverse, first)


class Post:
    def __init__(self, sems):
        self.sems, self.started = sems, []

    def send(self, source, target, recv_sem, place):
        copy = remote(source, target, self.sems.at[len(self.started)], recv_sem, place)
        copy.start()
        self.started.append(copy)

    def finish(self):
        for copy in self.started:
            copy.wait_send()


def arrived(spot, slot, recv_sem, spare_sem):
    remote(slot, slot, spare_sem, recv_sem, (spot.dp, spot.sibling)).wait_recv()


def backward_kernel(
    proj_ref, hid_ref, down_ref, gate_ref, up_ref, mixed_ref, hgrad_ref, vec_ref,
    tok_nat, q_pair, kv_nat, hat, factors, lse, att_nat,
    wout_hbm, wq_hbm, wk_hbm, wv_hbm, qgain_ref, kgain_ref, cos_ref, sine_ref,
    order_ref, inverse_ref, first_ref,
    in_grad, g_query, g_key, g_value, g_out, vec_out, gain_out, g_gate, g_up, g_down,
    wout_own, wq_all, wk_all, wv_all,
    proj_all, proj_nat, mix_turned, hid_all, down_all, gu_all, mix_all, vec_all, vec_far,
    ag_pair, k_turned, dq, dkv, grad_nat, stat_all, grad_send, grad_recv, grad_tok,
    part_low, wqkv_recv, wout_low, wout_recv, gain_own, gain_recv, gu_low, gu_recv, down_low, down_recv,
    local_sems, send_sems, recv_sems, post_sems, plane_sems, far_sems, stat_sems, grad_sems, wqkv_sems, wout_sems, gu_sems, self_sems,
):
    spot = Spot()
    devices, chips = 16, 8
    dp, seq, core, chip, z = spot.dp, spot.seq, spot.core, spot.chip, spot.z
    me = dp * devices + seq
    member = dp * 4 + spot.x * 2 + core
    spare = post_sems.at[0]
    loads = [
        pltpu.make_async_copy(wout_hbm.at[pl.ds(pl.multiple_of(chip * 256, 256), 256)], wout_own, local_sems.at[1]),
        pltpu.make_async_copy(wq_hbm, wq_all, local_sems.at[2]),
        pltpu.make_async_copy(wk_hbm, wk_all, local_sems.at[3]),
        pltpu.make_async_copy(wv_hbm, wv_all, local_sems.at[4]),
    ]
    for load in loads:
        load.start()
    barrier = pltpu.get_barrier_semaphore()
    for step in range(1, 2 * devices):
        other = (me + step) % (2 * devices)
        pl.semaphore_signal(barrier, inc=1, device_id=(other // devices, other % devices), device_id_type=MESH)
    for group in range(8):
        block = mixed_ref[:, group * 384 : (group + 1) * 384].T
        for piece in range(4):
            mix_turned[(group // 4) * 4 + piece, pl.ds((group % 4) * 96, 96), :] = block[piece * 96 : (piece + 1) * 96]
    pl.semaphore_wait(barrier, 2 * devices - 1)

    gather = RowGather(spot, proj_ref, proj_all, local_sems.at[0], send_sems, recv_sems)
    gather.start()

    post = Post(post_sems)
    plane_places = ((dp, spot.flip_x), (1 - dp, seq), (1 - dp, spot.flip_x))
    plane_members = (
        dp * 4 + (1 - spot.x) * 2 + core,
        (1 - dp) * 4 + spot.x * 2 + core,
        (1 - dp) * 4 + (1 - spot.x) * 2 + core,
    )
    sib_place = (dp, spot.sibling)
    keeps = [
        pltpu.make_async_copy(hid_ref, hid_all.at[member], local_sems.at[5]),
        pltpu.make_async_copy(down_ref, down_all.at[member], local_sems.at[6]),
        pltpu.make_async_copy(gate_ref.at[:, pl.ds(pl.multiple_of(member * 384, 128), 384)], gu_all.at[member, :, pl.ds(0, 384)], local_sems.at[7]),
        pltpu.make_async_copy(up_ref.at[:, pl.ds(pl.multiple_of(member * 384, 128), 384)], gu_all.at[member, :, pl.ds(384, 384)], local_sems.at[8]),
        pltpu.make_async_copy(mix_turned.at[member], mix_all.at[member], local_sems.at[9]),
        pltpu.make_async_copy(vec_ref, vec_all.at[member], local_sems.at[10]),
    ]
    for keep in keeps:
        keep.start()
    for place in plane_places:
        post.send(hid_ref, hid_all.at[member], plane_sems.at[0, member], place)
        post.send(down_ref, down_all.at[member], plane_sems.at[1, member], place)
    post.send(hid_ref, hid_all.at[member], plane_sems.at[0, member], sib_place)
    post.send(down_ref, down_all.at[member], plane_sems.at[1, member], sib_place)
    for step in range(1, 8):
        other = (member + step) % 8
        place = (other // 4, z * 4 + other % 4)
        lanes = pl.ds(pl.multiple_of(other * 384, 128), 384)
        post.send(mix_turned.at[other], mix_all.at[member], plane_sems.at[2, member], place)
        post.send(gate_ref.at[:, lanes], gu_all.at[member, :, pl.ds(0, 384)], plane_sems.at[3, member], place)
        post.send(up_ref.at[:, lanes], gu_all.at[member, :, pl.ds(384, 384)], plane_sems.at[4, member], place)
        post.send(vec_ref, vec_all.at[member], plane_sems.at[5, member], place)

    gather.forward()
    for other in plane_members:
        arrived(spot, hid_all.at[other], plane_sems.at[0, other], spare)
        post.send(hid_all.at[other], hid_all.at[other], plane_sems.at[0, other], sib_place)
        arrived(spot, down_all.at[other], plane_sems.at[1, other], spare)
        post.send(down_all.at[other], down_all.at[other], plane_sems.at[1, other], sib_place)
    gather.finish()

    loads[0].wait()
    for part in range(8):
        rows = pl.ds(part * TILE, TILE)
        chunk = jnp.concatenate([proj_all[inverse_ref[part * 2 + piece]] for piece in range(2)], axis=0)
        proj_nat[rows, :] = chunk
        att_grad = dot_nt(chunk, wout_own[...]).astype(LOW)
        ag_pair[part, :TILE, :] = att_grad[:, :HD]
        ag_pair[part, TILE:, :] = att_grad[:, HD:]
    wout_low[...] = dot_tn(att_nat[...].reshape(1024, 2 * HD), proj_nat[...]).astype(LOW)
    for piece in range(4):
        target = chip * 4 + piece
        rows = pl.ds(piece * 64, 64)
        slot = wout_recv.at[dp * 2 + core]

        @pl.when(target == me)
        def _():
            keep = pltpu.make_async_copy(wout_low.at[rows], slot, self_sems.at[0])
            keep.start()
            keep.wait()

        @pl.when(target != me)
        def _():
            remote(
                wout_low.at[rows], slot, wout_sems.at[piece], wout_sems.at[4 + dp * 2 + core],
                (target // devices, target % devices),
            ).start()

    k_turned[...] = kv_nat[:, :HD].T
    first_length = first_ref[core]
    dkv[...] = jnp.zeros_like(dkv)
    for tile in range(8):
        count = (tile + 1) * TILE
        queries, grads = q_pair[tile], ag_pair[tile]
        scores = dot_nt(kv_nat[:count, :HD], queries) * HD ** (-0.5)
        masked = jnp.where(allowed_places(tile, count, first_length), scores, MASK_FILL)
        probs = jnp.exp(masked - lse[tile : tile + 1, :])
        prob_grad = dot_nt(kv_nat[:count, HD:], grads)
        row_dot = jnp.sum(probs * prob_grad, axis=0, keepdims=True)
        score_grad = (probs * (prob_grad - row_dot)).astype(LOW)
        dkv[:count, :HD] += dot(score_grad, queries)
        dkv[:count, HD:] += dot(probs.astype(LOW), grads)
        turned = (dot(k_turned[:, :count], score_grad) * HD ** (-0.5)).T
        rows = pl.ds(tile * TILE, TILE)
        dq[rows, :HD] = turned[:TILE]
        dq[rows, HD:] = turned[TILE:]

    qgain = qgain_ref[pl.ds(chip * 2, 2), :]
    kgain = kgain_ref[pl.ds(chip, 1), :]
    gains = [jnp.zeros((1, HD), WIDE) for _ in range(3)]
    for part in range(8):
        rows = pl.ds(part * TILE, TILE)
        cos = jnp.concatenate([rope_rows(cos_ref, part * 2 + piece, first_length) for piece in range(2)], axis=0)
        sine = jnp.concatenate([rope_rows(sine_ref, part * 2 + piece, first_length) for piece in range(2)], axis=0)
        dots = []
        for head in range(3):
            turned = dq[rows, pl.ds(head * HD, HD)] if head < 2 else dkv[rows, :HD] * HD ** (-0.5)
            back = turned * cos - swap_halves(turned) * sine
            normal = hat[rows, pl.ds(head * HD, HD)]
            gain = qgain[head : head + 1] if head < 2 else kgain
            gains[head] = gains[head] + jnp.sum(back * normal, axis=0, keepdims=True)
            weighted = back * gain
            if head < 2:
                dq[rows, pl.ds(head * HD, HD)] = weighted
            else:
                dkv[rows, :HD] = weighted
            dots.append(jnp.sum(weighted * normal, axis=-1, keepdims=True))
        stat_all[pl.ds(chip, 1), :, rows] = rows_of(dots[0] + dots[1], dots[2])[None]
    for step in range(1, chips):
        other = (chip + step) % chips
        post.send(stat_all.at[chip], stat_all.at[chip], stat_sems.at[chip], (dp, other * 2 + core))
    gain_own[...] = jnp.concatenate([jnp.broadcast_to(gain, (8, HD)) for gain in gains], axis=1)
    for piece in range(4):
        target = chip * 4 + piece
        slot = gain_recv.at[dp * 2 + core]

        @pl.when(target == me)
        def _():
            keep = pltpu.make_async_copy(gain_own, slot, self_sems.at[0])
            keep.start()
            keep.wait()

        @pl.when(target != me)
        def _():
            remote(
                gain_own, slot, wout_sems.at[8 + piece], wout_sems.at[12 + dp * 2 + core],
                (target // devices, target % devices),
            ).start()

    for step in range(1, chips):
        other = (chip + step) % chips
        arrived(spot, stat_all.at[other], stat_sems.at[other], spare)
    total = stat_all[0]
    for other in range(1, chips):
        total = total + stat_all[other]
    width = jnp.where(lax.broadcasted_iota(jnp.int32, total.shape, 0) == 0, 1.0 / 2048, 1.0 / 1024)
    means = total * width
    for part in range(8):
        rows = pl.ds(part * TILE, TILE)
        mean = columns_of(means[:, part * TILE : (part + 1) * TILE])
        scale = columns_of(factors[:, rows])
        pieces = []
        for head in range(3):
            column = 0 if head < 2 else 1
            weighted = dq[rows, pl.ds(head * HD, HD)] if head < 2 else dkv[rows, :HD]
            normal = hat[rows, pl.ds(head * HD, HD)]
            pieces.append(scale[:, column : column + 1] * (weighted - normal * mean[:, column : column + 1]))
        pieces.append(dkv[rows, HD:])
        grad_nat[pl.ds(part * 2, 2)] = jnp.concatenate(pieces, axis=1).astype(LOW).reshape(2, 64, 512)

    grad_recv[pl.ds(chip, 1), pl.ds(core, 1)] = grad_nat[order_ref[seq]][None, None]
    for step in range(1, devices):
        other = (seq + step) % devices
        grad_send[step] = grad_nat[order_ref[other]]
        post.send(grad_send.at[step], grad_recv.at[chip, core], grad_sems.at[seq], (dp, other))
    part_low[...] = dot_tn(tok_nat[...], grad_nat[...].reshape(1024, 512)).astype(LOW)
    own_rows = pl.ds(pl.multiple_of(me * 32, 32), 32)
    wqkv_recv[pl.ds(me, 1)] = part_low[own_rows, :][None]
    for step in range(1, 2 * devices):
        other = (me + step) % (2 * devices)
        post.send(
            part_low.at[pl.ds(pl.multiple_of(other * 32, 32), 32)], wqkv_recv.at[me], wqkv_sems.at[me],
            (other // devices, other % devices),
        )

    for keep in keeps:
        keep.wait()
    for step in range(1, 8):
        other = (member + step) % 8
        arrived(spot, mix_all.at[other], plane_sems.at[2, other], spare)
        arrived(spot, gu_all.at[other, :, pl.ds(0, 384)], plane_sems.at[3, other], spare)
        arrived(spot, gu_all.at[other, :, pl.ds(384, 384)], plane_sems.at[4, other], spare)
        arrived(spot, vec_all.at[other], plane_sems.at[5, other], spare)
    for y in range(2):
        for x in range(2):
            other = y * 4 + x * 2 + 1 - core
            arrived(spot, hid_all.at[other], plane_sems.at[0, other], spare)
            arrived(spot, down_all.at[other], plane_sems.at[1, other], spare)
    vec = vec_all[0]
    for other in range(1, 8):
        vec = vec + vec_all[other]
    vec_far[pl.ds(z, 1)] = vec[None]
    mixes = jnp.concatenate([mix_all[other] for other in range(8)], axis=1)
    down_low[...] = dot(mixes, down_all[...].reshape(1024, 1024)).astype(LOW)
    down_recv[pl.ds(z, 1)] = down_low[pl.ds(pl.multiple_of(z * 96, 96), 96), :][None]
    for far in spot.far_z:
        place = (dp, far * 4 + spot.x * 2 + core)
        post.send(vec_far.at[z], vec_far.at[z], far_sems.at[0, z], place)
        post.send(down_low.at[pl.ds(pl.multiple_of(far * 96, 96), 96)], down_recv.at[z], far_sems.at[1, z], place)
    gu_low[...] = dot_tn(hid_all[...].reshape(1024, 1024), gu_all[...].reshape(1024, 768)).astype(LOW)
    gu_recv[pl.ds(z, 1), pl.ds(member, 1)] = gu_low[own_rows, :][None, None]
    for step in range(1, 2 * devices):
        other = (me + step) % (2 * devices)
        post.send(
            gu_low.at[pl.ds(pl.multiple_of(other * 32, 32), 32)], gu_recv.at[z, member], gu_sems.at[z, member],
            (other // devices, other % devices),
        )

    for step in range(1, devices):
        other = (seq + step) % devices
        arrived(spot, grad_recv.at[other // 2, other % 2], grad_sems.at[other], spare)
    for piece in range(chips):
        for micro in range(2):
            rows = pl.ds(micro * 64, 64)
            block = grad_recv[piece, micro]
            grad_tok[rows, piece * 256 : (piece + 1) * 256] = block[:, :256]
            grad_tok[rows, 2048 + piece * 128 : 2048 + (piece + 1) * 128] = block[:, 256:384]
            grad_tok[rows, 3072 + piece * 128 : 3072 + (piece + 1) * 128] = block[:, 384:]
    for load in loads[1:]:
        load.wait()
    in_grad[...] = (
        hgrad_ref[...]
        + dot_nt(grad_tok[:, :2048], wq_all[...])
        + dot_nt(grad_tok[:, 2048:3072], wk_all[...])
        + dot_nt(grad_tok[:, 3072:], wv_all[...])
    )

    for y in range(2):
        for micro in range(2):
            source = y * 2 + micro
            sender = y * devices + (me // 4) * 2 + micro

            @pl.when(sender != me)
            def _():
                arrived(spot, wout_recv.at[source], wout_sems.at[4 + source], spare)
                arrived(spot, gain_recv.at[source], wout_sems.at[12 + source], spare)

    g_out[...] = sum(wout_recv[source].astype(WIDE) for source in range(4))
    gain_out[...] = sum(gain_recv[source] for source in range(4))
    for step in range(1, 2 * devices):
        other = (me + step) % (2 * devices)
        arrived(spot, wqkv_recv.at[other], wqkv_sems.at[other], spare)
    for piece in range(chips):
        block = sum(
            wqkv_recv[y * devices + piece * 2 + micro].astype(WIDE) for y in range(2) for micro in range(2)
        )
        g_query[:, piece * 256 : (piece + 1) * 256] = block[:, :256]
        g_key[:, piece * 128 : (piece + 1) * 128] = block[:, 256:384]
        g_value[:, piece * 128 : (piece + 1) * 128] = block[:, 384:]
    for far in spot.far_z:
        arrived(spot, vec_far.at[far], far_sems.at[0, far], spare)
        arrived(spot, down_recv.at[far], far_sems.at[1, far], spare)
    vec_out[...] = sum(vec_far[far] for far in range(4))
    g_down[...] = sum(down_recv[far].astype(WIDE) for far in range(4))
    for step in range(1, 2 * devices):
        other = (me + step) % (2 * devices)
        far, slot = (other % devices) // 4, (other // devices) * 4 + other % 4
        arrived(spot, gu_recv.at[far, slot], gu_sems.at[far, slot], spare)
    for slot in range(8):
        block = sum(gu_recv[far, slot].astype(WIDE) for far in range(4))
        g_gate[:, slot * 384 : (slot + 1) * 384] = block[:, :384]
        g_up[:, slot * 384 : (slot + 1) * 384] = block[:, 384:]
    post.finish()
    for piece in range(4):

        @pl.when(chip * 4 + piece != me)
        def _():
            place = ((chip * 4 + piece) // devices, (chip * 4 + piece) % devices)
            rows = pl.ds(piece * 64, 64)
            remote(wout_low.at[rows], wout_recv.at[0], wout_sems.at[piece], wout_sems.at[4], place).wait_send()
            remote(gain_own, gain_recv.at[0], wout_sems.at[8 + piece], wout_sems.at[12], place).wait_send()


POST_SENDS = 8 + 28 + 6 + 7 + 15 + 31 + 6 + 31


def row_backward(*operands):
    length, width = 1024, 1024
    any_spec = pl.BlockSpec(memory_space=pl.ANY)
    vmem = pl.BlockSpec(memory_space=pltpu.VMEM)
    smem = pl.BlockSpec(memory_space=pltpu.SMEM)
    shape = jax.ShapeDtypeStruct
    dma = pltpu.SemaphoreType.DMA
    return pl.pallas_call(
        backward_kernel,
        out_shape=(
            shape((128, width), WIDE),
            shape((32, 2048), WIDE),
            shape((32, 1024), WIDE),
            shape((32, 1024), WIDE),
            shape((64, 1024), WIDE),
            shape((8, 1024), WIDE),
            shape((8, 384), WIDE),
            shape((32, 3072), WIDE),
            shape((32, 3072), WIDE),
            shape((96, 1024), WIDE),
        ),
        in_specs=[vmem] * 15 + [any_spec] * 4 + [vmem] * 4 + [smem] * 3,
        out_specs=(vmem,) * 10,
        scratch_shapes=[
            pltpu.VMEM((256, width), LOW),
            pltpu.VMEM((width, 2048), LOW),
            pltpu.VMEM((width, 1024), LOW),
            pltpu.VMEM((width, 1024), LOW),
            pltpu.VMEM((16, 64, width), LOW),
            pltpu.VMEM((length, width), LOW),
            pltpu.VMEM((8, 384, 128), LOW),
            pltpu.VMEM((8, 128, width), LOW),
            pltpu.VMEM((8, 128, width), LOW),
            pltpu.VMEM((8, 128, 768), LOW),
            pltpu.VMEM((8, 384, 128), LOW),
            pltpu.VMEM((8, 8, 1024), WIDE),
            pltpu.VMEM((4, 8, 1024), WIDE),
            pltpu.VMEM((8, 2 * TILE, HD), LOW),
            pltpu.VMEM((HD, length), LOW),
            pltpu.VMEM((length, 2 * HD), WIDE),
            pltpu.VMEM((length, 2 * HD), WIDE),
            pltpu.VMEM((16, 64, 512), LOW),
            pltpu.VMEM((8, 8, length), WIDE),
            pltpu.VMEM((16, 64, 512), LOW),
            pltpu.VMEM((8, 2, 64, 512), LOW),
            pltpu.VMEM((128, 4096), LOW),
            pltpu.VMEM((length, 512), LOW),
            pltpu.VMEM((32, 32, 512), LOW),
            pltpu.VMEM((256, width), LOW),
            pltpu.VMEM((4, 64, width), LOW),
            pltpu.VMEM((8, 384), WIDE),
            pltpu.VMEM((4, 8, 384), WIDE),
            pltpu.VMEM((1024, 768), LOW),
            pltpu.VMEM((4, 8, 32, 768), LOW),
            pltpu.VMEM((384, width), LOW),
            pltpu.VMEM((4, 96, width), LOW),
            dma((11,)),
            dma((GATHER_SENDS,)),
            dma((GATHER_RECVS,)),
            dma((POST_SENDS,)),
            dma((6, 8)),
            dma((2, 4)),
            dma((8,)),
            dma((16,)),
            dma((32,)),
            dma((16,)),
            dma((4, 8)),
            dma((1,)),
        ],
        compiler_params=pltpu.CompilerParams(
            collective_id=1, has_side_effects=True, vmem_limit_bytes=60 * 2**20
        ),
        name="row_backward",
    )(*operands)


def rope_tables(rot_places, head_size):
    frequency = jnp.power(ROPE_BASE, -jnp.arange(0, head_size, 2).astype(jnp.float32) / head_size)
    angles = rot_places.astype(jnp.float32)[:, None] * frequency[None, :]
    return (jnp.cos(angles), jnp.sin(angles))


def rotate(inputs, cos_table, sine_table, head_count, direction):
    row_count = inputs.shape[0]
    halves = inputs.reshape(row_count, head_count, 2, -1)
    first_half = halves[:, :, 0]
    second = halves[:, :, 1]
    cos_part = cos_table[:, None, :]
    sine_part = sine_table[:, None, :] * direction
    turned = jnp.stack(
        [first_half * cos_part - second * sine_part, second * cos_part + first_half * sine_part],
        axis=2,
    )
    return turned.reshape(row_count, -1)


def product(left, right):
    return jnp.dot(left, right, preferred_element_type=jnp.float32)


def weight_grad(left, right):
    return lax.dot_general(
        left, right, (((0,), (0,)), ((), ())), preferred_element_type=jnp.float32
    )


def back_product(left, right):
    return lax.dot_general(
        left, right, (((1,), (1,)), ((), ())), preferred_element_type=jnp.float32
    )


def heads_first(rows, group_count, head_size):
    shaped = rows.reshape(rows.shape[0], group_count, -1, head_size)
    return jnp.moveaxis(shaped, 1, 0)


def kv_first(rows, group_count, head_size):
    return jnp.moveaxis(rows.reshape(rows.shape[0], group_count, head_size), 1, 0)


def score_block(q_group, k_group, mask_rows, score_scale):
    raw_scores = (
        jnp.einsum("trd,ud->rtu", q_group, k_group, preferred_element_type=jnp.float32)
        * score_scale
    )
    return jnp.where(mask_rows[None], raw_scores, MASK_FILL)


def attend(pieces, score_scale, group_count, head_size):
    q_rows, key_rows, value_rows, mask_rows = pieces

    def attend_one_group(parts):
        q_group, k_group, v_group = parts
        masked = score_block(q_group, k_group, mask_rows, score_scale)
        row_max = jnp.max(masked, axis=-1)
        exp_terms = jnp.exp(masked - row_max[..., None])
        row_sum = jnp.sum(exp_terms, axis=-1)
        attn_prob = (exp_terms / row_sum[..., None]).astype(jnp.bfloat16)
        attended = jnp.einsum("rtu,ud->trd", attn_prob, v_group, preferred_element_type=jnp.float32)
        return (attended, row_max, row_sum)

    attended, row_max, row_sum = lax.map(
        attend_one_group,
        (
            heads_first(q_rows, group_count, head_size),
            kv_first(key_rows, group_count, head_size),
            kv_first(value_rows, group_count, head_size),
        ),
    )
    attended = jnp.moveaxis(attended, 0, 1)
    return (attended.reshape(q_rows.shape[0], -1), row_max, row_sum)


def score_grads(
    q_group, grad_group, k_group, v_group, mask_rows, row_max, row_sum, row_dot, score_scale
):
    masked = score_block(q_group, k_group, mask_rows, score_scale)
    attn_prob = jnp.exp(masked - row_max[..., None]) / row_sum[..., None]
    prob_grad = jnp.einsum("trd,ud->rtu", grad_group, v_group, preferred_element_type=jnp.float32)
    row_dot = jnp.sum(attn_prob * prob_grad, axis=-1)
    score_grad = (attn_prob * (prob_grad - row_dot[..., None])).astype(jnp.bfloat16)
    return (attn_prob.astype(jnp.bfloat16), score_grad, row_dot)


def on_device(
    tokens,
    cotangent,
    w_query,
    w_key,
    w_value,
    w_out,
    q_gain,
    k_gain,
    attn_gain,
    w_gate,
    w_up,
    w_down,
    mlp_gain,
    doc_lengths,
    block_order,
):
    micro_count = tokens.shape[0]
    block_len = tokens.shape[2]
    model_width = tokens.shape[3]
    seq_length = lax.axis_size("seq") * block_len
    head_count = w_query.shape[1] // HD
    group_count = w_key.shape[1] // HD
    score_scale = HD ** (-0.5)
    flat_tokens = tokens.reshape(micro_count * block_len, model_width)
    out_grad = cotangent.reshape(micro_count * block_len, model_width).astype(jnp.float32)
    first_lengths = doc_lengths[:, 0, 0]
    offsets = jnp.arange(block_len, dtype=jnp.int32)
    own_places = block_order[lax.axis_index("seq")] * block_len + offsets
    key_places = (block_order[:, None] * block_len + offsets[None, :]).reshape(seq_length)
    own_segments = (own_places[None, :] >= first_lengths[:, None]).astype(jnp.int32)
    all_segments = (key_places[None, :] >= first_lengths[:, None]).astype(jnp.int32)
    rot_places = (own_places[None, :] - own_segments * first_lengths[:, None]).reshape(-1)
    allowed = (own_segments[:, :, None] == all_segments[:, None, :]) & (
        key_places[None, None, :] <= own_places[None, :, None]
    )
    cos_table, sine_table = rope_tables(rot_places, HD)
    q_pre = product(flat_tokens, w_query)
    k_pre = product(flat_tokens, w_key)
    v_pre = product(flat_tokens, w_value)
    q_norm, q_hat, q_factor = rms_forward(q_pre, q_gain)
    k_norm, k_hat, k_factor = rms_forward(k_pre, k_gain)
    q_low = rotate(q_norm, cos_table, sine_table, head_count, 1.0).astype(jnp.bfloat16)
    k_low = rotate(k_norm, cos_table, sine_table, group_count, 1.0).astype(jnp.bfloat16)
    v_low = v_pre.astype(jnp.bfloat16)
    q_blocks = q_low.reshape(micro_count, block_len, -1)
    k_blocks = k_low.reshape(micro_count, block_len, -1)
    v_blocks = v_low.reshape(micro_count, block_len, -1)
    key_all, value_all = (
        lax.all_gather(k_blocks, "seq", axis=1, tiled=True),
        lax.all_gather(v_blocks, "seq", axis=1, tiled=True),
    )

    def forward_block(pieces):
        return attend(pieces, score_scale, group_count, HD)

    attended, row_max, row_sum = lax.map(forward_block, (q_blocks, key_all, value_all, allowed))
    att_low = attended.reshape(micro_count * block_len, -1).astype(jnp.bfloat16)
    attn_proj = product(att_low, w_out)
    attn_normed, attn_hat, attn_factor = rms_forward(attn_proj, attn_gain)
    hidden = flat_tokens.astype(jnp.float32) + attn_normed
    hidden_low = hidden.astype(jnp.bfloat16)
    gate_pre = product(hidden_low, w_gate)
    up_pre = product(hidden_low, w_up)
    mixed_low = (jax.nn.silu(gate_pre) * up_pre).astype(jnp.bfloat16)
    down_pre = product(mixed_low, w_down)
    down_normed, down_hat, down_factor = rms_forward(down_pre, mlp_gain)
    layer_out = (hidden + down_normed).astype(jnp.bfloat16).reshape(tokens.shape)
    down_grad, grad_mlp_gain = rms_backward(out_grad, mlp_gain, down_hat, down_factor)
    down_grad = down_grad.astype(jnp.bfloat16)
    grad_w_down = weight_grad(mixed_low, down_grad)
    mixed_grad = back_product(down_grad, w_down)
    sigmoid_gate = jax.nn.sigmoid(gate_pre)
    gate_grad = (
        mixed_grad * up_pre * sigmoid_gate * (1.0 + gate_pre * (1.0 - sigmoid_gate))
    ).astype(jnp.bfloat16)
    up_grad = (mixed_grad * gate_pre * sigmoid_gate).astype(jnp.bfloat16)
    grad_w_gate = weight_grad(hidden_low, gate_grad)
    grad_w_up = weight_grad(hidden_low, up_grad)
    hidden_grad = out_grad + back_product(gate_grad, w_gate) + back_product(up_grad, w_up)
    proj_grad, grad_attn_gain = rms_backward(hidden_grad, attn_gain, attn_hat, attn_factor)
    proj_grad = proj_grad.astype(jnp.bfloat16)
    grad_w_out = weight_grad(att_low, proj_grad)
    att_grad = back_product(proj_grad, w_out).astype(jnp.bfloat16)
    grad_blocks = att_grad.reshape(micro_count, block_len, -1)
    key_back, value_back = (key_all, value_all)

    def query_pass(pieces):
        q_rows, grad_rows, key_rows, value_rows, mask_rows, max_rows, sum_rows = pieces

        def query_one_group(parts):
            q_group, grad_group, k_group, v_group, max_group, sum_group = parts
            prob_low, score_grad, unused = score_grads(
                q_group,
                grad_group,
                k_group,
                v_group,
                mask_rows,
                max_group,
                sum_group,
                None,
                score_scale,
            )
            q_grad = (
                jnp.einsum("rtu,ud->trd", score_grad, k_group, preferred_element_type=jnp.float32)
                * score_scale
            )
            key_terms = (
                jnp.einsum("rtu,trd->ud", score_grad, q_group, preferred_element_type=jnp.float32)
                * score_scale
            )
            value_terms = jnp.einsum(
                "rtu,trd->ud", prob_low, grad_group, preferred_element_type=jnp.float32
            )
            return (q_grad, key_terms, value_terms)

        q_grad, key_terms, value_terms = lax.map(
            query_one_group,
            (
                heads_first(q_rows, group_count, HD),
                heads_first(grad_rows, group_count, HD),
                kv_first(key_rows, group_count, HD),
                kv_first(value_rows, group_count, HD),
                max_rows,
                sum_rows,
            ),
        )
        q_grad = jnp.moveaxis(q_grad, 0, 1).reshape(block_len, -1)
        key_terms = jnp.moveaxis(key_terms, 0, 1).reshape(seq_length, -1)
        value_terms = jnp.moveaxis(value_terms, 0, 1).reshape(seq_length, -1)
        key_own, value_own = (
            lax.psum_scatter(key_terms, "seq", scatter_dimension=0, tiled=True),
            lax.psum_scatter(value_terms, "seq", scatter_dimension=0, tiled=True),
        )
        return (q_grad, key_own, value_own)

    q_rot_grad, k_rot_grad, value_grad = lax.map(
        query_pass, (q_blocks, grad_blocks, key_back, value_back, allowed, row_max, row_sum)
    )
    q_rot_grad = q_rot_grad.reshape(micro_count * block_len, -1)
    k_rot_grad = k_rot_grad.reshape(micro_count * block_len, -1)
    v_grad = value_grad.reshape(micro_count * block_len, -1).astype(jnp.bfloat16)
    q_norm_grad = rotate(q_rot_grad, cos_table, sine_table, head_count, -1.0)
    k_norm_grad = rotate(k_rot_grad, cos_table, sine_table, group_count, -1.0)
    q_grad, grad_q_gain = rms_backward(q_norm_grad, q_gain, q_hat, q_factor)
    k_grad, grad_k_gain = rms_backward(k_norm_grad, k_gain, k_hat, k_factor)
    q_grad = q_grad.astype(jnp.bfloat16)
    k_grad = k_grad.astype(jnp.bfloat16)
    grad_w_query = weight_grad(flat_tokens, q_grad)
    grad_w_key = weight_grad(flat_tokens, k_grad)
    grad_w_value = weight_grad(flat_tokens, v_grad)
    input_grad = (
        hidden_grad
        + back_product(q_grad, w_query)
        + back_product(k_grad, w_key)
        + back_product(v_grad, w_value)
    )
    input_grad = input_grad.reshape(tokens.shape)
    summed = (
        lax.psum_scatter(grad_w_query, ("dp", "seq"), scatter_dimension=0, tiled=True),
        lax.psum_scatter(grad_w_key, ("dp", "seq"), scatter_dimension=0, tiled=True),
        lax.psum_scatter(grad_w_value, ("dp", "seq"), scatter_dimension=0, tiled=True),
        lax.psum_scatter(grad_w_out, ("dp", "seq"), scatter_dimension=0, tiled=True),
        lax.psum_scatter(grad_q_gain, ("dp", "seq"), scatter_dimension=0, tiled=True),
        lax.psum_scatter(grad_k_gain, ("dp", "seq"), scatter_dimension=0, tiled=True),
        lax.psum_scatter(grad_attn_gain, ("dp", "seq"), scatter_dimension=0, tiled=True),
        lax.psum_scatter(grad_w_gate, ("dp", "seq"), scatter_dimension=0, tiled=True),
        lax.psum_scatter(grad_w_up, ("dp", "seq"), scatter_dimension=0, tiled=True),
        lax.psum_scatter(grad_w_down, ("dp", "seq"), scatter_dimension=0, tiled=True),
        lax.psum_scatter(grad_mlp_gain, ("dp", "seq"), scatter_dimension=0, tiled=True),
    )
    return (
        layer_out,
        input_grad,
        summed[0],
        summed[1],
        summed[2],
        summed[3],
        summed[4],
        summed[5],
        summed[6],
        summed[7],
        summed[8],
        summed[9],
        summed[10],
    )


def rms_forward(inputs, gain_vec):
    factor = lax.rsqrt(jnp.mean(inputs * inputs, axis=-1, keepdims=True) + EPSILON)
    normal = inputs * factor
    return (normal * gain_vec, normal, factor)


def rms_backward(grad_in, gain_vec, normal, factor):
    weighted = grad_in * gain_vec
    gain_grad = jnp.sum(grad_in * normal, axis=0)
    inner_mean = jnp.mean(weighted * normal, axis=-1, keepdims=True)
    return (factor * (weighted - normal * inner_mean), gain_grad)


def split_by_heads(
    tokens, cotangent, w_query, w_key, w_value, w_out, q_gain, k_gain, attn_gain,
    w_gate, w_up, w_down, mlp_gain, doc_lengths, block_order,
):
    micro_count, _, block_len, width = tokens.shape
    own_tokens = tokens[:, 0]
    flat_tokens = tokens.reshape(micro_count * block_len, width)
    out_grad = cotangent.reshape(micro_count * block_len, width).astype(WIDE)
    first = doc_lengths[:, 0, 0]
    cos, sine = rope_constants(1024)
    index = jnp.arange(16, dtype=jnp.int32)
    inverse = jnp.sum(jnp.where(block_order[None, :] == index[:, None], index[None, :], 0), axis=1).astype(jnp.int32)
    q_gain_rows, k_gain_rows = q_gain.reshape(16, HD), k_gain.reshape(8, HD)
    att_tok, tok_nat, q_pair, kv_nat, hat, factors, lse, att_nat = row_forward(
        own_tokens, w_query, w_key, w_value, q_gain_rows, k_gain_rows, cos, sine, block_order, inverse, first
    )
    attn_proj = dot(att_tok.reshape(micro_count * block_len, -1), w_out)
    attn_normed, attn_hat, attn_factor = rms_forward(attn_proj, attn_gain)
    hidden = flat_tokens.astype(WIDE) + attn_normed
    hidden_low = hidden.astype(LOW)
    gate_pre = dot(hidden_low, w_gate)
    up_pre = dot(hidden_low, w_up)
    sigmoid_gate = jax.nn.sigmoid(gate_pre)
    mixed_low = (gate_pre * sigmoid_gate * up_pre).astype(LOW)
    down_pre = dot(mixed_low, w_down)
    down_normed, down_hat, down_factor = rms_forward(down_pre, mlp_gain)
    layer_out = (hidden + down_normed).astype(LOW).reshape(tokens.shape)
    down_grad, grad_mlp_gain = rms_backward(out_grad, mlp_gain, down_hat, down_factor)
    down_grad = down_grad.astype(LOW)
    mixed_grad = dot_nt(down_grad, w_down)
    gate_grad = (mixed_grad * up_pre * sigmoid_gate * (1.0 + gate_pre * (1.0 - sigmoid_gate))).astype(LOW)
    up_grad = (mixed_grad * gate_pre * sigmoid_gate).astype(LOW)
    hidden_grad = out_grad + dot_nt(gate_grad, w_gate) + dot_nt(up_grad, w_up)
    proj_grad, grad_attn_gain = rms_backward(hidden_grad, attn_gain, attn_hat, attn_factor)
    proj_grad = proj_grad.astype(LOW).reshape(micro_count, block_len, width)
    vec = jnp.concatenate([grad_attn_gain[None], grad_mlp_gain[None], jnp.zeros((6, width), WIDE)], axis=0)
    in_grad, g_query, g_key, g_value, g_out, vec_sum, gain_sum, g_gate, g_up, g_down = row_backward(
        proj_grad, hidden_low, down_grad, gate_grad, up_grad, mixed_low, hidden_grad, vec,
        tok_nat, q_pair, kv_nat, hat, factors, lse, att_nat,
        w_out, w_query, w_key, w_value, q_gain_rows, k_gain_rows, cos, sine, block_order, inverse, first,
    )
    seq = lax.axis_index("seq")
    me = lax.axis_index("dp") * 16 + seq
    part = seq % 4
    return (
        layer_out,
        in_grad.reshape(tokens.shape),
        g_query,
        g_key,
        g_value,
        g_out,
        lax.dynamic_slice(gain_sum, (0, part * 64), (1, 64))[0],
        lax.dynamic_slice(gain_sum, (0, 256 + part * 32), (1, 32))[0],
        lax.dynamic_slice(vec_sum, (0, me * 32), (1, 32))[0],
        g_gate,
        g_up,
        g_down,
        lax.dynamic_slice(vec_sum, (1, me * 32), (1, 32))[0],
    )


SPECS_IN = (
    P(None, "dp", "seq", None), P(None, "dp", "seq", None),
    P(), P(), P(), P(), P(), P(), P(), P(), P(), P(), P(),
    P(None, "dp", None), P(),
)
SPECS_OUT = (
    P(None, "dp", "seq", None), P(None, "dp", "seq", None),
    P(("dp", "seq"), None), P(("dp", "seq"), None), P(("dp", "seq"), None), P(("dp", "seq"), None),
    P(("dp", "seq")), P(("dp", "seq")), P(("dp", "seq")),
    P(("dp", "seq"), None), P(("dp", "seq"), None), P(("dp", "seq"), None),
    P(("dp", "seq")),
)


def solution(mesh):
    body = split_by_heads if mesh.shape["seq"] == 16 and mesh.shape["dp"] == 2 else on_device
    return jax.shard_map(body, mesh=mesh, in_specs=SPECS_IN, out_specs=SPECS_OUT, check_vma=False)
```

```python
import functools

import jax
import jax.numpy as jnp
import numpy as np
from jax import lax
from jax.experimental import pallas as pl
from jax.experimental.pallas import tpu as pltpu
from jax.sharding import PartitionSpec as P

HD = 128
EPSILON = 1e-06
ROPE_BASE = 500000.0
MASK_FILL = -1e30
MESH = pl.DeviceIdType.MESH
LOW = jnp.bfloat16
WIDE = jnp.float32
TILE = 128
CHUNK = 256


def remote(source, target, send_sem, recv_sem, place):
    return pltpu.make_async_remote_copy(
        src_ref=source,
        dst_ref=target,
        send_sem=send_sem,
        recv_sem=recv_sem,
        device_id=place,
        device_id_type=MESH,
    )


def dot(left, right):
    return jnp.dot(left, right, preferred_element_type=WIDE)


def dot_nt(left, right):
    return lax.dot_general(left, right, (((1,), (1,)), ((), ())), preferred_element_type=WIDE)


def dot_tn(left, right):
    return lax.dot_general(left, right, (((0,), (0,)), ((), ())), preferred_element_type=WIDE)


class Spot:
    def __init__(self):
        self.dp = lax.axis_index("dp")
        self.seq = lax.axis_index("seq")
        self.core = self.seq % 2
        self.chip = self.seq // 2
        self.x = self.chip % 2
        self.z = self.chip // 2
        self.sibling = self.seq + 1 - 2 * self.core
        self.flip_x = self.seq + 2 - 4 * self.x
        self.far_z = (
            self.z + 1 - 2 * (self.z % 2),
            self.z + 2 - 4 * (self.z // 2),
            3 - self.z,
        )


def greet_row(spot, devices):
    barrier = pltpu.get_barrier_semaphore()
    for step in range(1, devices):
        pl.semaphore_signal(
            barrier,
            inc=1,
            device_id=(spot.dp, (spot.seq + step) % devices),
            device_id_type=MESH,
        )
    pl.semaphore_wait(barrier, devices - 1)


class RowGather:
    def __init__(self, spot, own, held, local_sem, send_sems, recv_sems):
        self.spot, self.own, self.held = spot, own, held
        self.send_sems, self.recv_sems = send_sems, recv_sems
        self.sent = []
        self.local = pltpu.make_async_copy(own.at[spot.core], held.at[spot.seq], local_sem)

    def send(self, source, slots, recv_sem, target):
        copy = remote(
            source, slots, self.send_sems.at[len(self.sent)], recv_sem, (self.spot.dp, target)
        )
        copy.start()
        self.sent.append(copy)

    def start(self):
        spot = self.spot
        own_slot = self.held.at[spot.seq]
        own_sem = self.recv_sems.at[spot.seq]
        for far in spot.far_z:
            for micro in range(2):
                self.send(self.own.at[micro], own_slot, own_sem, far * 4 + spot.x * 2 + micro)
        for micro in range(2):
            self.send(
                self.own.at[micro], own_slot, own_sem, spot.z * 4 + (1 - spot.x) * 2 + micro
            )
        self.send(self.own.at[1 - spot.core], own_slot, own_sem, spot.sibling)
        self.local.start()

    def arrived(self, slots, recv_sem):
        remote(slots, slots, self.send_sems.at[0], recv_sem, (self.spot.dp, self.spot.sibling)).wait_recv()

    def forward(self):
        spot = self.spot
        for far in spot.far_z:
            first = far * 4 + spot.x * 2
            for core in range(2):
                self.arrived(self.held.at[first + core], self.recv_sems.at[first + core])
            pair = self.held.at[pl.ds(first, 2)]
            self.send(pair, pair, self.recv_sems.at[16 + far], spot.flip_x)

    def finish(self):
        spot = self.spot
        self.arrived(self.held.at[spot.sibling], self.recv_sems.at[spot.sibling])
        for core in range(2):
            slot = spot.z * 4 + (1 - spot.x) * 2 + core
            self.arrived(self.held.at[slot], self.recv_sems.at[slot])
        for far in spot.far_z:
            first = far * 4 + (1 - spot.x) * 2
            self.arrived(self.held.at[pl.ds(first, 2)], self.recv_sems.at[16 + far])
        self.local.wait()
        for copy in self.sent:
            copy.wait_send()


GATHER_SENDS = 12
GATHER_RECVS = 20


def rope_rows(table, block, first_length):
    start = block * 64
    inside = table[pl.ds(64 + start, 64), :]
    shifted = table[pl.ds(64 + jnp.maximum(start - first_length, -64), 64), :]
    places = start + lax.broadcasted_iota(jnp.int32, (64, HD), 0)
    return jnp.where(places < first_length, inside, shifted)


def swap_halves(head):
    return pltpu.roll(head, HD // 2, axis=1)


def columns_of(rows):
    return jnp.concatenate([rows] * 16, axis=0).T[:, :8]


def rows_of(first, second):
    lane = lax.broadcasted_iota(jnp.int32, (first.shape[0], HD), 1)
    return jnp.where(lane == 0, first, second).T[:8]


def allowed_places(tile, count, first_length):
    keys = lax.broadcasted_iota(jnp.int32, (count, 2 * TILE), 0)
    lanes = lax.broadcasted_iota(jnp.int32, (1, 2 * TILE), 1)
    queries = tile * TILE + lanes % TILE
    earliest = jnp.where(queries < first_length, 0, first_length)
    return (keys >= earliest) & (keys <= queries)


def invert(order_ref, inverse_ref):
    def fill(block, carry):
        place = jnp.int32(0)
        for slot in range(16):
            place = jnp.maximum(place, jnp.where(order_ref[slot] == block, slot, 0))
        inverse_ref[block] = place
        return carry

    lax.fori_loop(0, 16, fill, 0)


def forward_kernel(
    tok_ref, wq_hbm, wk_hbm, wv_hbm, qgain_ref, kgain_ref, cos_ref, sine_ref,
    order_ref, docs_ref,
    att_tok, tok_nat, q_pair, kv_nat, hat, factors, lse,
    att_nat, tok_all, w_own, stat_all, att_send, att_recv, kv_turned,
    inverse_ref, local_sems, send_sems, recv_sems, stat_send, stat_recv, att_ssem, att_rsem,
):
    spot = Spot()
    devices = 16
    chips = 8
    chip = spot.chip
    loads = [
        pltpu.make_async_copy(wq_hbm.at[:, pl.ds(pl.multiple_of(chip * 256, 256), 256)], w_own.at[:, pl.ds(0, 256)], local_sems.at[1]),
        pltpu.make_async_copy(wk_hbm.at[:, pl.ds(pl.multiple_of(chip * 128, 128), 128)], w_own.at[:, pl.ds(256, 128)], local_sems.at[2]),
        pltpu.make_async_copy(wv_hbm.at[:, pl.ds(pl.multiple_of(chip * 128, 128), 128)], w_own.at[:, pl.ds(384, 128)], local_sems.at[3]),
    ]
    for load in loads:
        load.start()
    greet_row(spot, devices)
    gather = RowGather(spot, tok_ref, tok_all, local_sems.at[0], send_sems, recv_sems)
    gather.start()
    invert(order_ref, inverse_ref)
    gather.forward()
    for load in loads:
        load.wait()
    gather.finish()

    first_length = docs_ref[spot.core, 0, 0]
    for part in range(4):
        rows = pl.ds(part * CHUNK, CHUNK)
        chunk = jnp.concatenate([tok_all[inverse_ref[part * 4 + piece]] for piece in range(4)], axis=0)
        tok_nat[rows, :] = chunk
        pre = dot(chunk, w_own[...])
        hat[rows, :] = pre[:, :384]
        kv_nat[rows, 128:] = pre[:, 384:].astype(LOW)
        squares = pre[:, :384] * pre[:, :384]
        stat_all[pl.ds(chip, 1), :, rows] = rows_of(
            jnp.sum(squares[:, :256], axis=-1, keepdims=True),
            jnp.sum(squares[:, 256:], axis=-1, keepdims=True),
        )[None]
    stat_copies = []
    for step in range(1, chips):
        other = (chip + step) % chips
        copy = remote(
            stat_all.at[chip], stat_all.at[chip], stat_send.at[step - 1], stat_recv.at[chip],
            (spot.dp, other * 2 + spot.core),
        )
        copy.start()
        stat_copies.append(copy)
    for step in range(1, chips):
        other = (chip + step) % chips
        remote(
            stat_all.at[other], stat_all.at[other], stat_send.at[0], stat_recv.at[other],
            (spot.dp, spot.sibling),
        ).wait_recv()
    total = stat_all[0]
    for other in range(1, chips):
        total = total + stat_all[other]
    width = jnp.where(lax.broadcasted_iota(jnp.int32, total.shape, 0) == 0, 1.0 / 2048, 1.0 / 1024)
    factors[...] = lax.rsqrt(total * width + EPSILON)
    qgain = qgain_ref[pl.ds(chip * 2, 2), :]
    kgain = kgain_ref[pl.ds(chip, 1), :]
    for part in range(8):
        rows = pl.ds(part * TILE, TILE)
        scale = columns_of(factors[:, rows])
        cos = jnp.concatenate([rope_rows(cos_ref, part * 2 + piece, first_length) for piece in range(2)], axis=0)
        sine = jnp.concatenate([rope_rows(sine_ref, part * 2 + piece, first_length) for piece in range(2)], axis=0)
        for head in range(3):
            lanes = pl.ds(head * HD, HD)
            column = scale[:, 0:1] if head < 2 else scale[:, 1:2]
            gain = qgain[head : head + 1] if head < 2 else kgain
            normal = hat[rows, lanes] * column
            hat[rows, lanes] = normal
            normed = normal * gain
            turned = (normed * cos + swap_halves(normed) * sine).astype(LOW)
            if head < 2:
                q_pair[part, pl.ds(head * HD, HD), :] = turned
            else:
                kv_nat[rows, :HD] = turned
    kv_turned[...] = kv_nat[:, HD:].T
    for tile in range(8):
        count = (tile + 1) * TILE
        scores = dot_nt(kv_nat[:count, :HD], q_pair[tile]) * HD ** (-0.5)
        masked = jnp.where(allowed_places(tile, count, first_length), scores, MASK_FILL)
        top = jnp.max(masked, axis=0, keepdims=True)
        terms = jnp.exp(masked - top)
        weight = jnp.sum(terms, axis=0, keepdims=True)
        lse[pl.ds(tile, 1), :] = top + jnp.log(weight)
        turned = dot(kv_turned[:, :count], terms.astype(LOW)) / weight
        attended = turned.T.astype(LOW)
        att_nat[pl.ds(tile * 2, 2), :, :HD] = attended[:TILE].reshape(2, 64, HD)
        att_nat[pl.ds(tile * 2, 2), :, HD:] = attended[TILE:].reshape(2, 64, HD)
    own_part = (spot.core, slice(None), pl.ds(pl.multiple_of(chip * 256, 256), 256))
    att_recv[pl.ds(chip, 1), pl.ds(spot.core, 1)] = att_nat[order_ref[spot.seq]][None, None]
    sent = []
    for step in range(1, devices):
        other = (spot.seq + step) % devices
        att_send[step] = att_nat[order_ref[other]]
        copy = remote(
            att_send.at[step], att_recv.at[chip, spot.core], att_ssem.at[step],
            att_rsem.at[spot.seq], (spot.dp, other),
        )
        copy.start()
        sent.append(copy)
    for step in range(1, devices):
        other = (spot.seq + step) % devices
        slot = att_recv.at[other // 2, other % 2]
        remote(slot, slot, att_ssem.at[0], att_rsem.at[other], (spot.dp, spot.sibling)).wait_recv()
    for piece in range(chips):
        for micro in range(2):
            att_tok[micro, :, piece * 256 : (piece + 1) * 256] = att_recv[piece, micro]
    for copy in sent + stat_copies:
        copy.wait_send()


def rope_constants(length):
    frequency = np.power(np.float32(ROPE_BASE), -np.arange(0, HD, 2).astype(np.float32) / np.float32(HD)).astype(np.float32)
    angles = (np.arange(length, dtype=np.float32)[:, None] * frequency[None, :]).astype(np.float32).astype(np.float64)
    cos, sine = np.cos(angles), np.sin(angles)
    front = np.zeros((64, HD))
    cos = np.concatenate([front, np.concatenate([cos, cos], axis=1)], axis=0)
    sine = np.concatenate([front, np.concatenate([-sine, sine], axis=1)], axis=0)
    return jnp.asarray(cos, WIDE), jnp.asarray(sine, WIDE)


def row_forward(tokens, w_query, w_key, w_value, q_gain, k_gain, cos, sine, order, docs):
    length = 1024
    width = tokens.shape[-1]
    any_spec = pl.BlockSpec(memory_space=pl.ANY)
    vmem = pl.BlockSpec(memory_space=pltpu.VMEM)
    smem = pl.BlockSpec(memory_space=pltpu.SMEM)
    shape = jax.ShapeDtypeStruct
    return pl.pallas_call(
        forward_kernel,
        out_shape=(
            shape((2, 64, 2048), LOW),
            shape((length, width), LOW),
            shape((8, 2 * TILE, HD), LOW),
            shape((length, 2 * HD), LOW),
            shape((length, 3 * HD), WIDE),
            shape((8, length), WIDE),
            shape((8, 2 * TILE), WIDE),
        ),
        in_specs=[vmem, any_spec, any_spec, any_spec, vmem, vmem, vmem, vmem, smem, smem],
        out_specs=(vmem,) * 7,
        scratch_shapes=[
            pltpu.VMEM((16, 64, 2 * HD), LOW),
            pltpu.VMEM((16, 64, width), LOW),
            pltpu.VMEM((width, 512), LOW),
            pltpu.VMEM((8, 8, length), WIDE),
            pltpu.VMEM((16, 64, 2 * HD), LOW),
            pltpu.VMEM((8, 2, 64, 2 * HD), LOW),
            pltpu.VMEM((HD, length), LOW),
            pltpu.SMEM((16,), jnp.int32),
            pltpu.SemaphoreType.DMA((4,)),
            pltpu.SemaphoreType.DMA((GATHER_SENDS,)),
            pltpu.SemaphoreType.DMA((GATHER_RECVS,)),
            pltpu.SemaphoreType.DMA((8,)),
            pltpu.SemaphoreType.DMA((8,)),
            pltpu.SemaphoreType.DMA((16,)),
            pltpu.SemaphoreType.DMA((16,)),
        ],
        compiler_params=pltpu.CompilerParams(
            collective_id=0, has_side_effects=True, vmem_limit_bytes=56 * 2**20
        ),
        name="row_forward",
    )(tokens, w_query, w_key, w_value, q_gain, k_gain, cos, sine, order, docs)


class Post:
    def __init__(self, sems):
        self.sems, self.started, self.used = sems, [], 0

    def send(self, source, target, recv_sem, place, when=None):
        copy = remote(source, target, self.sems.at[self.used], recv_sem, place)
        self.used += 1
        self.started.append((copy, when))
        if when is None:
            copy.start()
        else:
            pl.when(when)(copy.start)

    def finish(self):
        for copy, when in self.started:
            if when is None:
                copy.wait_send()
            else:
                pl.when(when)(copy.wait_send)


def arrived(spot, slot, recv_sem, spare_sem):
    remote(slot, slot, spare_sem, recv_sem, (spot.dp, spot.sibling)).wait_recv()


def aligned(start, size):
    return pl.ds(pl.multiple_of(start, size), size)


class AlongZ:
    def __init__(self, spot, post, spare):
        self.spot, self.post, self.spare = spot, post, spare
        half = spot.z // 2
        self.partner = spot.far_z[0]
        self.far_inner = 2 - half
        self.far_outer = 3 - 3 * half
        self.inner = ((spot.z + 1) // 2) % 2 == 1
        self.outer = ((spot.z + 1) // 2) % 2 == 0

    def place(self, z):
        return (self.spot.dp, z * 4 + self.spot.x * 2 + self.spot.core)

    def send(self, part, size, landing, transit, sems):
        spot, post = self.spot, self.post
        landing[2] = part[aligned(spot.z * size, size), :]
        post.send(part.at[aligned(self.partner * size, size)], landing.at[0], sems.at[0], self.place(self.partner))
        for slot, far in enumerate((self.far_inner, self.far_outer)):
            post.send(
                part.at[aligned(far * size, size)], transit.at[slot], sems.at[2 + slot], self.place(self.partner),
                self.outer,
            )

    def combine(self, part, size, landing, transit, sems):
        for slot, far in enumerate((self.far_inner, self.far_outer)):

            @pl.when(self.inner)
            def _():
                arrived(self.spot, transit.at[slot], sems.at[2 + slot], self.spare)
                added = transit[slot].astype(WIDE) + part[aligned(far * size, size), :].astype(WIDE)
                transit[slot] = added.astype(LOW)

            self.post.send(transit.at[slot], landing.at[1], sems.at[1], self.place(far), self.inner)

    def total(self, landing, sems):
        arrived(self.spot, landing.at[0], sems.at[0], self.spare)
        arrived(self.spot, landing.at[1], sems.at[1], self.spare)
        return landing[0].astype(WIDE) + landing[1].astype(WIDE) + landing[2].astype(WIDE)


def row_scale(values):
    return lax.rsqrt(jnp.mean(values * values, axis=-1, keepdims=True) + EPSILON)


def norm_back(grad, gain, normal, factor):
    weighted = grad * gain
    return factor * (weighted - normal * jnp.mean(weighted * normal, axis=-1, keepdims=True))


def backward_kernel(
    att_ref, tok_ref, cot_ref, again_ref, mgain_ref, qgain_ref, kgain_ref, factors, lse,
    tok_hbm, q_hbm, kv_hbm, hat_hbm, cos_hbm, sine_hbm,
    wout_hbm, wg_hbm, wu_hbm, wd_hbm, wq_hbm, wk_hbm, wv_hbm, order_ref, docs_ref,
    layer_out, in_grad, g_query, g_key, g_value, g_out, vec_out, gain_out, g_gate, g_up, g_down,
    wout, wgate, wup, wdown, q_pair, kv_nat, hat, cos_ref, sine_ref,
    att_hat, hidden, hid_own, gate_pre, up_pre, mixed, mix_turned, att_turned, down_own, gu_own, proj_own, ag_own, vec_own,
    hid_all, down_all, proj_all, gu_all, mix_all, att_all, vec_all, vec_far,
    down_land, down_transit, wout_part, wout_land, wout_transit, gu_land, gu_transit,
    ag_recv, ag_pair, k_turned, stat_all, grad_nat, grad_recv, part_sib, wqkv_recv, gain_own, gain_recv,
    inverse_ref, local_sems, post_sems, plane_sems, vec_sems, down_sems, wout_sems, gu_sems, gut_sems, ag_sems, stat_sems, grad_sems, sib_sem, wqkv_sems, gain_sems,
):
    spot = Spot()
    devices, chips = 16, 8
    dp, seq, core, chip, z = spot.dp, spot.seq, spot.core, spot.chip, spot.z
    me = dp * devices + seq
    member = dp * 4 + spot.x * 2 + core
    spare = post_sems.at[0]
    post = Post(post_sems)
    along = AlongZ(spot, post, spare)

    def load(source, target, index):
        copy = pltpu.make_async_copy(source, target, local_sems.at[index])
        copy.start()
        return copy

    barrier = pltpu.get_barrier_semaphore()
    for step in range(1, 2 * devices):
        other = (me + step) % (2 * devices)
        pl.semaphore_signal(barrier, inc=1, device_id=(other // devices, other % devices), device_id_type=MESH)
    load_out = load(wout_hbm, wout, 0)
    load_gate = load(wg_hbm, wgate, 1)
    load_up = load(wu_hbm, wup, 2)
    load_down = load(wd_hbm, wdown, 3)
    later = [load(kv_hbm, kv_nat, 4), load(q_hbm, q_pair, 5), load(hat_hbm, hat, 6), load(cos_hbm, cos_ref, 7), load(sine_hbm, sine_ref, 8)]
    invert(order_ref, inverse_ref)

    for group in range(8):
        block = att_ref[:, :, group * 256 : (group + 1) * 256].reshape(128, 256).T
        for piece in range(4):
            att_turned[(group // 4) * 4 + piece, pl.ds((group % 4) * 64, 64), :] = block[piece * 64 : (piece + 1) * 64]
    load_out.wait()
    attn_proj = dot(att_ref[...].reshape(128, 2048), wout[...])
    att_factor = row_scale(attn_proj)
    normal = attn_proj * att_factor
    att_hat[...] = normal
    stream = tok_ref[...].reshape(128, 1024).astype(WIDE) + normal * again_ref[...]
    hidden[...] = stream
    hid_own[...] = stream.astype(LOW)
    pl.semaphore_wait(barrier, 2 * devices - 1)

    plane_places = ((dp, spot.flip_x), (1 - dp, seq), (1 - dp, spot.flip_x))
    plane_members = (
        dp * 4 + (1 - spot.x) * 2 + core,
        (1 - dp) * 4 + spot.x * 2 + core,
        (1 - dp) * 4 + (1 - spot.x) * 2 + core,
    )
    sib_place = (dp, spot.sibling)
    keeps = {}

    def spread(own, held, kind, index):
        keeps[kind] = load(own, held.at[member], index)
        for place in plane_places + (sib_place,):
            post.send(own, held.at[member], plane_sems.at[kind, member], place)

    def pass_on(held, kind):
        for other in plane_members:
            arrived(spot, held.at[other], plane_sems.at[kind, other], spare)
            post.send(held.at[other], held.at[other], plane_sems.at[kind, other], sib_place)

    def whole(held, kind):
        keeps[kind].wait()
        for y in range(2):
            for x in range(2):
                other = y * 4 + x * 2 + 1 - core
                arrived(spot, held.at[other], plane_sems.at[kind, other], spare)

    def deal(own, held, kind, index):
        keeps[kind] = load(own.at[member], held.at[member], index)
        for step in range(1, 8):
            other = (member + step) % 8
            post.send(own.at[other], held.at[member], plane_sems.at[kind, member], (other // 4, z * 4 + other % 4))

    def dealt(held, kind):
        keeps[kind].wait()
        for step in range(1, 8):
            other = (member + step) % 8
            arrived(spot, held.at[other], plane_sems.at[kind, other], spare)

    spread(hid_own, hid_all, 0, 9)
    deal(att_turned, att_all, 3, 10)

    load_gate.wait()
    load_up.wait()
    for group in range(8):
        lanes = slice(group * 384, (group + 1) * 384)
        gate = dot(hid_own[...], wgate[:, lanes])
        up = dot(hid_own[...], wup[:, lanes])
        gate_pre[group] = gate
        up_pre[group] = up
        block = (gate * jax.nn.sigmoid(gate) * up).astype(LOW)
        mixed[:, lanes] = block
        turned = block.T
        for piece in range(4):
            mix_turned[(group // 4) * 4 + piece, pl.ds((group % 4) * 96, 96), :] = turned[piece * 96 : (piece + 1) * 96]
    deal(mix_turned, mix_all, 4, 11)
    load_down.wait()
    down_pre = dot(mixed[...], wdown[...])
    factor = row_scale(down_pre)
    normal = down_pre * factor
    cot = cot_ref[...].reshape(128, 1024).astype(WIDE)
    layer_out[...] = (hidden[...] + normal * mgain_ref[...]).astype(LOW)
    down_own[...] = norm_back(cot, mgain_ref[...], normal, factor).astype(LOW)
    vec_own[...] = jnp.zeros_like(vec_own)
    vec_own[1:2, :] = jnp.sum(cot * normal, axis=0, keepdims=True)
    spread(down_own, down_all, 1, 12)

    for step in range(1, 9):
        group = (member + step) % 8
        grad = dot_nt(down_own[...], wdown[aligned(group * 384, 384), :])
        gate, up = gate_pre[group], up_pre[group]
        sigmoid = jax.nn.sigmoid(gate)
        gu_own[group, :, :384] = (grad * up * sigmoid * (1.0 + gate * (1.0 - sigmoid))).astype(LOW)
        gu_own[group, :, 384:] = (grad * gate * sigmoid).astype(LOW)
        if step < 8:
            post.send(gu_own.at[group], gu_all.at[member], plane_sems.at[5, member], (group // 4, z * 4 + group % 4))
    keeps[5] = load(gu_own.at[member], gu_all.at[member], 13)
    hgrad = cot
    for group in range(8):
        lanes = slice(group * 384, (group + 1) * 384)
        hgrad = hgrad + dot_nt(gu_own[group, :, :384], wgate[:, lanes]) + dot_nt(gu_own[group, :, 384:], wup[:, lanes])
    hidden[...] = hgrad
    normal = att_hat[...]
    proj_own[...] = norm_back(hgrad, again_ref[...], normal, att_factor).astype(LOW)
    vec_own[0:1, :] = jnp.sum(hgrad * normal, axis=0, keepdims=True)
    load_query = load(wq_hbm, wgate.at[:, pl.ds(0, 2048)], 1)
    load_key = load(wk_hbm, wgate.at[:, pl.ds(2048, 1024)], 2)
    load_value = load(wv_hbm, wup.at[:, pl.ds(0, 1024)], 3)

    att_grad = dot_nt(proj_own[...], wout[...]).astype(LOW)
    ag_own[...] = att_grad.reshape(2, 64, 2048)
    keep_ag = load(ag_own.at[core, :, aligned(chip * 256, 256)], ag_recv.at[seq], 14)
    for step in range(1, devices):
        other = (seq + step) % devices
        post.send(
            ag_own.at[other % 2, :, aligned((other // 2) * 256, 256)], ag_recv.at[seq], ag_sems.at[seq], (dp, other)
        )
    load_tok = load(tok_hbm, wout.at[pl.ds(0, 1024)], 0)
    spread(proj_own, proj_all, 2, 15)
    keep_vec = load(vec_own, vec_all.at[member], 16)
    for step in range(1, 8):
        other = (member + step) % 8
        post.send(vec_own, vec_all.at[member], vec_sems.at[member], (other // 4, z * 4 + other % 4))
    pass_on(hid_all, 0)
    pass_on(down_all, 1)

    dealt(mix_all, 4)
    whole(down_all, 1)
    down_part = wdown.at[pl.ds(0, 384)]
    mixes = jnp.concatenate([mix_all[other] for other in range(8)], axis=1)
    down_part[...] = dot(mixes, down_all[...].reshape(1024, 1024)).astype(LOW)
    along.send(down_part, 96, down_land, down_transit, down_sems)
    pass_on(proj_all, 2)

    for copy in later:
        copy.wait()
    keep_ag.wait()
    for step in range(1, devices):
        other = (seq + step) % devices
        arrived(spot, ag_recv.at[other], ag_sems.at[other], spare)
    for tile in range(8):
        block = jnp.concatenate([ag_recv[inverse_ref[tile * 2 + piece]] for piece in range(2)], axis=0)
        ag_pair[tile, :TILE, :] = block[:, :HD]
        ag_pair[tile, TILE:, :] = block[:, HD:]
    k_turned[...] = kv_nat[:, :HD].T
    first_length = docs_ref[core, 0, 0]
    up_pre[:, :, :256] = jnp.zeros((8, TILE, 256), WIDE)
    for tile in range(8):
        count = (tile + 1) * TILE
        queries, grads = q_pair[tile], ag_pair[tile]
        scores = dot_nt(kv_nat[:count, :HD], queries) * HD ** (-0.5)
        masked = jnp.where(allowed_places(tile, count, first_length), scores, MASK_FILL)
        probs = jnp.exp(masked - lse[tile : tile + 1, :])
        prob_grad = dot_nt(kv_nat[:count, HD:], grads)
        row_dot = jnp.sum(probs * prob_grad, axis=0, keepdims=True)
        score_grad = (probs * (prob_grad - row_dot)).astype(LOW)
        up_pre[: tile + 1, :, :HD] += dot(score_grad, queries).reshape(tile + 1, TILE, HD)
        up_pre[: tile + 1, :, HD:256] += dot(probs.astype(LOW), grads).reshape(tile + 1, TILE, HD)
        turned = (dot(k_turned[:, :count], score_grad) * HD ** (-0.5)).T
        gate_pre[tile, :, :HD] = turned[:TILE]
        gate_pre[tile, :, HD:256] = turned[TILE:]

    qgain = qgain_ref[pl.ds(chip * 2, 2), :]
    kgain = kgain_ref[pl.ds(chip, 1), :]
    gains = [jnp.zeros((1, HD), WIDE) for _ in range(3)]
    for part in range(8):
        rows = pl.ds(part * TILE, TILE)
        cos = jnp.concatenate([rope_rows(cos_ref, part * 2 + piece, first_length) for piece in range(2)], axis=0)
        sine = jnp.concatenate([rope_rows(sine_ref, part * 2 + piece, first_length) for piece in range(2)], axis=0)
        dots = []
        for head in range(3):
            lanes = slice(head * HD, (head + 1) * HD)
            turned = gate_pre[part, :, lanes] if head < 2 else up_pre[part, :, :HD] * HD ** (-0.5)
            back = turned * cos - swap_halves(turned) * sine
            normal = hat[rows, lanes]
            gain = qgain[head : head + 1] if head < 2 else kgain
            gains[head] = gains[head] + jnp.sum(back * normal, axis=0, keepdims=True)
            weighted = back * gain
            if head < 2:
                gate_pre[part, :, lanes] = weighted
            else:
                up_pre[part, :, :HD] = weighted
            dots.append(jnp.sum(weighted * normal, axis=-1, keepdims=True))
        stat_all[pl.ds(chip, 1), :, rows] = rows_of(dots[0] + dots[1], dots[2])[None]
    for step in range(1, chips):
        other = (chip + step) % chips
        post.send(stat_all.at[chip], stat_all.at[chip], stat_sems.at[chip], (dp, other * 2 + core))
    gain_own[...] = jnp.concatenate([jnp.broadcast_to(gain, (8, HD)) for gain in gains], axis=1)
    for piece in range(4):
        target = chip * 4 + piece
        slot = gain_recv.at[dp * 2 + core]

        @pl.when(target == me)
        def _():
            gain_recv[pl.ds(dp * 2 + core, 1)] = gain_own[...][None]

        post.send(gain_own, slot, gain_sems.at[dp * 2 + core], (target // devices, target % devices), target != me)

    keeps[5].wait()
    for step in range(1, 8):
        other = (member + step) % 8
        arrived(spot, gu_all.at[other], plane_sems.at[5, other], spare)
    whole(hid_all, 0)
    gu_part = wout.at[pl.ds(1024, 1024), pl.ds(0, 768)]
    gu_part[...] = dot_tn(hid_all[...].reshape(1024, 1024), gu_all[...].reshape(1024, 768)).astype(LOW)
    for y in range(2):
        for slot, far in enumerate((along.far_inner, along.far_outer)):
            post.send(
                gu_part.at[aligned(y * 512 + far * 128, 128)], gu_transit.at[slot, y], gut_sems.at[slot, y],
                along.place(along.partner), along.outer,
            )
    for step in range(8):
        other = (member + step) % 8
        first = (other // 4) * 512 + (other % 4) * 32
        post.send(
            gu_part.at[aligned(first + along.partner * 128, 32)], gu_land.at[0, member], gu_sems.at[0, member],
            (other // 4, along.partner * 4 + other % 4),
        )
        if step > 0:
            post.send(
                gu_part.at[aligned(first + z * 128, 32)], gu_land.at[2, member], gu_sems.at[2, member],
                (other // 4, z * 4 + other % 4),
            )
    gu_land[2, pl.ds(member, 1)] = gu_part[aligned((member // 4) * 512 + z * 128 + (member % 4) * 32, 32), :][None]

    for step in range(1, chips):
        other = (chip + step) % chips
        arrived(spot, stat_all.at[other], stat_sems.at[other], spare)
    total = stat_all[0]
    for other in range(1, chips):
        total = total + stat_all[other]
    width = jnp.where(lax.broadcasted_iota(jnp.int32, total.shape, 0) == 0, 1.0 / 2048, 1.0 / 1024)
    means = total * width
    grad_send = wdown.at[pl.ds(1024, 1024), pl.ds(512, 512)]
    for part in range(8):
        rows = pl.ds(part * TILE, TILE)
        mean = columns_of(means[:, part * TILE : (part + 1) * TILE])
        scale = columns_of(factors[:, rows])
        for head in range(3):
            column = 0 if head < 2 else 1
            weighted = gate_pre[part, :, head * HD : (head + 1) * HD] if head < 2 else up_pre[part, :, :HD]
            normal = hat[rows, pl.ds(head * HD, HD)]
            grad = scale[:, column : column + 1] * (weighted - normal * mean[:, column : column + 1])
            grad_nat[pl.ds(part * 2, 2), :, head * HD : (head + 1) * HD] = grad.astype(LOW).reshape(2, 64, HD)
        grad_nat[pl.ds(part * 2, 2), :, 3 * HD :] = up_pre[part, :, HD:256].astype(LOW).reshape(2, 64, HD)
    grad_recv[pl.ds(chip, 1), pl.ds(core, 1)] = grad_nat[order_ref[seq]][None, None]
    for step in range(1, devices):
        other = (seq + step) % devices
        rows = pl.ds(step * 64, 64)
        grad_send[rows, :] = grad_nat[order_ref[other]]
        post.send(grad_send.at[rows], grad_recv.at[chip, core], grad_sems.at[seq], (dp, other))

    load_tok.wait()
    part_low = wdown.at[pl.ds(2048, 1024), pl.ds(0, 512)]
    part_low[...] = dot_tn(wout[:1024, :], grad_nat[...].reshape(1024, 512)).astype(LOW)
    post.send(part_low.at[aligned((1 - core) * 512, 512)], part_sib, sib_sem.at[0], sib_place)

    along.combine(down_part, 96, down_land, down_transit, down_sems)
    for slot, far in enumerate((along.far_inner, along.far_outer)):
        for y in range(2):

            @pl.when(along.inner)
            def _():
                arrived(spot, gu_transit.at[slot, y], gut_sems.at[slot, y], spare)
                added = gu_transit[slot, y].astype(WIDE) + gu_part[aligned(y * 512 + far * 128, 128), :].astype(WIDE)
                gu_transit[slot, y] = added.astype(LOW)

            for piece in range(4):
                post.send(
                    gu_transit.at[slot, y, pl.ds(piece * 32, 32)], gu_land.at[1, member], gu_sems.at[1, member],
                    (y, far * 4 + piece), along.inner,
                )

    arrived(spot, part_sib, sib_sem.at[0], spare)
    part_sum = wdown.at[pl.ds(2048, 512), pl.ds(512, 512)]
    part_sum[...] = (part_low[aligned(core * 512, 512), :].astype(WIDE) + part_sib[...].astype(WIDE)).astype(LOW)
    own_slot = dp * chips + chip

    @pl.when(core == dp)
    def _():
        wqkv_recv[pl.ds(own_slot, 1)] = part_sum[aligned(seq * 32, 32), :][None]

    post.send(part_sum.at[aligned(seq * 32, 32)], wqkv_recv.at[own_slot], wqkv_sems.at[own_slot], (1 - dp, seq), core != dp)
    for step in range(1, devices):
        other = (seq + step) % devices
        post.send(part_sum.at[aligned(other * 32, 32)], wqkv_recv.at[own_slot], wqkv_sems.at[own_slot], (core, other))

    dealt(att_all, 3)
    whole(proj_all, 2)
    turned = jnp.concatenate([att_all[other] for other in range(8)], axis=1)
    wout_part[...] = dot(turned, proj_all[...].reshape(1024, 1024)).astype(LOW)
    along.send(wout_part, 64, wout_land, wout_transit, wout_sems)
    keep_vec.wait()
    for step in range(1, 8):
        other = (member + step) % 8
        arrived(spot, vec_all.at[other], vec_sems.at[other], spare)
    vec = vec_all[0]
    for other in range(1, 8):
        vec = vec + vec_all[other]
    vec_far[pl.ds(z, 1)] = vec[None]
    for far in spot.far_z:
        post.send(vec_far.at[z], vec_far.at[z], vec_sems.at[8 + z], along.place(far))
    along.combine(wout_part, 64, wout_land, wout_transit, wout_sems)

    for step in range(1, devices):
        other = (seq + step) % devices
        arrived(spot, grad_recv.at[other // 2, other % 2], grad_sems.at[other], spare)
    load_query.wait()
    load_key.wait()
    load_value.wait()
    grad_k, grad_v = [], []
    gradient = hidden[...]
    for piece in range(chips):
        block = grad_recv[piece].reshape(128, 512)
        gradient = gradient + dot_nt(block[:, :256], wgate[:, piece * 256 : (piece + 1) * 256])
        grad_k.append(block[:, 256:384])
        grad_v.append(block[:, 384:])
    gradient = gradient + dot_nt(jnp.concatenate(grad_k, axis=1), wgate[:, 2048:])
    in_grad[...] = gradient + dot_nt(jnp.concatenate(grad_v, axis=1), wup[:, :1024])

    for y in range(2):
        for micro in range(2):
            source = y * 2 + micro
            sender = y * devices + (me // 4) * 2 + micro

            @pl.when(sender != me)
            def _():
                arrived(spot, gain_recv.at[source], gain_sems.at[source], spare)

    gain_out[...] = sum(gain_recv[source] for source in range(4))
    for source in range(16):
        sender = (source // chips) * devices + (source % chips) * 2 + dp

        @pl.when(sender != me)
        def _():
            arrived(spot, wqkv_recv.at[source], wqkv_sems.at[source], spare)

    for piece in range(chips):
        block = wqkv_recv[piece].astype(WIDE) + wqkv_recv[chips + piece].astype(WIDE)
        g_query[:, piece * 256 : (piece + 1) * 256] = block[:, :256]
        g_key[:, piece * 128 : (piece + 1) * 128] = block[:, 256:384]
        g_value[:, piece * 128 : (piece + 1) * 128] = block[:, 384:]
    for far in spot.far_z:
        arrived(spot, vec_far.at[far], vec_sems.at[8 + far], spare)
    vec_out[...] = sum(vec_far[far] for far in range(4))
    g_down[...] = along.total(down_land, down_sems)
    for step in range(8):
        other = (member + step) % 8
        for kind in range(3):
            if kind < 2 or step > 0:
                arrived(spot, gu_land.at[kind, other], gu_sems.at[kind, other], spare)
    for slot in range(8):
        block = sum(gu_land[kind, slot].astype(WIDE) for kind in range(3))
        g_gate[:, slot * 384 : (slot + 1) * 384] = block[:, :384]
        g_up[:, slot * 384 : (slot + 1) * 384] = block[:, 384:]
    g_out[...] = along.total(wout_land, wout_sems)
    post.finish()


POST_SENDS = 288


def row_backward(*operands):
    length, width = 1024, 1024
    any_spec = pl.BlockSpec(memory_space=pl.ANY)
    vmem = pl.BlockSpec(memory_space=pltpu.VMEM)
    smem = pl.BlockSpec(memory_space=pltpu.SMEM)
    shape = jax.ShapeDtypeStruct
    dma = pltpu.SemaphoreType.DMA
    return pl.pallas_call(
        backward_kernel,
        out_shape=(
            shape((128, width), LOW),
            shape((128, width), WIDE),
            shape((32, 2048), WIDE),
            shape((32, 1024), WIDE),
            shape((32, 1024), WIDE),
            shape((64, 1024), WIDE),
            shape((8, 1024), WIDE),
            shape((8, 384), WIDE),
            shape((32, 3072), WIDE),
            shape((32, 3072), WIDE),
            shape((96, 1024), WIDE),
        ),
        in_specs=[vmem] * 9 + [any_spec] * 13 + [smem] * 2,
        out_specs=(vmem,) * 11,
        scratch_shapes=[
            pltpu.VMEM((2048, width), LOW),
            pltpu.VMEM((width, 3072), LOW),
            pltpu.VMEM((width, 3072), LOW),
            pltpu.VMEM((3072, width), LOW),
            pltpu.VMEM((8, 2 * TILE, HD), LOW),
            pltpu.VMEM((length, 2 * HD), LOW),
            pltpu.VMEM((length, 3 * HD), WIDE),
            pltpu.VMEM((length + 64, HD), WIDE),
            pltpu.VMEM((length + 64, HD), WIDE),
            pltpu.VMEM((128, width), WIDE),
            pltpu.VMEM((128, width), WIDE),
            pltpu.VMEM((128, width), LOW),
            pltpu.VMEM((8, 128, 384), WIDE),
            pltpu.VMEM((8, 128, 384), WIDE),
            pltpu.VMEM((128, 3072), LOW),
            pltpu.VMEM((8, 384, 128), LOW),
            pltpu.VMEM((8, 256, 128), LOW),
            pltpu.VMEM((128, width), LOW),
            pltpu.VMEM((8, 128, 768), LOW),
            pltpu.VMEM((128, width), LOW),
            pltpu.VMEM((2, 64, 2048), LOW),
            pltpu.VMEM((8, width), WIDE),
            pltpu.VMEM((8, 128, width), LOW),
            pltpu.VMEM((8, 128, width), LOW),
            pltpu.VMEM((8, 128, width), LOW),
            pltpu.VMEM((8, 128, 768), LOW),
            pltpu.VMEM((8, 384, 128), LOW),
            pltpu.VMEM((8, 256, 128), LOW),
            pltpu.VMEM((8, 8, width), WIDE),
            pltpu.VMEM((4, 8, width), WIDE),
            pltpu.VMEM((3, 96, width), LOW),
            pltpu.VMEM((2, 96, width), LOW),
            pltpu.VMEM((256, width), LOW),
            pltpu.VMEM((3, 64, width), LOW),
            pltpu.VMEM((2, 64, width), LOW),
            pltpu.VMEM((3, 8, 32, 768), LOW),
            pltpu.VMEM((2, 2, 128, 768), LOW),
            pltpu.VMEM((16, 64, 256), LOW),
            pltpu.VMEM((8, 2 * TILE, HD), LOW),
            pltpu.VMEM((HD, length), LOW),
            pltpu.VMEM((8, 8, length), WIDE),
            pltpu.VMEM((16, 64, 512), LOW),
            pltpu.VMEM((8, 2, 64, 512), LOW),
            pltpu.VMEM((512, 512), LOW),
            pltpu.VMEM((16, 32, 512), LOW),
            pltpu.VMEM((8, 384), WIDE),
            pltpu.VMEM((4, 8, 384), WIDE),
            pltpu.SMEM((16,), jnp.int32),
            dma((17,)),
            dma((POST_SENDS,)),
            dma((6, 8)),
            dma((12,)),
            dma((4,)),
            dma((4,)),
            dma((3, 8)),
            dma((2, 2)),
            dma((16,)),
            dma((8,)),
            dma((16,)),
            dma((1,)),
            dma((16,)),
            dma((4,)),
        ],
        compiler_params=pltpu.CompilerParams(
            collective_id=1, has_side_effects=True, vmem_limit_bytes=63 * 2**20
        ),
        name="row_backward",
    )(*operands)


def finish_kernel(*refs):
    count = 9
    sources, vec_ref, gain_ref = refs[:count], refs[count], refs[count + 1]
    targets, small = refs[count + 2 : 2 * count + 2], refs[2 * count + 2 :]
    for source, target in zip(sources, targets):
        target[...] = source[...]
    seq = lax.axis_index("seq")
    me = lax.axis_index("dp") * 16 + seq
    part = seq % 4
    gains, vec = gain_ref[...], vec_ref[...]
    q_out, k_out, attn_out, mlp_out = small
    q_all = pltpu.roll(gains[:, :256], (256 - part * 64) % 256, axis=1)
    k_all = pltpu.roll(gains[:, 256:], (128 - part * 32) % 128, axis=1)
    vec = pltpu.roll(vec, (1024 - me * 32) % 1024, axis=1)
    q_out[...] = q_all[0:1, :64]
    k_out[...] = k_all[0:1, :32]
    attn_out[...] = vec[0:1, :32]
    mlp_out[...] = vec[1:2, :32]


def finish(arrays, vec, gains):
    vmem = pl.BlockSpec(memory_space=pltpu.VMEM)
    shape = jax.ShapeDtypeStruct
    count = len(arrays)
    return pl.pallas_call(
        finish_kernel,
        out_shape=tuple(shape(a.shape, a.dtype) for a in arrays)
        + (shape((1, 64), WIDE), shape((1, 32), WIDE), shape((1, 32), WIDE), shape((1, 32), WIDE)),
        in_specs=[vmem] * (count + 2),
        out_specs=(vmem,) * (count + 4),
        name="finish",
    )(*arrays, vec, gains)


def rms_forward(inputs, gain_vec):
    factor = lax.rsqrt(jnp.mean(inputs * inputs, axis=-1, keepdims=True) + EPSILON)
    normal = inputs * factor
    return (normal * gain_vec, normal, factor)


def rms_backward(grad_in, gain_vec, normal, factor):
    weighted = grad_in * gain_vec
    gain_grad = jnp.sum(grad_in * normal, axis=0)
    inner_mean = jnp.mean(weighted * normal, axis=-1, keepdims=True)
    return (factor * (weighted - normal * inner_mean), gain_grad)


def rope_tables(rot_places, head_size):
    frequency = jnp.power(ROPE_BASE, -jnp.arange(0, head_size, 2).astype(jnp.float32) / head_size)
    angles = rot_places.astype(jnp.float32)[:, None] * frequency[None, :]
    return (jnp.cos(angles), jnp.sin(angles))


def rotate(inputs, cos_table, sine_table, head_count, direction):
    row_count = inputs.shape[0]
    halves = inputs.reshape(row_count, head_count, 2, -1)
    first_half = halves[:, :, 0]
    second = halves[:, :, 1]
    cos_part = cos_table[:, None, :]
    sine_part = sine_table[:, None, :] * direction
    turned = jnp.stack(
        [first_half * cos_part - second * sine_part, second * cos_part + first_half * sine_part],
        axis=2,
    )
    return turned.reshape(row_count, -1)


def product(left, right):
    return jnp.dot(left, right, preferred_element_type=jnp.float32)


def weight_grad(left, right):
    return lax.dot_general(
        left, right, (((0,), (0,)), ((), ())), preferred_element_type=jnp.float32
    )


def back_product(left, right):
    return lax.dot_general(
        left, right, (((1,), (1,)), ((), ())), preferred_element_type=jnp.float32
    )


def heads_first(rows, group_count, head_size):
    shaped = rows.reshape(rows.shape[0], group_count, -1, head_size)
    return jnp.moveaxis(shaped, 1, 0)


def kv_first(rows, group_count, head_size):
    return jnp.moveaxis(rows.reshape(rows.shape[0], group_count, head_size), 1, 0)


def score_block(q_group, k_group, mask_rows, score_scale):
    raw_scores = (
        jnp.einsum("trd,ud->rtu", q_group, k_group, preferred_element_type=jnp.float32)
        * score_scale
    )
    return jnp.where(mask_rows[None], raw_scores, MASK_FILL)


def attend(pieces, score_scale, group_count, head_size):
    q_rows, key_rows, value_rows, mask_rows = pieces

    def attend_one_group(parts):
        q_group, k_group, v_group = parts
        masked = score_block(q_group, k_group, mask_rows, score_scale)
        row_max = jnp.max(masked, axis=-1)
        exp_terms = jnp.exp(masked - row_max[..., None])
        row_sum = jnp.sum(exp_terms, axis=-1)
        attn_prob = (exp_terms / row_sum[..., None]).astype(jnp.bfloat16)
        attended = jnp.einsum("rtu,ud->trd", attn_prob, v_group, preferred_element_type=jnp.float32)
        return (attended, row_max, row_sum)

    attended, row_max, row_sum = lax.map(
        attend_one_group,
        (
            heads_first(q_rows, group_count, head_size),
            kv_first(key_rows, group_count, head_size),
            kv_first(value_rows, group_count, head_size),
        ),
    )
    attended = jnp.moveaxis(attended, 0, 1)
    return (attended.reshape(q_rows.shape[0], -1), row_max, row_sum)


def score_grads(
    q_group, grad_group, k_group, v_group, mask_rows, row_max, row_sum, row_dot, score_scale
):
    masked = score_block(q_group, k_group, mask_rows, score_scale)
    attn_prob = jnp.exp(masked - row_max[..., None]) / row_sum[..., None]
    prob_grad = jnp.einsum("trd,ud->rtu", grad_group, v_group, preferred_element_type=jnp.float32)
    row_dot = jnp.sum(attn_prob * prob_grad, axis=-1)
    score_grad = (attn_prob * (prob_grad - row_dot[..., None])).astype(jnp.bfloat16)
    return (attn_prob.astype(jnp.bfloat16), score_grad, row_dot)


def on_device(
    tokens,
    cotangent,
    w_query,
    w_key,
    w_value,
    w_out,
    q_gain,
    k_gain,
    attn_gain,
    w_gate,
    w_up,
    w_down,
    mlp_gain,
    doc_lengths,
    block_order,
):
    micro_count = tokens.shape[0]
    block_len = tokens.shape[2]
    model_width = tokens.shape[3]
    seq_length = lax.axis_size("seq") * block_len
    head_count = w_query.shape[1] // HD
    group_count = w_key.shape[1] // HD
    score_scale = HD ** (-0.5)
    flat_tokens = tokens.reshape(micro_count * block_len, model_width)
    out_grad = cotangent.reshape(micro_count * block_len, model_width).astype(jnp.float32)
    first_lengths = doc_lengths[:, 0, 0]
    offsets = jnp.arange(block_len, dtype=jnp.int32)
    own_places = block_order[lax.axis_index("seq")] * block_len + offsets
    key_places = (block_order[:, None] * block_len + offsets[None, :]).reshape(seq_length)
    own_segments = (own_places[None, :] >= first_lengths[:, None]).astype(jnp.int32)
    all_segments = (key_places[None, :] >= first_lengths[:, None]).astype(jnp.int32)
    rot_places = (own_places[None, :] - own_segments * first_lengths[:, None]).reshape(-1)
    allowed = (own_segments[:, :, None] == all_segments[:, None, :]) & (
        key_places[None, None, :] <= own_places[None, :, None]
    )
    cos_table, sine_table = rope_tables(rot_places, HD)
    q_pre = product(flat_tokens, w_query)
    k_pre = product(flat_tokens, w_key)
    v_pre = product(flat_tokens, w_value)
    q_norm, q_hat, q_factor = rms_forward(q_pre, q_gain)
    k_norm, k_hat, k_factor = rms_forward(k_pre, k_gain)
    q_low = rotate(q_norm, cos_table, sine_table, head_count, 1.0).astype(jnp.bfloat16)
    k_low = rotate(k_norm, cos_table, sine_table, group_count, 1.0).astype(jnp.bfloat16)
    v_low = v_pre.astype(jnp.bfloat16)
    q_blocks = q_low.reshape(micro_count, block_len, -1)
    k_blocks = k_low.reshape(micro_count, block_len, -1)
    v_blocks = v_low.reshape(micro_count, block_len, -1)
    key_all, value_all = (
        lax.all_gather(k_blocks, "seq", axis=1, tiled=True),
        lax.all_gather(v_blocks, "seq", axis=1, tiled=True),
    )

    def forward_block(pieces):
        return attend(pieces, score_scale, group_count, HD)

    attended, row_max, row_sum = lax.map(forward_block, (q_blocks, key_all, value_all, allowed))
    att_low = attended.reshape(micro_count * block_len, -1).astype(jnp.bfloat16)
    attn_proj = product(att_low, w_out)
    attn_normed, attn_hat, attn_factor = rms_forward(attn_proj, attn_gain)
    hidden = flat_tokens.astype(jnp.float32) + attn_normed
    hidden_low = hidden.astype(jnp.bfloat16)
    gate_pre = product(hidden_low, w_gate)
    up_pre = product(hidden_low, w_up)
    mixed_low = (jax.nn.silu(gate_pre) * up_pre).astype(jnp.bfloat16)
    down_pre = product(mixed_low, w_down)
    down_normed, down_hat, down_factor = rms_forward(down_pre, mlp_gain)
    layer_out = (hidden + down_normed).astype(jnp.bfloat16).reshape(tokens.shape)
    down_grad, grad_mlp_gain = rms_backward(out_grad, mlp_gain, down_hat, down_factor)
    down_grad = down_grad.astype(jnp.bfloat16)
    grad_w_down = weight_grad(mixed_low, down_grad)
    mixed_grad = back_product(down_grad, w_down)
    sigmoid_gate = jax.nn.sigmoid(gate_pre)
    gate_grad = (
        mixed_grad * up_pre * sigmoid_gate * (1.0 + gate_pre * (1.0 - sigmoid_gate))
    ).astype(jnp.bfloat16)
    up_grad = (mixed_grad * gate_pre * sigmoid_gate).astype(jnp.bfloat16)
    grad_w_gate = weight_grad(hidden_low, gate_grad)
    grad_w_up = weight_grad(hidden_low, up_grad)
    hidden_grad = out_grad + back_product(gate_grad, w_gate) + back_product(up_grad, w_up)
    proj_grad, grad_attn_gain = rms_backward(hidden_grad, attn_gain, attn_hat, attn_factor)
    proj_grad = proj_grad.astype(jnp.bfloat16)
    grad_w_out = weight_grad(att_low, proj_grad)
    att_grad = back_product(proj_grad, w_out).astype(jnp.bfloat16)
    grad_blocks = att_grad.reshape(micro_count, block_len, -1)
    key_back, value_back = (key_all, value_all)

    def query_pass(pieces):
        q_rows, grad_rows, key_rows, value_rows, mask_rows, max_rows, sum_rows = pieces

        def query_one_group(parts):
            q_group, grad_group, k_group, v_group, max_group, sum_group = parts
            prob_low, score_grad, unused = score_grads(
                q_group,
                grad_group,
                k_group,
                v_group,
                mask_rows,
                max_group,
                sum_group,
                None,
                score_scale,
            )
            q_grad = (
                jnp.einsum("rtu,ud->trd", score_grad, k_group, preferred_element_type=jnp.float32)
                * score_scale
            )
            key_terms = (
                jnp.einsum("rtu,trd->ud", score_grad, q_group, preferred_element_type=jnp.float32)
                * score_scale
            )
            value_terms = jnp.einsum(
                "rtu,trd->ud", prob_low, grad_group, preferred_element_type=jnp.float32
            )
            return (q_grad, key_terms, value_terms)

        q_grad, key_terms, value_terms = lax.map(
            query_one_group,
            (
                heads_first(q_rows, group_count, HD),
                heads_first(grad_rows, group_count, HD),
                kv_first(key_rows, group_count, HD),
                kv_first(value_rows, group_count, HD),
                max_rows,
                sum_rows,
            ),
        )
        q_grad = jnp.moveaxis(q_grad, 0, 1).reshape(block_len, -1)
        key_terms = jnp.moveaxis(key_terms, 0, 1).reshape(seq_length, -1)
        value_terms = jnp.moveaxis(value_terms, 0, 1).reshape(seq_length, -1)
        key_own, value_own = (
            lax.psum_scatter(key_terms, "seq", scatter_dimension=0, tiled=True),
            lax.psum_scatter(value_terms, "seq", scatter_dimension=0, tiled=True),
        )
        return (q_grad, key_own, value_own)

    q_rot_grad, k_rot_grad, value_grad = lax.map(
        query_pass, (q_blocks, grad_blocks, key_back, value_back, allowed, row_max, row_sum)
    )
    q_rot_grad = q_rot_grad.reshape(micro_count * block_len, -1)
    k_rot_grad = k_rot_grad.reshape(micro_count * block_len, -1)
    v_grad = value_grad.reshape(micro_count * block_len, -1).astype(jnp.bfloat16)
    q_norm_grad = rotate(q_rot_grad, cos_table, sine_table, head_count, -1.0)
    k_norm_grad = rotate(k_rot_grad, cos_table, sine_table, group_count, -1.0)
    q_grad, grad_q_gain = rms_backward(q_norm_grad, q_gain, q_hat, q_factor)
    k_grad, grad_k_gain = rms_backward(k_norm_grad, k_gain, k_hat, k_factor)
    q_grad = q_grad.astype(jnp.bfloat16)
    k_grad = k_grad.astype(jnp.bfloat16)
    grad_w_query = weight_grad(flat_tokens, q_grad)
    grad_w_key = weight_grad(flat_tokens, k_grad)
    grad_w_value = weight_grad(flat_tokens, v_grad)
    input_grad = (
        hidden_grad
        + back_product(q_grad, w_query)
        + back_product(k_grad, w_key)
        + back_product(v_grad, w_value)
    )
    input_grad = input_grad.reshape(tokens.shape)
    summed = (
        lax.psum_scatter(grad_w_query, ("dp", "seq"), scatter_dimension=0, tiled=True),
        lax.psum_scatter(grad_w_key, ("dp", "seq"), scatter_dimension=0, tiled=True),
        lax.psum_scatter(grad_w_value, ("dp", "seq"), scatter_dimension=0, tiled=True),
        lax.psum_scatter(grad_w_out, ("dp", "seq"), scatter_dimension=0, tiled=True),
        lax.psum_scatter(grad_q_gain, ("dp", "seq"), scatter_dimension=0, tiled=True),
        lax.psum_scatter(grad_k_gain, ("dp", "seq"), scatter_dimension=0, tiled=True),
        lax.psum_scatter(grad_attn_gain, ("dp", "seq"), scatter_dimension=0, tiled=True),
        lax.psum_scatter(grad_w_gate, ("dp", "seq"), scatter_dimension=0, tiled=True),
        lax.psum_scatter(grad_w_up, ("dp", "seq"), scatter_dimension=0, tiled=True),
        lax.psum_scatter(grad_w_down, ("dp", "seq"), scatter_dimension=0, tiled=True),
        lax.psum_scatter(grad_mlp_gain, ("dp", "seq"), scatter_dimension=0, tiled=True),
    )
    return (
        layer_out,
        input_grad,
        summed[0],
        summed[1],
        summed[2],
        summed[3],
        summed[4],
        summed[5],
        summed[6],
        summed[7],
        summed[8],
        summed[9],
        summed[10],
    )


def split_by_heads(
    tokens, cotangent, w_query, w_key, w_value, w_out, q_gain, k_gain, attn_gain,
    w_gate, w_up, w_down, mlp_gain, doc_lengths, block_order,
):
    cos, sine = rope_constants(1024)
    q_gain_rows, k_gain_rows = q_gain.reshape(16, HD), k_gain.reshape(8, HD)
    own_tokens = tokens[:, 0]
    att_tok, tok_nat, q_pair, kv_nat, hat, factors, lse = row_forward(
        own_tokens, w_query, w_key, w_value, q_gain_rows, k_gain_rows, cos, sine, block_order, doc_lengths
    )
    layer_out, in_grad, g_query, g_key, g_value, g_out, vec, gains, g_gate, g_up, g_down = row_backward(
        att_tok, own_tokens, cotangent[:, 0], attn_gain[None], mlp_gain[None], q_gain_rows, k_gain_rows, factors, lse,
        tok_nat, q_pair, kv_nat, hat, cos, sine,
        w_out, w_gate, w_up, w_down, w_query, w_key, w_value, block_order, doc_lengths,
    )
    (
        layer_out, in_grad, g_query, g_key, g_value, g_out, g_gate, g_up, g_down,
        g_q_gain, g_k_gain, g_attn_gain, g_mlp_gain,
    ) = finish((layer_out, in_grad, g_query, g_key, g_value, g_out, g_gate, g_up, g_down), vec, gains)
    return (
        layer_out.reshape(tokens.shape),
        in_grad.reshape(tokens.shape),
        g_query,
        g_key,
        g_value,
        g_out,
        g_q_gain[0],
        g_k_gain[0],
        g_attn_gain[0],
        g_gate,
        g_up,
        g_down,
        g_mlp_gain[0],
    )


SPECS_IN = (
    P(None, "dp", "seq", None), P(None, "dp", "seq", None),
    P(), P(), P(), P(), P(), P(), P(), P(), P(), P(), P(),
    P(None, "dp", None), P(),
)
SPECS_OUT = (
    P(None, "dp", "seq", None), P(None, "dp", "seq", None),
    P(("dp", "seq"), None), P(("dp", "seq"), None), P(("dp", "seq"), None), P(("dp", "seq"), None),
    P(("dp", "seq")), P(("dp", "seq")), P(("dp", "seq")),
    P(("dp", "seq"), None), P(("dp", "seq"), None), P(("dp", "seq"), None),
    P(("dp", "seq")),
)


def solution(mesh):
    body = split_by_heads if mesh.shape["seq"] == 16 and mesh.shape["dp"] == 2 else on_device
    return jax.shard_map(body, mesh=mesh, in_specs=SPECS_IN, out_specs=SPECS_OUT, check_vma=False)
```

```python
import functools

import jax
import jax.numpy as jnp
import numpy as np
from jax import lax
from jax.experimental import pallas as pl
from jax.experimental.pallas import tpu as pltpu
from jax.sharding import PartitionSpec as P

HD = 128
EPSILON = 1e-06
ROPE_BASE = 500000.0
MASK_FILL = -1e30
MESH = pl.DeviceIdType.MESH
LOW = jnp.bfloat16
WIDE = jnp.float32
TILE = 128
CHUNK = 256


def remote(source, target, send_sem, recv_sem, place):
    return pltpu.make_async_remote_copy(
        src_ref=source,
        dst_ref=target,
        send_sem=send_sem,
        recv_sem=recv_sem,
        device_id=place,
        device_id_type=MESH,
    )


def dot(left, right):
    return jnp.dot(left, right, preferred_element_type=WIDE)


def dot_nt(left, right):
    return lax.dot_general(left, right, (((1,), (1,)), ((), ())), preferred_element_type=WIDE)


def dot_tn(left, right):
    return lax.dot_general(left, right, (((0,), (0,)), ((), ())), preferred_element_type=WIDE)


class Spot:
    def __init__(self):
        self.dp = lax.axis_index("dp")
        self.seq = lax.axis_index("seq")
        self.core = self.seq % 2
        self.chip = self.seq // 2
        self.x = self.chip % 2
        self.z = self.chip // 2
        self.sibling = self.seq + 1 - 2 * self.core
        self.flip_x = self.seq + 2 - 4 * self.x
        self.far_z = (
            self.z + 1 - 2 * (self.z % 2),
            self.z + 2 - 4 * (self.z // 2),
            3 - self.z,
        )


def greet_row(spot, devices):
    barrier = pltpu.get_barrier_semaphore()
    for step in range(1, devices):
        pl.semaphore_signal(
            barrier,
            inc=1,
            device_id=(spot.dp, (spot.seq + step) % devices),
            device_id_type=MESH,
        )
    pl.semaphore_wait(barrier, devices - 1)


class RowGather:
    def __init__(self, spot, own, held, local_sem, send_sems, recv_sems):
        self.spot, self.own, self.held = spot, own, held
        self.send_sems, self.recv_sems = send_sems, recv_sems
        self.sent = []
        self.local = pltpu.make_async_copy(own.at[spot.core], held.at[spot.seq], local_sem)

    def send(self, source, slots, recv_sem, target):
        copy = remote(
            source, slots, self.send_sems.at[len(self.sent)], recv_sem, (self.spot.dp, target)
        )
        copy.start()
        self.sent.append(copy)

    def start(self):
        spot = self.spot
        own_slot = self.held.at[spot.seq]
        own_sem = self.recv_sems.at[spot.seq]
        for far in spot.far_z:
            for micro in range(2):
                self.send(self.own.at[micro], own_slot, own_sem, far * 4 + spot.x * 2 + micro)
        for micro in range(2):
            self.send(
                self.own.at[micro], own_slot, own_sem, spot.z * 4 + (1 - spot.x) * 2 + micro
            )
        self.send(self.own.at[1 - spot.core], own_slot, own_sem, spot.sibling)
        self.local.start()

    def arrived(self, slots, recv_sem):
        remote(slots, slots, self.send_sems.at[0], recv_sem, (self.spot.dp, self.spot.sibling)).wait_recv()

    def forward(self):
        spot = self.spot
        for far in spot.far_z:
            first = far * 4 + spot.x * 2
            for core in range(2):
                self.arrived(self.held.at[first + core], self.recv_sems.at[first + core])
            pair = self.held.at[pl.ds(first, 2)]
            self.send(pair, pair, self.recv_sems.at[16 + far], spot.flip_x)

    def finish(self):
        spot = self.spot
        self.arrived(self.held.at[spot.sibling], self.recv_sems.at[spot.sibling])
        for core in range(2):
            slot = spot.z * 4 + (1 - spot.x) * 2 + core
            self.arrived(self.held.at[slot], self.recv_sems.at[slot])
        for far in spot.far_z:
            first = far * 4 + (1 - spot.x) * 2
            self.arrived(self.held.at[pl.ds(first, 2)], self.recv_sems.at[16 + far])
        self.local.wait()
        for copy in self.sent:
            copy.wait_send()


GATHER_SENDS = 12
GATHER_RECVS = 20


def rope_rows(table, block, first_length):
    start = block * 64
    inside = table[pl.ds(64 + start, 64), :]
    shifted = table[pl.ds(64 + jnp.maximum(start - first_length, -64), 64), :]
    places = start + lax.broadcasted_iota(jnp.int32, (64, HD), 0)
    return jnp.where(places < first_length, inside, shifted)


def swap_halves(head):
    return pltpu.roll(head, HD // 2, axis=1)


def columns_of(rows):
    return jnp.concatenate([rows] * 16, axis=0).T[:, :8]


def rows_of(first, second):
    lane = lax.broadcasted_iota(jnp.int32, (first.shape[0], HD), 1)
    return jnp.where(lane == 0, first, second).T[:8]


def allowed_places(tile, count, first_length):
    keys = lax.broadcasted_iota(jnp.int32, (count, 2 * TILE), 0)
    lanes = lax.broadcasted_iota(jnp.int32, (1, 2 * TILE), 1)
    queries = tile * TILE + lanes % TILE
    earliest = jnp.where(queries < first_length, 0, first_length)
    return (keys >= earliest) & (keys <= queries)


def invert(order_ref, inverse_ref):
    def fill(block, carry):
        place = jnp.int32(0)
        for slot in range(16):
            place = jnp.maximum(place, jnp.where(order_ref[slot] == block, slot, 0))
        inverse_ref[block] = place
        return carry

    lax.fori_loop(0, 16, fill, 0)


def forward_kernel(
    tok_ref, wq_hbm, wk_hbm, wv_hbm, qgain_ref, kgain_ref, cos_ref, sine_ref,
    order_ref, docs_ref,
    att_tok, tok_nat, q_pair, kv_nat, hat, factors, lse,
    att_nat, tok_all, wq_all, wk_all, wv_own, stat_all, att_send, att_recv, kv_turned,
    inverse_ref, local_sems, send_sems, recv_sems, stat_send, stat_recv, att_ssem, att_rsem,
):
    spot = Spot()
    devices = 16
    chips = 8
    chip = spot.chip
    loads = [
        pltpu.make_async_copy(wq_hbm, wq_all, local_sems.at[1]),
        pltpu.make_async_copy(wk_hbm, wk_all, local_sems.at[2]),
        pltpu.make_async_copy(
            wv_hbm.at[:, pl.ds(pl.multiple_of(chip * 128, 128), 128)], wv_own, local_sems.at[3]
        ),
    ]
    for load in loads:
        load.start()
    greet_row(spot, devices)
    gather = RowGather(spot, tok_ref, tok_all, local_sems.at[0], send_sems, recv_sems)
    gather.start()
    invert(order_ref, inverse_ref)

    for load in loads:
        load.wait()
    own = tok_ref[...].reshape(128, tok_ref.shape[-1])
    sums = []
    for weight in (wq_all, wk_all):
        parts = [dot(own, weight[:, first : first + 512]) for first in range(0, weight.shape[1], 512)]
        sums.append(sum(jnp.sum(part * part, axis=-1, keepdims=True) for part in parts) / weight.shape[1])
    stat_all[pl.ds(spot.seq, 1)] = lax.rsqrt(rows_of(sums[0], sums[1]) + EPSILON)[None]
    stat_copies = []
    for step in range(1, devices):
        other = (spot.seq + step) % devices
        copy = remote(
            stat_all.at[spot.seq], stat_all.at[spot.seq], stat_send.at[step], stat_recv.at[spot.seq], (spot.dp, other)
        )
        copy.start()
        stat_copies.append(copy)
    gather.forward()
    for step in range(1, devices):
        other = (spot.seq + step) % devices
        remote(
            stat_all.at[other], stat_all.at[other], stat_send.at[0], stat_recv.at[other], (spot.dp, spot.sibling)
        ).wait_recv()
    gather.finish()

    first_length = docs_ref[spot.core, 0, 0]
    for part in range(4):
        rows = pl.ds(part * CHUNK, CHUNK)
        chunk = jnp.concatenate([tok_all[inverse_ref[part * 4 + piece]] for piece in range(4)], axis=0)
        tok_nat[rows, :] = chunk
        hat[rows, :256] = dot(chunk, wq_all[:, pl.ds(pl.multiple_of(chip * 256, 256), 256)])
        hat[rows, 256:] = dot(chunk, wk_all[:, pl.ds(pl.multiple_of(chip * 128, 128), 128)])
        kv_nat[rows, 128:] = dot(chunk, wv_own[...]).astype(LOW)
    for block in range(16):
        both = stat_all[inverse_ref[block]]
        both = jnp.where(spot.core == 0, both, pltpu.roll(both, 64, axis=1))
        factors[:, block * 64 : (block + 1) * 64] = both[:, :64]
    qgain = qgain_ref[pl.ds(chip * 2, 2), :]
    kgain = kgain_ref[pl.ds(chip, 1), :]
    for part in range(8):
        rows = pl.ds(part * TILE, TILE)
        scale = columns_of(factors[:, rows])
        cos = jnp.concatenate([rope_rows(cos_ref, part * 2 + piece, first_length) for piece in range(2)], axis=0)
        sine = jnp.concatenate([rope_rows(sine_ref, part * 2 + piece, first_length) for piece in range(2)], axis=0)
        for head in range(3):
            lanes = pl.ds(head * HD, HD)
            column = scale[:, 0:1] if head < 2 else scale[:, 1:2]
            gain = qgain[head : head + 1] if head < 2 else kgain
            normal = hat[rows, lanes] * column
            hat[rows, lanes] = normal
            normed = normal * gain
            turned = (normed * cos + swap_halves(normed) * sine).astype(LOW)
            if head < 2:
                q_pair[part, pl.ds(head * HD, HD), :] = turned
            else:
                kv_nat[rows, :HD] = turned
    kv_turned[...] = kv_nat[:, HD:].T
    for tile in range(8):
        count = (tile + 1) * TILE
        scores = dot_nt(kv_nat[:count, :HD], q_pair[tile]) * HD ** (-0.5)
        masked = jnp.where(allowed_places(tile, count, first_length), scores, MASK_FILL)
        top = jnp.max(masked, axis=0, keepdims=True)
        terms = jnp.exp(masked - top)
        weight = jnp.sum(terms, axis=0, keepdims=True)
        lse[pl.ds(tile, 1), :] = top + jnp.log(weight)
        turned = dot(kv_turned[:, :count], terms.astype(LOW)) / weight
        attended = turned.T.astype(LOW)
        att_nat[pl.ds(tile * 2, 2), :, :HD] = attended[:TILE].reshape(2, 64, HD)
        att_nat[pl.ds(tile * 2, 2), :, HD:] = attended[TILE:].reshape(2, 64, HD)
    own_part = (spot.core, slice(None), pl.ds(pl.multiple_of(chip * 256, 256), 256))
    att_recv[pl.ds(chip, 1), pl.ds(spot.core, 1)] = att_nat[order_ref[spot.seq]][None, None]
    sent = []
    for step in range(1, devices):
        other = (spot.seq + step) % devices
        att_send[step] = att_nat[order_ref[other]]
        copy = remote(
            att_send.at[step], att_recv.at[chip, spot.core], att_ssem.at[step],
            att_rsem.at[spot.seq], (spot.dp, other),
        )
        copy.start()
        sent.append(copy)
    for step in range(1, devices):
        other = (spot.seq + step) % devices
        slot = att_recv.at[other // 2, other % 2]
        remote(slot, slot, att_ssem.at[0], att_rsem.at[other], (spot.dp, spot.sibling)).wait_recv()
    for piece in range(chips):
        for micro in range(2):
            att_tok[micro, :, piece * 256 : (piece + 1) * 256] = att_recv[piece, micro]
    for copy in sent + stat_copies:
        copy.wait_send()


def rope_constants(length):
    frequency = np.power(np.float32(ROPE_BASE), -np.arange(0, HD, 2).astype(np.float32) / np.float32(HD)).astype(np.float32)
    angles = (np.arange(length, dtype=np.float32)[:, None] * frequency[None, :]).astype(np.float32).astype(np.float64)
    cos, sine = np.cos(angles), np.sin(angles)
    front = np.zeros((64, HD))
    cos = np.concatenate([front, np.concatenate([cos, cos], axis=1)], axis=0)
    sine = np.concatenate([front, np.concatenate([-sine, sine], axis=1)], axis=0)
    return jnp.asarray(cos, WIDE), jnp.asarray(sine, WIDE)


def row_forward(tokens, w_query, w_key, w_value, q_gain, k_gain, cos, sine, order, docs):
    length = 1024
    width = tokens.shape[-1]
    any_spec = pl.BlockSpec(memory_space=pl.ANY)
    vmem = pl.BlockSpec(memory_space=pltpu.VMEM)
    smem = pl.BlockSpec(memory_space=pltpu.SMEM)
    shape = jax.ShapeDtypeStruct
    return pl.pallas_call(
        forward_kernel,
        out_shape=(
            shape((2, 64, 2048), LOW),
            shape((length, width), LOW),
            shape((8, 2 * TILE, HD), LOW),
            shape((length, 2 * HD), LOW),
            shape((length, 3 * HD), WIDE),
            shape((8, length), WIDE),
            shape((8, 2 * TILE), WIDE),
        ),
        in_specs=[vmem, any_spec, any_spec, any_spec, vmem, vmem, vmem, vmem, smem, smem],
        out_specs=(vmem,) * 7,
        scratch_shapes=[
            pltpu.VMEM((16, 64, 2 * HD), LOW),
            pltpu.VMEM((16, 64, width), LOW),
            pltpu.VMEM((width, 2048), LOW),
            pltpu.VMEM((width, 1024), LOW),
            pltpu.VMEM((width, 128), LOW),
            pltpu.VMEM((16, 8, 128), WIDE),
            pltpu.VMEM((16, 64, 2 * HD), LOW),
            pltpu.VMEM((8, 2, 64, 2 * HD), LOW),
            pltpu.VMEM((HD, length), LOW),
            pltpu.SMEM((16,), jnp.int32),
            pltpu.SemaphoreType.DMA((4,)),
            pltpu.SemaphoreType.DMA((GATHER_SENDS,)),
            pltpu.SemaphoreType.DMA((GATHER_RECVS,)),
            pltpu.SemaphoreType.DMA((16,)),
            pltpu.SemaphoreType.DMA((16,)),
            pltpu.SemaphoreType.DMA((16,)),
            pltpu.SemaphoreType.DMA((16,)),
        ],
        compiler_params=pltpu.CompilerParams(
            collective_id=0, has_side_effects=True, vmem_limit_bytes=56 * 2**20
        ),
        name="row_forward",
    )(tokens, w_query, w_key, w_value, q_gain, k_gain, cos, sine, order, docs)


class Post:
    def __init__(self, sems):
        self.sems, self.started, self.used = sems, [], 0

    def send(self, source, target, recv_sem, place, when=None):
        copy = remote(source, target, self.sems.at[self.used], recv_sem, place)
        self.used += 1
        self.started.append((copy, when))
        if when is None:
            copy.start()
        else:
            pl.when(when)(copy.start)

    def finish(self):
        for copy, when in self.started:
            if when is None:
                copy.wait_send()
            else:
                pl.when(when)(copy.wait_send)


def arrived(spot, slot, recv_sem, spare_sem):
    remote(slot, slot, spare_sem, recv_sem, (spot.dp, spot.sibling)).wait_recv()


def aligned(start, size):
    return pl.ds(pl.multiple_of(start, size), size)


class AlongZ:
    def __init__(self, spot, post, spare):
        self.spot, self.post, self.spare = spot, post, spare
        half = spot.z // 2
        self.partner = spot.far_z[0]
        self.far_inner = 2 - half
        self.far_outer = 3 - 3 * half
        self.inner = ((spot.z + 1) // 2) % 2 == 1
        self.outer = ((spot.z + 1) // 2) % 2 == 0

    def place(self, z):
        return (self.spot.dp, z * 4 + self.spot.x * 2 + self.spot.core)

    def send(self, part, size, landing, transit, sems):
        spot, post = self.spot, self.post
        landing[2] = part[aligned(spot.z * size, size), :]
        for slot, far in enumerate((self.far_inner, self.far_outer)):
            post.send(
                part.at[aligned(far * size, size)], transit.at[slot], sems.at[2 + slot], self.place(self.partner),
                self.outer,
            )
        post.send(part.at[aligned(self.partner * size, size)], landing.at[0], sems.at[0], self.place(self.partner))

    def combine(self, part, size, landing, transit, sems):
        for slot, far in enumerate((self.far_inner, self.far_outer)):

            @pl.when(self.inner)
            def _():
                arrived(self.spot, transit.at[slot], sems.at[2 + slot], self.spare)
                added = transit[slot].astype(WIDE) + part[aligned(far * size, size), :].astype(WIDE)
                transit[slot] = added.astype(LOW)

            self.post.send(transit.at[slot], landing.at[1], sems.at[1], self.place(far), self.inner)

    def total(self, landing, sems):
        arrived(self.spot, landing.at[0], sems.at[0], self.spare)
        arrived(self.spot, landing.at[1], sems.at[1], self.spare)
        return landing[0].astype(WIDE) + landing[1].astype(WIDE) + landing[2].astype(WIDE)


def row_scale(values):
    return lax.rsqrt(jnp.mean(values * values, axis=-1, keepdims=True) + EPSILON)


def norm_back(grad, gain, normal, factor):
    weighted = grad * gain
    return factor * (weighted - normal * jnp.mean(weighted * normal, axis=-1, keepdims=True))


def backward_kernel(
    att_ref, tok_ref, cot_ref, again_ref, mgain_ref, qgain_ref, kgain_ref, factors, lse,
    tok_hbm, q_hbm, kv_hbm, hat_hbm, cos_hbm, sine_hbm,
    wout_hbm, wg_hbm, wu_hbm, wd_hbm, wq_hbm, wk_hbm, wv_hbm, order_ref, docs_ref,
    layer_out, in_grad, g_query, g_key, g_value, g_out, vec_out, gain_out, g_gate, g_up, g_down,
    wout, wgate, wup, wdown, q_pair, kv_nat, hat, cos_ref, sine_ref,
    att_hat, hidden, hid_own, gate_pre, up_pre, mixed, mix_turned, att_turned, down_own, gu_own, proj_own, ag_own, vec_own,
    hid_all, down_all, proj_all, gu_all, mix_all, att_all, vec_all, vec_far,
    down_land, down_transit, wout_part, wout_land, gu_land, gu_transit,
    ag_recv, ag_pair, k_turned, stat_all, grad_nat, grad_recv, part_sib, wqkv_recv, gain_own, gain_recv,
    inverse_ref, local_sems, post_sems, hid_sems, dpl_sems, proj_sems, attp_sems, mix_sems, gup_sems, vec_sems, down_sems, wout_sems, gu_sems, gut_sems, ag_sems, stat_sems, grad_sems, sib_sem, wqkv_sems, gain_sems,
):
    spot = Spot()
    devices, chips = 16, 8
    dp, seq, core, chip, z = spot.dp, spot.seq, spot.core, spot.chip, spot.z
    me = dp * devices + seq
    member = dp * 4 + spot.x * 2 + core
    spare = post_sems.at[0]
    post = Post(post_sems)
    along = AlongZ(spot, post, spare)

    def load(source, target, index):
        copy = pltpu.make_async_copy(source, target, local_sems.at[index])
        copy.start()
        return copy

    barrier = pltpu.get_barrier_semaphore()
    for step in range(1, 2 * devices):
        other = (me + step) % (2 * devices)
        pl.semaphore_signal(barrier, inc=1, device_id=(other // devices, other % devices), device_id_type=MESH)
    load_out = load(wout_hbm, wout, 0)
    load_gate = load(wg_hbm, wgate, 1)
    load_up = load(wu_hbm, wup, 2)
    load_down = load(wd_hbm, wdown, 3)
    later = [load(kv_hbm, kv_nat, 4), load(q_hbm, q_pair, 5), load(hat_hbm, hat, 6), load(cos_hbm, cos_ref, 7), load(sine_hbm, sine_ref, 8)]
    invert(order_ref, inverse_ref)

    for group in range(8):
        block = att_ref[:, :, group * 256 : (group + 1) * 256].reshape(128, 256).T
        for piece in range(4):
            att_turned[(group // 4) * 4 + piece, pl.ds((group % 4) * 64, 64), :] = block[piece * 64 : (piece + 1) * 64]
    load_out.wait()
    attn_proj = dot(att_ref[...].reshape(128, 2048), wout[...])
    att_factor = row_scale(attn_proj)
    normal = attn_proj * att_factor
    att_hat[...] = normal
    stream = tok_ref[...].reshape(128, 1024).astype(WIDE) + normal * again_ref[...]
    hidden[...] = stream
    hid_own[...] = stream.astype(LOW)
    pl.semaphore_wait(barrier, 2 * devices - 1)

    x_place, y_place, sib_place = (dp, spot.flip_x), (1 - dp, seq), (dp, spot.sibling)
    x_member = dp * 4 + (1 - spot.x) * 2 + core
    y_member = (1 - dp) * 4 + spot.x * 2 + core
    diagonal = (1 - dp) * 4 + (1 - spot.x) * 2 + core
    keeps = {}

    def spread(own, held, sems, index):
        keeps[index] = load(own, held.at[member], index)
        for place in (x_place, y_place, sib_place):
            post.send(own, held.at[member], sems.at[member], place)

    def pass_on(held, sems, across):
        turn = (x_member, y_place) if across == "y" else (y_member, x_place)
        straight = y_member if across == "y" else x_member
        for other, places in ((turn[0], (turn[1], sib_place)), (straight, (sib_place,))):
            arrived(spot, held.at[other], sems.at[other], spare)
            for place in places:
                post.send(held.at[other], held.at[other], sems.at[other], place)

    def pass_diagonal(held, sems):
        arrived(spot, held.at[diagonal], sems.at[diagonal], spare)
        post.send(held.at[diagonal], held.at[diagonal], sems.at[diagonal], sib_place)

    def whole(held, sems, index):
        keeps[index].wait()
        for y in range(2):
            for x in range(2):
                other = y * 4 + x * 2 + 1 - core
                arrived(spot, held.at[other], sems.at[other], spare)

    def deal(own, held, sems, index):
        keeps[index] = load(own.at[member], held.at[member], index)
        for step in range(1, 8):
            other = (member + step) % 8
            post.send(own.at[other], held.at[member], sems.at[member], (other // 4, z * 4 + other % 4))

    def dealt(held, sems, index):
        keeps[index].wait()
        for step in range(1, 8):
            other = (member + step) % 8
            arrived(spot, held.at[other], sems.at[other], spare)

    spread(hid_own, hid_all, hid_sems, 9)

    load_gate.wait()
    load_up.wait()
    for group in range(8):
        lanes = slice(group * 384, (group + 1) * 384)
        gate = dot(hid_own[...], wgate[:, lanes])
        up = dot(hid_own[...], wup[:, lanes])
        gate_pre[group] = gate
        up_pre[group] = up
        block = (gate * jax.nn.sigmoid(gate) * up).astype(LOW)
        mixed[:, lanes] = block
        turned = block.T
        for piece in range(4):
            mix_turned[(group // 4) * 4 + piece, pl.ds((group % 4) * 96, 96), :] = turned[piece * 96 : (piece + 1) * 96]
    deal(mix_turned, mix_all, mix_sems, 11)
    pass_on(hid_all, hid_sems, "y")
    load_down.wait()
    down_pre = dot(mixed[...], wdown[...])
    factor = row_scale(down_pre)
    normal = down_pre * factor
    cot = cot_ref[...].reshape(128, 1024).astype(WIDE)
    layer_out[...] = (hidden[...] + normal * mgain_ref[...]).astype(LOW)
    down_own[...] = norm_back(cot, mgain_ref[...], normal, factor).astype(LOW)
    vec_own[...] = jnp.zeros_like(vec_own)
    vec_own[1:2, :] = jnp.sum(cot * normal, axis=0, keepdims=True)
    spread(down_own, down_all, dpl_sems, 12)

    for step in range(1, 9):
        group = (member + step) % 8
        grad = dot_nt(down_own[...], wdown[aligned(group * 384, 384), :])
        gate, up = gate_pre[group], up_pre[group]
        sigmoid = jax.nn.sigmoid(gate)
        gu_own[group, :, :384] = (grad * up * sigmoid * (1.0 + gate * (1.0 - sigmoid))).astype(LOW)
        gu_own[group, :, 384:] = (grad * gate * sigmoid).astype(LOW)
    hgrad = cot
    for group in range(8):
        lanes = slice(group * 384, (group + 1) * 384)
        hgrad = hgrad + dot_nt(gu_own[group, :, :384], wgate[:, lanes]) + dot_nt(gu_own[group, :, 384:], wup[:, lanes])
    hidden[...] = hgrad
    normal = att_hat[...]
    proj_own[...] = norm_back(hgrad, again_ref[...], normal, att_factor).astype(LOW)
    vec_own[0:1, :] = jnp.sum(hgrad * normal, axis=0, keepdims=True)
    load_query = load(wq_hbm, wgate.at[:, pl.ds(0, 2048)], 1)
    load_key = load(wk_hbm, wgate.at[:, pl.ds(2048, 1024)], 2)
    load_value = load(wv_hbm, wup.at[:, pl.ds(0, 1024)], 3)

    att_grad = dot_nt(proj_own[...], wout[...]).astype(LOW)
    ag_own[...] = att_grad.reshape(2, 64, 2048)
    keep_ag = load(ag_own.at[core, :, aligned(chip * 256, 256)], ag_recv.at[seq], 14)
    for step in range(1, devices):
        other = (seq + step) % devices
        post.send(
            ag_own.at[other % 2, :, aligned((other // 2) * 256, 256)], ag_recv.at[seq], ag_sems.at[seq], (dp, other)
        )
    load_tok = load(tok_hbm, wout.at[pl.ds(0, 1024)], 0)
    pass_diagonal(hid_all, hid_sems)
    pass_on(down_all, dpl_sems, "x")
    deal(gu_own, gu_all, gup_sems, 13)
    deal(att_turned, att_all, attp_sems, 10)
    spread(proj_own, proj_all, proj_sems, 15)
    keep_vec = load(vec_own, vec_all.at[member], 16)
    for step in range(1, 8):
        other = (member + step) % 8
        post.send(vec_own, vec_all.at[member], vec_sems.at[member], (other // 4, z * 4 + other % 4))
    for copy in later:
        copy.wait()
    keep_ag.wait()
    for step in range(1, devices):
        other = (seq + step) % devices
        arrived(spot, ag_recv.at[other], ag_sems.at[other], spare)
    for tile in range(8):
        block = jnp.concatenate([ag_recv[inverse_ref[tile * 2 + piece]] for piece in range(2)], axis=0)
        ag_pair[tile, :TILE, :] = block[:, :HD]
        ag_pair[tile, TILE:, :] = block[:, HD:]
    k_turned[...] = kv_nat[:, :HD].T
    first_length = docs_ref[core, 0, 0]
    up_pre[:, :, :256] = jnp.zeros((8, TILE, 256), WIDE)
    down_part = wdown.at[pl.ds(0, 384)]
    for tile in range(7, -1, -1):
        if tile == 4:
            pass_diagonal(down_all, dpl_sems)
            dealt(mix_all, mix_sems, 11)
            whole(down_all, dpl_sems, 12)
            mixes = jnp.concatenate([mix_all[other] for other in range(8)], axis=1)
            down_part[...] = dot(mixes, down_all[...].reshape(1024, 1024)).astype(LOW)
            along.send(down_part, 96, down_land, down_transit, down_sems)
        count = (tile + 1) * TILE
        queries, grads = q_pair[tile], ag_pair[tile]
        scores = dot_nt(kv_nat[:count, :HD], queries) * HD ** (-0.5)
        masked = jnp.where(allowed_places(tile, count, first_length), scores, MASK_FILL)
        probs = jnp.exp(masked - lse[tile : tile + 1, :])
        prob_grad = dot_nt(kv_nat[:count, HD:], grads)
        row_dot = jnp.sum(probs * prob_grad, axis=0, keepdims=True)
        score_grad = (probs * (prob_grad - row_dot)).astype(LOW)
        up_pre[: tile + 1, :, :HD] += dot(score_grad, queries).reshape(tile + 1, TILE, HD)
        up_pre[: tile + 1, :, HD:256] += dot(probs.astype(LOW), grads).reshape(tile + 1, TILE, HD)
        turned = (dot(k_turned[:, :count], score_grad) * HD ** (-0.5)).T
        gate_pre[tile, :, :HD] = turned[:TILE]
        gate_pre[tile, :, HD:256] = turned[TILE:]

    qgain = qgain_ref[pl.ds(chip * 2, 2), :]
    kgain = kgain_ref[pl.ds(chip, 1), :]
    gains = [jnp.zeros((1, HD), WIDE) for _ in range(3)]
    for part in range(8):
        rows = pl.ds(part * TILE, TILE)
        cos = jnp.concatenate([rope_rows(cos_ref, part * 2 + piece, first_length) for piece in range(2)], axis=0)
        sine = jnp.concatenate([rope_rows(sine_ref, part * 2 + piece, first_length) for piece in range(2)], axis=0)
        dots = []
        for head in range(3):
            lanes = slice(head * HD, (head + 1) * HD)
            turned = gate_pre[part, :, lanes] if head < 2 else up_pre[part, :, :HD] * HD ** (-0.5)
            back = turned * cos - swap_halves(turned) * sine
            normal = hat[rows, lanes]
            gain = qgain[head : head + 1] if head < 2 else kgain
            gains[head] = gains[head] + jnp.sum(back * normal, axis=0, keepdims=True)
            weighted = back * gain
            if head < 2:
                gate_pre[part, :, lanes] = weighted
            else:
                up_pre[part, :, :HD] = weighted
            dots.append(jnp.sum(weighted * normal, axis=-1, keepdims=True))
        stat_all[pl.ds(chip, 1), :, rows] = rows_of(dots[0] + dots[1], dots[2])[None]
    for step in range(1, chips):
        other = (chip + step) % chips
        post.send(stat_all.at[chip], stat_all.at[chip], stat_sems.at[chip], (dp, other * 2 + core))
    gain_own[...] = jnp.concatenate([jnp.broadcast_to(gain, (8, HD)) for gain in gains], axis=1)
    for piece in range(4):
        target = chip * 4 + piece
        slot = gain_recv.at[dp * 2 + core]

        @pl.when(target == me)
        def _():
            gain_recv[pl.ds(dp * 2 + core, 1)] = gain_own[...][None]

        post.send(gain_own, slot, gain_sems.at[dp * 2 + core], (target // devices, target % devices), target != me)

    along.combine(down_part, 96, down_land, down_transit, down_sems)
    for step in range(1, chips):
        other = (chip + step) % chips
        arrived(spot, stat_all.at[other], stat_sems.at[other], spare)
    total = stat_all[0]
    for other in range(1, chips):
        total = total + stat_all[other]
    width = jnp.where(lax.broadcasted_iota(jnp.int32, total.shape, 0) == 0, 1.0 / 2048, 1.0 / 1024)
    means = total * width
    grad_send = wdown.at[pl.ds(1024, 1024), pl.ds(512, 512)]
    for part in range(8):
        rows = pl.ds(part * TILE, TILE)
        mean = columns_of(means[:, part * TILE : (part + 1) * TILE])
        scale = columns_of(factors[:, rows])
        for head in range(3):
            column = 0 if head < 2 else 1
            weighted = gate_pre[part, :, head * HD : (head + 1) * HD] if head < 2 else up_pre[part, :, :HD]
            normal = hat[rows, pl.ds(head * HD, HD)]
            grad = scale[:, column : column + 1] * (weighted - normal * mean[:, column : column + 1])
            grad_nat[pl.ds(part * 2, 2), :, head * HD : (head + 1) * HD] = grad.astype(LOW).reshape(2, 64, HD)
        grad_nat[pl.ds(part * 2, 2), :, 3 * HD :] = up_pre[part, :, HD:256].astype(LOW).reshape(2, 64, HD)
    grad_recv[pl.ds(chip, 1), pl.ds(core, 1)] = grad_nat[order_ref[seq]][None, None]
    for step in range(1, devices):
        other = (seq + step) % devices
        rows = pl.ds(step * 64, 64)
        grad_send[rows, :] = grad_nat[order_ref[other]]
        post.send(grad_send.at[rows], grad_recv.at[chip, core], grad_sems.at[seq], (dp, other))

    load_tok.wait()
    part_low = wdown.at[pl.ds(2048, 1024), pl.ds(0, 512)]
    part_low[...] = dot_tn(wout[:1024, :], grad_nat[...].reshape(1024, 512)).astype(LOW)
    post.send(part_low.at[aligned((1 - core) * 512, 512)], part_sib, sib_sem.at[0], sib_place)

    dealt(gu_all, gup_sems, 13)
    whole(hid_all, hid_sems, 9)
    gu_part = wout.at[pl.ds(1024, 1024), pl.ds(0, 768)]
    gu_part[...] = dot_tn(hid_all[...].reshape(1024, 1024), gu_all[...].reshape(1024, 768)).astype(LOW)
    for y in range(2):
        for slot, far in enumerate((along.far_inner, along.far_outer)):
            post.send(
                gu_part.at[aligned(y * 512 + far * 128, 128)], gu_transit.at[slot, y], gut_sems.at[slot, y],
                along.place(along.partner), along.outer,
            )
    for step in range(8):
        other = (member + step) % 8
        first = (other // 4) * 512 + (other % 4) * 32
        post.send(
            gu_part.at[aligned(first + along.partner * 128, 32)], gu_land.at[0, member], gu_sems.at[0, member],
            (other // 4, along.partner * 4 + other % 4),
        )
        if step > 0:
            post.send(
                gu_part.at[aligned(first + z * 128, 32)], gu_land.at[2, member], gu_sems.at[2, member],
                (other // 4, z * 4 + other % 4),
            )
    gu_land[2, pl.ds(member, 1)] = gu_part[aligned((member // 4) * 512 + z * 128 + (member % 4) * 32, 32), :][None]

    arrived(spot, part_sib, sib_sem.at[0], spare)
    part_sum = wdown.at[pl.ds(2048, 512), pl.ds(512, 512)]
    part_sum[...] = (part_low[aligned(core * 512, 512), :].astype(WIDE) + part_sib[...].astype(WIDE)).astype(LOW)
    own_slot = dp * chips + chip

    @pl.when(core == dp)
    def _():
        wqkv_recv[pl.ds(own_slot, 1)] = part_sum[aligned(seq * 32, 32), :][None]

    post.send(part_sum.at[aligned(seq * 32, 32)], wqkv_recv.at[own_slot], wqkv_sems.at[own_slot], (1 - dp, seq), core != dp)
    for step in range(1, devices):
        other = (seq + step) % devices
        post.send(part_sum.at[aligned(other * 32, 32)], wqkv_recv.at[own_slot], wqkv_sems.at[own_slot], (core, other))

    pass_on(proj_all, proj_sems, "y")
    pass_diagonal(proj_all, proj_sems)
    dealt(att_all, attp_sems, 10)
    whole(proj_all, proj_sems, 15)
    turned = jnp.concatenate([att_all[other] for other in range(8)], axis=1)
    wout_part[...] = dot(turned, proj_all[...].reshape(1024, 1024)).astype(LOW)
    wout_land[pl.ds(z, 1)] = wout_part[aligned(z * 64, 64), :][None]
    for far in spot.far_z:
        post.send(wout_part.at[aligned(far * 64, 64)], wout_land.at[z], wout_sems.at[z], along.place(far))
    keep_vec.wait()
    for step in range(1, 8):
        other = (member + step) % 8
        arrived(spot, vec_all.at[other], vec_sems.at[other], spare)
    vec = vec_all[0]
    for other in range(1, 8):
        vec = vec + vec_all[other]
    vec_far[pl.ds(z, 1)] = vec[None]
    for far in spot.far_z:
        post.send(vec_far.at[z], vec_far.at[z], vec_sems.at[8 + z], along.place(far))

    for step in range(1, devices):
        other = (seq + step) % devices
        arrived(spot, grad_recv.at[other // 2, other % 2], grad_sems.at[other], spare)
    load_query.wait()
    load_key.wait()
    load_value.wait()
    grad_k, grad_v = [], []
    gradient = hidden[...]
    for piece in range(chips):
        block = grad_recv[piece].reshape(128, 512)
        gradient = gradient + dot_nt(block[:, :256], wgate[:, piece * 256 : (piece + 1) * 256])
        grad_k.append(block[:, 256:384])
        grad_v.append(block[:, 384:])
    gradient = gradient + dot_nt(jnp.concatenate(grad_k, axis=1), wgate[:, 2048:])
    in_grad[...] = gradient + dot_nt(jnp.concatenate(grad_v, axis=1), wup[:, :1024])

    for slot, far in enumerate((along.far_inner, along.far_outer)):
        for y in range(2):

            @pl.when(along.inner)
            def _():
                arrived(spot, gu_transit.at[slot, y], gut_sems.at[slot, y], spare)
                added = gu_transit[slot, y].astype(WIDE) + gu_part[aligned(y * 512 + far * 128, 128), :].astype(WIDE)
                gu_transit[slot, y] = added.astype(LOW)

            for piece in range(4):
                post.send(
                    gu_transit.at[slot, y, pl.ds(piece * 32, 32)], gu_land.at[1, member], gu_sems.at[1, member],
                    (y, far * 4 + piece), along.inner,
                )

    for y in range(2):
        for micro in range(2):
            source = y * 2 + micro
            sender = y * devices + (me // 4) * 2 + micro

            @pl.when(sender != me)
            def _():
                arrived(spot, gain_recv.at[source], gain_sems.at[source], spare)

    gain_out[...] = sum(gain_recv[source] for source in range(4))
    for source in range(16):
        sender = (source // chips) * devices + (source % chips) * 2 + dp

        @pl.when(sender != me)
        def _():
            arrived(spot, wqkv_recv.at[source], wqkv_sems.at[source], spare)

    for piece in range(chips):
        block = wqkv_recv[piece].astype(WIDE) + wqkv_recv[chips + piece].astype(WIDE)
        g_query[:, piece * 256 : (piece + 1) * 256] = block[:, :256]
        g_key[:, piece * 128 : (piece + 1) * 128] = block[:, 256:384]
        g_value[:, piece * 128 : (piece + 1) * 128] = block[:, 384:]
    for far in spot.far_z:
        arrived(spot, vec_far.at[far], vec_sems.at[8 + far], spare)
    vec_out[...] = sum(vec_far[far] for far in range(4))
    g_down[...] = along.total(down_land, down_sems)
    for step in range(8):
        other = (member + step) % 8
        for kind in range(3):
            if kind < 2 or step > 0:
                arrived(spot, gu_land.at[kind, other], gu_sems.at[kind, other], spare)
    for slot in range(8):
        block = sum(gu_land[kind, slot].astype(WIDE) for kind in range(3))
        g_gate[:, slot * 384 : (slot + 1) * 384] = block[:, :384]
        g_up[:, slot * 384 : (slot + 1) * 384] = block[:, 384:]
    for far in spot.far_z:
        arrived(spot, wout_land.at[far], wout_sems.at[far], spare)
    g_out[...] = sum(wout_land[far].astype(WIDE) for far in range(4))
    post.finish()


POST_SENDS = 288


def row_backward(*operands):
    length, width = 1024, 1024
    any_spec = pl.BlockSpec(memory_space=pl.ANY)
    vmem = pl.BlockSpec(memory_space=pltpu.VMEM)
    smem = pl.BlockSpec(memory_space=pltpu.SMEM)
    shape = jax.ShapeDtypeStruct
    dma = pltpu.SemaphoreType.DMA
    return pl.pallas_call(
        backward_kernel,
        out_shape=(
            shape((128, width), LOW),
            shape((128, width), WIDE),
            shape((32, 2048), WIDE),
            shape((32, 1024), WIDE),
            shape((32, 1024), WIDE),
            shape((64, 1024), WIDE),
            shape((8, 1024), WIDE),
            shape((8, 384), WIDE),
            shape((32, 3072), WIDE),
            shape((32, 3072), WIDE),
            shape((96, 1024), WIDE),
        ),
        in_specs=[vmem] * 9 + [any_spec] * 13 + [smem] * 2,
        out_specs=(vmem,) * 11,
        scratch_shapes=[
            pltpu.VMEM((2048, width), LOW),
            pltpu.VMEM((width, 3072), LOW),
            pltpu.VMEM((width, 3072), LOW),
            pltpu.VMEM((3072, width), LOW),
            pltpu.VMEM((8, 2 * TILE, HD), LOW),
            pltpu.VMEM((length, 2 * HD), LOW),
            pltpu.VMEM((length, 3 * HD), WIDE),
            pltpu.VMEM((length + 64, HD), WIDE),
            pltpu.VMEM((length + 64, HD), WIDE),
            pltpu.VMEM((128, width), WIDE),
            pltpu.VMEM((128, width), WIDE),
            pltpu.VMEM((128, width), LOW),
            pltpu.VMEM((8, 128, 384), WIDE),
            pltpu.VMEM((8, 128, 384), WIDE),
            pltpu.VMEM((128, 3072), LOW),
            pltpu.VMEM((8, 384, 128), LOW),
            pltpu.VMEM((8, 256, 128), LOW),
            pltpu.VMEM((128, width), LOW),
            pltpu.VMEM((8, 128, 768), LOW),
            pltpu.VMEM((128, width), LOW),
            pltpu.VMEM((2, 64, 2048), LOW),
            pltpu.VMEM((8, width), WIDE),
            pltpu.VMEM((8, 128, width), LOW),
            pltpu.VMEM((8, 128, width), LOW),
            pltpu.VMEM((8, 128, width), LOW),
            pltpu.VMEM((8, 128, 768), LOW),
            pltpu.VMEM((8, 384, 128), LOW),
            pltpu.VMEM((8, 256, 128), LOW),
            pltpu.VMEM((8, 8, width), WIDE),
            pltpu.VMEM((4, 8, width), WIDE),
            pltpu.VMEM((3, 96, width), LOW),
            pltpu.VMEM((2, 96, width), LOW),
            pltpu.VMEM((256, width), LOW),
            pltpu.VMEM((4, 64, width), LOW),
            pltpu.VMEM((3, 8, 32, 768), LOW),
            pltpu.VMEM((2, 2, 128, 768), LOW),
            pltpu.VMEM((16, 64, 256), LOW),
            pltpu.VMEM((8, 2 * TILE, HD), LOW),
            pltpu.VMEM((HD, length), LOW),
            pltpu.VMEM((8, 8, length), WIDE),
            pltpu.VMEM((16, 64, 512), LOW),
            pltpu.VMEM((8, 2, 64, 512), LOW),
            pltpu.VMEM((512, 512), LOW),
            pltpu.VMEM((16, 32, 512), LOW),
            pltpu.VMEM((8, 384), WIDE),
            pltpu.VMEM((4, 8, 384), WIDE),
            pltpu.SMEM((16,), jnp.int32),
            dma((17,)),
            dma((POST_SENDS,)),
            dma((8,)),
            dma((8,)),
            dma((8,)),
            dma((8,)),
            dma((8,)),
            dma((8,)),
            dma((12,)),
            dma((4,)),
            dma((4,)),
            dma((3, 8)),
            dma((2, 2)),
            dma((16,)),
            dma((8,)),
            dma((16,)),
            dma((1,)),
            dma((16,)),
            dma((4,)),
        ],
        compiler_params=pltpu.CompilerParams(
            collective_id=1, has_side_effects=True, vmem_limit_bytes=63 * 2**20
        ),
        name="row_backward",
    )(*operands)


def finish_kernel(*refs):
    count = 9
    sources, vec_ref, gain_ref = refs[:count], refs[count], refs[count + 1]
    targets, small = refs[count + 2 : 2 * count + 2], refs[2 * count + 2 :]
    for source, target in zip(sources, targets):
        target[...] = source[...]
    seq = lax.axis_index("seq")
    me = lax.axis_index("dp") * 16 + seq
    part = seq % 4
    gains, vec = gain_ref[...], vec_ref[...]
    q_out, k_out, attn_out, mlp_out = small
    q_all = pltpu.roll(gains[:, :256], (256 - part * 64) % 256, axis=1)
    k_all = pltpu.roll(gains[:, 256:], (128 - part * 32) % 128, axis=1)
    vec = pltpu.roll(vec, (1024 - me * 32) % 1024, axis=1)
    q_out[...] = q_all[0:1, :64]
    k_out[...] = k_all[0:1, :32]
    attn_out[...] = vec[0:1, :32]
    mlp_out[...] = vec[1:2, :32]


def finish(arrays, vec, gains):
    vmem = pl.BlockSpec(memory_space=pltpu.VMEM)
    shape = jax.ShapeDtypeStruct
    count = len(arrays)
    return pl.pallas_call(
        finish_kernel,
        out_shape=tuple(shape(a.shape, a.dtype) for a in arrays)
        + (shape((1, 64), WIDE), shape((1, 32), WIDE), shape((1, 32), WIDE), shape((1, 32), WIDE)),
        in_specs=[vmem] * (count + 2),
        out_specs=(vmem,) * (count + 4),
        name="finish",
    )(*arrays, vec, gains)


def rms_forward(inputs, gain_vec):
    factor = lax.rsqrt(jnp.mean(inputs * inputs, axis=-1, keepdims=True) + EPSILON)
    normal = inputs * factor
    return (normal * gain_vec, normal, factor)


def rms_backward(grad_in, gain_vec, normal, factor):
    weighted = grad_in * gain_vec
    gain_grad = jnp.sum(grad_in * normal, axis=0)
    inner_mean = jnp.mean(weighted * normal, axis=-1, keepdims=True)
    return (factor * (weighted - normal * inner_mean), gain_grad)


def rope_tables(rot_places, head_size):
    frequency = jnp.power(ROPE_BASE, -jnp.arange(0, head_size, 2).astype(jnp.float32) / head_size)
    angles = rot_places.astype(jnp.float32)[:, None] * frequency[None, :]
    return (jnp.cos(angles), jnp.sin(angles))


def rotate(inputs, cos_table, sine_table, head_count, direction):
    row_count = inputs.shape[0]
    halves = inputs.reshape(row_count, head_count, 2, -1)
    first_half = halves[:, :, 0]
    second = halves[:, :, 1]
    cos_part = cos_table[:, None, :]
    sine_part = sine_table[:, None, :] * direction
    turned = jnp.stack(
        [first_half * cos_part - second * sine_part, second * cos_part + first_half * sine_part],
        axis=2,
    )
    return turned.reshape(row_count, -1)


def product(left, right):
    return jnp.dot(left, right, preferred_element_type=jnp.float32)


def weight_grad(left, right):
    return lax.dot_general(
        left, right, (((0,), (0,)), ((), ())), preferred_element_type=jnp.float32
    )


def back_product(left, right):
    return lax.dot_general(
        left, right, (((1,), (1,)), ((), ())), preferred_element_type=jnp.float32
    )


def heads_first(rows, group_count, head_size):
    shaped = rows.reshape(rows.shape[0], group_count, -1, head_size)
    return jnp.moveaxis(shaped, 1, 0)


def kv_first(rows, group_count, head_size):
    return jnp.moveaxis(rows.reshape(rows.shape[0], group_count, head_size), 1, 0)


def score_block(q_group, k_group, mask_rows, score_scale):
    raw_scores = (
        jnp.einsum("trd,ud->rtu", q_group, k_group, preferred_element_type=jnp.float32)
        * score_scale
    )
    return jnp.where(mask_rows[None], raw_scores, MASK_FILL)


def attend(pieces, score_scale, group_count, head_size):
    q_rows, key_rows, value_rows, mask_rows = pieces

    def attend_one_group(parts):
        q_group, k_group, v_group = parts
        masked = score_block(q_group, k_group, mask_rows, score_scale)
        row_max = jnp.max(masked, axis=-1)
        exp_terms = jnp.exp(masked - row_max[..., None])
        row_sum = jnp.sum(exp_terms, axis=-1)
        attn_prob = (exp_terms / row_sum[..., None]).astype(jnp.bfloat16)
        attended = jnp.einsum("rtu,ud->trd", attn_prob, v_group, preferred_element_type=jnp.float32)
        return (attended, row_max, row_sum)

    attended, row_max, row_sum = lax.map(
        attend_one_group,
        (
            heads_first(q_rows, group_count, head_size),
            kv_first(key_rows, group_count, head_size),
            kv_first(value_rows, group_count, head_size),
        ),
    )
    attended = jnp.moveaxis(attended, 0, 1)
    return (attended.reshape(q_rows.shape[0], -1), row_max, row_sum)


def score_grads(
    q_group, grad_group, k_group, v_group, mask_rows, row_max, row_sum, row_dot, score_scale
):
    masked = score_block(q_group, k_group, mask_rows, score_scale)
    attn_prob = jnp.exp(masked - row_max[..., None]) / row_sum[..., None]
    prob_grad = jnp.einsum("trd,ud->rtu", grad_group, v_group, preferred_element_type=jnp.float32)
    row_dot = jnp.sum(attn_prob * prob_grad, axis=-1)
    score_grad = (attn_prob * (prob_grad - row_dot[..., None])).astype(jnp.bfloat16)
    return (attn_prob.astype(jnp.bfloat16), score_grad, row_dot)


def on_device(
    tokens,
    cotangent,
    w_query,
    w_key,
    w_value,
    w_out,
    q_gain,
    k_gain,
    attn_gain,
    w_gate,
    w_up,
    w_down,
    mlp_gain,
    doc_lengths,
    block_order,
):
    micro_count = tokens.shape[0]
    block_len = tokens.shape[2]
    model_width = tokens.shape[3]
    seq_length = lax.axis_size("seq") * block_len
    head_count = w_query.shape[1] // HD
    group_count = w_key.shape[1] // HD
    score_scale = HD ** (-0.5)
    flat_tokens = tokens.reshape(micro_count * block_len, model_width)
    out_grad = cotangent.reshape(micro_count * block_len, model_width).astype(jnp.float32)
    first_lengths = doc_lengths[:, 0, 0]
    offsets = jnp.arange(block_len, dtype=jnp.int32)
    own_places = block_order[lax.axis_index("seq")] * block_len + offsets
    key_places = (block_order[:, None] * block_len + offsets[None, :]).reshape(seq_length)
    own_segments = (own_places[None, :] >= first_lengths[:, None]).astype(jnp.int32)
    all_segments = (key_places[None, :] >= first_lengths[:, None]).astype(jnp.int32)
    rot_places = (own_places[None, :] - own_segments * first_lengths[:, None]).reshape(-1)
    allowed = (own_segments[:, :, None] == all_segments[:, None, :]) & (
        key_places[None, None, :] <= own_places[None, :, None]
    )
    cos_table, sine_table = rope_tables(rot_places, HD)
    q_pre = product(flat_tokens, w_query)
    k_pre = product(flat_tokens, w_key)
    v_pre = product(flat_tokens, w_value)
    q_norm, q_hat, q_factor = rms_forward(q_pre, q_gain)
    k_norm, k_hat, k_factor = rms_forward(k_pre, k_gain)
    q_low = rotate(q_norm, cos_table, sine_table, head_count, 1.0).astype(jnp.bfloat16)
    k_low = rotate(k_norm, cos_table, sine_table, group_count, 1.0).astype(jnp.bfloat16)
    v_low = v_pre.astype(jnp.bfloat16)
    q_blocks = q_low.reshape(micro_count, block_len, -1)
    k_blocks = k_low.reshape(micro_count, block_len, -1)
    v_blocks = v_low.reshape(micro_count, block_len, -1)
    key_all, value_all = (
        lax.all_gather(k_blocks, "seq", axis=1, tiled=True),
        lax.all_gather(v_blocks, "seq", axis=1, tiled=True),
    )

    def forward_block(pieces):
        return attend(pieces, score_scale, group_count, HD)

    attended, row_max, row_sum = lax.map(forward_block, (q_blocks, key_all, value_all, allowed))
    att_low = attended.reshape(micro_count * block_len, -1).astype(jnp.bfloat16)
    attn_proj = product(att_low, w_out)
    attn_normed, attn_hat, attn_factor = rms_forward(attn_proj, attn_gain)
    hidden = flat_tokens.astype(jnp.float32) + attn_normed
    hidden_low = hidden.astype(jnp.bfloat16)
    gate_pre = product(hidden_low, w_gate)
    up_pre = product(hidden_low, w_up)
    mixed_low = (jax.nn.silu(gate_pre) * up_pre).astype(jnp.bfloat16)
    down_pre = product(mixed_low, w_down)
    down_normed, down_hat, down_factor = rms_forward(down_pre, mlp_gain)
    layer_out = (hidden + down_normed).astype(jnp.bfloat16).reshape(tokens.shape)
    down_grad, grad_mlp_gain = rms_backward(out_grad, mlp_gain, down_hat, down_factor)
    down_grad = down_grad.astype(jnp.bfloat16)
    grad_w_down = weight_grad(mixed_low, down_grad)
    mixed_grad = back_product(down_grad, w_down)
    sigmoid_gate = jax.nn.sigmoid(gate_pre)
    gate_grad = (
        mixed_grad * up_pre * sigmoid_gate * (1.0 + gate_pre * (1.0 - sigmoid_gate))
    ).astype(jnp.bfloat16)
    up_grad = (mixed_grad * gate_pre * sigmoid_gate).astype(jnp.bfloat16)
    grad_w_gate = weight_grad(hidden_low, gate_grad)
    grad_w_up = weight_grad(hidden_low, up_grad)
    hidden_grad = out_grad + back_product(gate_grad, w_gate) + back_product(up_grad, w_up)
    proj_grad, grad_attn_gain = rms_backward(hidden_grad, attn_gain, attn_hat, attn_factor)
    proj_grad = proj_grad.astype(jnp.bfloat16)
    grad_w_out = weight_grad(att_low, proj_grad)
    att_grad = back_product(proj_grad, w_out).astype(jnp.bfloat16)
    grad_blocks = att_grad.reshape(micro_count, block_len, -1)
    key_back, value_back = (key_all, value_all)

    def query_pass(pieces):
        q_rows, grad_rows, key_rows, value_rows, mask_rows, max_rows, sum_rows = pieces

        def query_one_group(parts):
            q_group, grad_group, k_group, v_group, max_group, sum_group = parts
            prob_low, score_grad, unused = score_grads(
                q_group,
                grad_group,
                k_group,
                v_group,
                mask_rows,
                max_group,
                sum_group,
                None,
                score_scale,
            )
            q_grad = (
                jnp.einsum("rtu,ud->trd", score_grad, k_group, preferred_element_type=jnp.float32)
                * score_scale
            )
            key_terms = (
                jnp.einsum("rtu,trd->ud", score_grad, q_group, preferred_element_type=jnp.float32)
                * score_scale
            )
            value_terms = jnp.einsum(
                "rtu,trd->ud", prob_low, grad_group, preferred_element_type=jnp.float32
            )
            return (q_grad, key_terms, value_terms)

        q_grad, key_terms, value_terms = lax.map(
            query_one_group,
            (
                heads_first(q_rows, group_count, HD),
                heads_first(grad_rows, group_count, HD),
                kv_first(key_rows, group_count, HD),
                kv_first(value_rows, group_count, HD),
                max_rows,
                sum_rows,
            ),
        )
        q_grad = jnp.moveaxis(q_grad, 0, 1).reshape(block_len, -1)
        key_terms = jnp.moveaxis(key_terms, 0, 1).reshape(seq_length, -1)
        value_terms = jnp.moveaxis(value_terms, 0, 1).reshape(seq_length, -1)
        key_own, value_own = (
            lax.psum_scatter(key_terms, "seq", scatter_dimension=0, tiled=True),
            lax.psum_scatter(value_terms, "seq", scatter_dimension=0, tiled=True),
        )
        return (q_grad, key_own, value_own)

    q_rot_grad, k_rot_grad, value_grad = lax.map(
        query_pass, (q_blocks, grad_blocks, key_back, value_back, allowed, row_max, row_sum)
    )
    q_rot_grad = q_rot_grad.reshape(micro_count * block_len, -1)
    k_rot_grad = k_rot_grad.reshape(micro_count * block_len, -1)
    v_grad = value_grad.reshape(micro_count * block_len, -1).astype(jnp.bfloat16)
    q_norm_grad = rotate(q_rot_grad, cos_table, sine_table, head_count, -1.0)
    k_norm_grad = rotate(k_rot_grad, cos_table, sine_table, group_count, -1.0)
    q_grad, grad_q_gain = rms_backward(q_norm_grad, q_gain, q_hat, q_factor)
    k_grad, grad_k_gain = rms_backward(k_norm_grad, k_gain, k_hat, k_factor)
    q_grad = q_grad.astype(jnp.bfloat16)
    k_grad = k_grad.astype(jnp.bfloat16)
    grad_w_query = weight_grad(flat_tokens, q_grad)
    grad_w_key = weight_grad(flat_tokens, k_grad)
    grad_w_value = weight_grad(flat_tokens, v_grad)
    input_grad = (
        hidden_grad
        + back_product(q_grad, w_query)
        + back_product(k_grad, w_key)
        + back_product(v_grad, w_value)
    )
    input_grad = input_grad.reshape(tokens.shape)
    summed = (
        lax.psum_scatter(grad_w_query, ("dp", "seq"), scatter_dimension=0, tiled=True),
        lax.psum_scatter(grad_w_key, ("dp", "seq"), scatter_dimension=0, tiled=True),
        lax.psum_scatter(grad_w_value, ("dp", "seq"), scatter_dimension=0, tiled=True),
        lax.psum_scatter(grad_w_out, ("dp", "seq"), scatter_dimension=0, tiled=True),
        lax.psum_scatter(grad_q_gain, ("dp", "seq"), scatter_dimension=0, tiled=True),
        lax.psum_scatter(grad_k_gain, ("dp", "seq"), scatter_dimension=0, tiled=True),
        lax.psum_scatter(grad_attn_gain, ("dp", "seq"), scatter_dimension=0, tiled=True),
        lax.psum_scatter(grad_w_gate, ("dp", "seq"), scatter_dimension=0, tiled=True),
        lax.psum_scatter(grad_w_up, ("dp", "seq"), scatter_dimension=0, tiled=True),
        lax.psum_scatter(grad_w_down, ("dp", "seq"), scatter_dimension=0, tiled=True),
        lax.psum_scatter(grad_mlp_gain, ("dp", "seq"), scatter_dimension=0, tiled=True),
    )
    return (
        layer_out,
        input_grad,
        summed[0],
        summed[1],
        summed[2],
        summed[3],
        summed[4],
        summed[5],
        summed[6],
        summed[7],
        summed[8],
        summed[9],
        summed[10],
    )


def split_by_heads(
    tokens, cotangent, w_query, w_key, w_value, w_out, q_gain, k_gain, attn_gain,
    w_gate, w_up, w_down, mlp_gain, doc_lengths, block_order,
):
    cos, sine = rope_constants(1024)
    q_gain_rows, k_gain_rows = q_gain.reshape(16, HD), k_gain.reshape(8, HD)
    own_tokens = tokens[:, 0]
    att_tok, tok_nat, q_pair, kv_nat, hat, factors, lse = row_forward(
        own_tokens, w_query, w_key, w_value, q_gain_rows, k_gain_rows, cos, sine, block_order, doc_lengths
    )
    layer_out, in_grad, g_query, g_key, g_value, g_out, vec, gains, g_gate, g_up, g_down = row_backward(
        att_tok, own_tokens, cotangent[:, 0], attn_gain[None], mlp_gain[None], q_gain_rows, k_gain_rows, factors, lse,
        tok_nat, q_pair, kv_nat, hat, cos, sine,
        w_out, w_gate, w_up, w_down, w_query, w_key, w_value, block_order, doc_lengths,
    )
    (
        layer_out, in_grad, g_query, g_key, g_value, g_out, g_gate, g_up, g_down,
        g_q_gain, g_k_gain, g_attn_gain, g_mlp_gain,
    ) = finish((layer_out, in_grad, g_query, g_key, g_value, g_out, g_gate, g_up, g_down), vec, gains)
    return (
        layer_out.reshape(tokens.shape),
        in_grad.reshape(tokens.shape),
        g_query,
        g_key,
        g_value,
        g_out,
        g_q_gain[0],
        g_k_gain[0],
        g_attn_gain[0],
        g_gate,
        g_up,
        g_down,
        g_mlp_gain[0],
    )


SPECS_IN = (
    P(None, "dp", "seq", None), P(None, "dp", "seq", None),
    P(), P(), P(), P(), P(), P(), P(), P(), P(), P(), P(),
    P(None, "dp", None), P(),
)
SPECS_OUT = (
    P(None, "dp", "seq", None), P(None, "dp", "seq", None),
    P(("dp", "seq"), None), P(("dp", "seq"), None), P(("dp", "seq"), None), P(("dp", "seq"), None),
    P(("dp", "seq")), P(("dp", "seq")), P(("dp", "seq")),
    P(("dp", "seq"), None), P(("dp", "seq"), None), P(("dp", "seq"), None),
    P(("dp", "seq")),
)


def solution(mesh):
    body = split_by_heads if mesh.shape["seq"] == 16 and mesh.shape["dp"] == 2 else on_device
    return jax.shard_map(body, mesh=mesh, in_specs=SPECS_IN, out_specs=SPECS_OUT, check_vma=False)
```

```python
import functools

import jax
import jax.numpy as jnp
import numpy as np
from jax import lax
from jax.experimental import pallas as pl
from jax.experimental.pallas import tpu as pltpu
from jax.sharding import PartitionSpec as P

HD = 128
EPSILON = 1e-06
ROPE_BASE = 500000.0
MASK_FILL = -1e30
MESH = pl.DeviceIdType.MESH
LOW = jnp.bfloat16
WIDE = jnp.float32
TILE = 128
CHUNK = 256


def remote(source, target, send_sem, recv_sem, place):
    return pltpu.make_async_remote_copy(
        src_ref=source,
        dst_ref=target,
        send_sem=send_sem,
        recv_sem=recv_sem,
        device_id=place,
        device_id_type=MESH,
    )


def dot(left, right):
    return jnp.dot(left, right, preferred_element_type=WIDE)


def dot_nt(left, right):
    return lax.dot_general(left, right, (((1,), (1,)), ((), ())), preferred_element_type=WIDE)


def dot_tn(left, right):
    return lax.dot_general(left, right, (((0,), (0,)), ((), ())), preferred_element_type=WIDE)


class Spot:
    def __init__(self):
        self.dp = lax.axis_index("dp")
        self.seq = lax.axis_index("seq")
        self.core = self.seq % 2
        self.chip = self.seq // 2
        self.x = self.chip % 2
        self.z = self.chip // 2
        self.sibling = self.seq + 1 - 2 * self.core
        self.flip_x = self.seq + 2 - 4 * self.x
        self.far_z = (
            self.z + 1 - 2 * (self.z % 2),
            self.z + 2 - 4 * (self.z // 2),
            3 - self.z,
        )


class RowGather:
    def __init__(self, spot, own, held, local_sem, send_sems, recv_sems):
        self.spot, self.own, self.held = spot, own, held
        self.send_sems, self.recv_sems = send_sems, recv_sems
        self.sent = []
        self.local = pltpu.make_async_copy(own.at[spot.core], held.at[spot.seq], local_sem)

    def send(self, source, slots, recv_sem, target):
        copy = remote(
            source, slots, self.send_sems.at[len(self.sent)], recv_sem, (self.spot.dp, target)
        )
        copy.start()
        self.sent.append(copy)

    def start(self):
        spot = self.spot
        own_slot = self.held.at[spot.seq]
        own_sem = self.recv_sems.at[spot.seq]
        for far in spot.far_z:
            for micro in range(2):
                self.send(self.own.at[micro], own_slot, own_sem, far * 4 + spot.x * 2 + micro)
        for micro in range(2):
            self.send(
                self.own.at[micro], own_slot, own_sem, spot.z * 4 + (1 - spot.x) * 2 + micro
            )
        self.send(self.own.at[1 - spot.core], own_slot, own_sem, spot.sibling)
        self.local.start()

    def arrived(self, slots, recv_sem):
        remote(slots, slots, self.send_sems.at[0], recv_sem, (self.spot.dp, self.spot.sibling)).wait_recv()

    def forward(self):
        spot = self.spot
        for far in spot.far_z:
            first = far * 4 + spot.x * 2
            for core in range(2):
                self.arrived(self.held.at[first + core], self.recv_sems.at[first + core])
            pair = self.held.at[pl.ds(first, 2)]
            self.send(pair, pair, self.recv_sems.at[16 + far], spot.flip_x)

    def finish(self):
        spot = self.spot
        self.arrived(self.held.at[spot.sibling], self.recv_sems.at[spot.sibling])
        for core in range(2):
            slot = spot.z * 4 + (1 - spot.x) * 2 + core
            self.arrived(self.held.at[slot], self.recv_sems.at[slot])
        for far in spot.far_z:
            first = far * 4 + (1 - spot.x) * 2
            self.arrived(self.held.at[pl.ds(first, 2)], self.recv_sems.at[16 + far])
        self.local.wait()

    def drain(self):
        for copy in self.sent:
            copy.wait_send()


GATHER_SENDS = 12
GATHER_RECVS = 20


def rope_rows(table, block, first_length):
    start = block * 64
    inside = table[pl.ds(64 + start, 64), :]
    shifted = table[pl.ds(64 + jnp.maximum(start - first_length, -64), 64), :]
    places = start + lax.broadcasted_iota(jnp.int32, (64, HD), 0)
    both = jnp.where(places < first_length, inside, shifted)
    swapped = swap_halves(both)
    low_half = lax.broadcasted_iota(jnp.int32, (64, HD), 1) < HD // 2
    return jnp.where(low_half, both, swapped), jnp.where(low_half, -swapped, both)


def rope_part(table, part, first_length):
    first, second = (rope_rows(table, part * 2 + piece, first_length) for piece in range(2))
    return jnp.concatenate([first[0], second[0]], axis=0), jnp.concatenate([first[1], second[1]], axis=0)


def swap_halves(head):
    return pltpu.roll(head, HD // 2, axis=1)


def columns_of(rows):
    return jnp.concatenate([rows] * 16, axis=0).T[:, :8]


def rows_of(first, second):
    lane = lax.broadcasted_iota(jnp.int32, (first.shape[0], HD), 1)
    return jnp.where(lane == 0, first, second).T[:8]


def allowed_places(tile, count, first_length):
    keys = lax.broadcasted_iota(jnp.int32, (count, 2 * TILE), 0)
    lanes = lax.broadcasted_iota(jnp.int32, (1, 2 * TILE), 1)
    queries = tile * TILE + lanes % TILE
    earliest = jnp.where(queries < first_length, 0, first_length)
    return (keys >= earliest) & (keys <= queries)


def invert(order_ref, inverse_ref):
    def fill(block, carry):
        place = jnp.int32(0)
        for slot in range(16):
            place = jnp.maximum(place, jnp.where(order_ref[slot] == block, slot, 0))
        inverse_ref[block] = place
        return carry

    lax.fori_loop(0, 16, fill, 0)


class Post:
    def __init__(self, sems):
        self.sems, self.started, self.used = sems, [], 0

    def send(self, source, target, recv_sem, place, when=None):
        copy = remote(source, target, self.sems.at[self.used], recv_sem, place)
        self.used += 1
        self.started.append((copy, when))
        if when is None:
            copy.start()
        else:
            pl.when(when)(copy.start)

    def finish(self):
        started, self.started = self.started, []
        for copy, when in started:
            if when is None:
                copy.wait_send()
            else:
                pl.when(when)(copy.wait_send)


def arrived(spot, slot, recv_sem, spare_sem):
    remote(slot, slot, spare_sem, recv_sem, (spot.dp, spot.sibling)).wait_recv()


def aligned(start, size):
    return pl.ds(pl.multiple_of(start, size), size)


class AlongZ:
    def __init__(self, spot, post, spare):
        self.spot, self.post, self.spare = spot, post, spare
        half = spot.z // 2
        self.partner = spot.far_z[0]
        self.far_inner = 2 - half
        self.far_outer = 3 - 3 * half
        self.inner = ((spot.z + 1) // 2) % 2 == 1
        self.outer = ((spot.z + 1) // 2) % 2 == 0

    def place(self, z):
        return (self.spot.dp, z * 4 + self.spot.x * 2 + self.spot.core)

    def send(self, part, size, landing, transit, sems):
        spot, post = self.spot, self.post
        landing[2] = part[aligned(spot.z * size, size), :]
        for slot, far in enumerate((self.far_inner, self.far_outer)):
            post.send(
                part.at[aligned(far * size, size)], transit.at[slot], sems.at[2 + slot], self.place(self.partner),
                self.outer,
            )
        post.send(part.at[aligned(self.partner * size, size)], landing.at[0], sems.at[0], self.place(self.partner))

    def combine(self, part, size, landing, transit, sems):
        for slot, far in enumerate((self.far_inner, self.far_outer)):

            @pl.when(self.inner)
            def _():
                arrived(self.spot, transit.at[slot], sems.at[2 + slot], self.spare)
                added = transit[slot].astype(WIDE) + part[aligned(far * size, size), :].astype(WIDE)
                transit[slot] = added.astype(LOW)

            self.post.send(transit.at[slot], landing.at[1], sems.at[1], self.place(far), self.inner)

    def total(self, landing, sems):
        arrived(self.spot, landing.at[0], sems.at[0], self.spare)
        arrived(self.spot, landing.at[1], sems.at[1], self.spare)
        return landing[0].astype(WIDE) + landing[1].astype(WIDE) + landing[2].astype(WIDE)


def row_scale(values):
    return lax.rsqrt(jnp.mean(values * values, axis=-1, keepdims=True) + EPSILON)


def norm_back(grad, gain, normal, factor):
    weighted = grad * gain
    return factor * (weighted - normal * jnp.mean(weighted * normal, axis=-1, keepdims=True))


def layer_kernel(
    tok_ref, cot_ref, again_ref, mgain_ref, qgain_ref, kgain_ref,
    rope_hbm, wout_hbm, wg_hbm, wu_hbm, wd_hbm, wq_hbm, wk_hbm, wv_hbm, order_ref, docs_ref,
    layer_out, in_grad, g_query, g_key, g_value, g_out, vec_out, gain_out, g_gate, g_up, g_down,
    tok_all, own_stats, factors, lse, att_recv,
    wout, wgate, wup, wdown, q_pair, kv_nat, hat, rope_ref,
    hidden, hid_own, gate_pre, up_pre, mix_turned, att_turned, down_own, gu_own, proj_own, ag_own, vec_own,
    hid_all, down_all, proj_all, gu_all, mix_all, att_all, vec_all, vec_far,
    down_land, down_transit, wout_land, gu_land, gu_transit,
    ag_recv, ag_pair, k_turned, stat_all, grad_nat, grad_recv, part_sib, part_far, wqkv_recv, gain_own, gain_recv,
    inverse_ref, send_sems, recv_sems, own_sems, att_sems,
    local_sems, post_sems, hid_sems, dpl_sems, proj_sems, attp_sems, mix_sems, gup_sems,
    vec_sems, down_sems, wout_sems, gu_sems, gut_sems, ag_sems, stat_sems, grad_sems, sib_sem, wqkv_sems, gain_sems,
):
    spot = Spot()
    devices, chips = 16, 8
    dp, seq, core, chip, z = spot.dp, spot.seq, spot.core, spot.chip, spot.z
    me = dp * devices + seq
    member = dp * 4 + spot.x * 2 + core
    spare = post_sems.at[0]
    post = Post(post_sems)
    along = AlongZ(spot, post, spare)

    def load(source, target, index):
        copy = pltpu.make_async_copy(source, target, local_sems.at[index])
        copy.start()
        return copy

    barrier = pltpu.get_barrier_semaphore()
    for step in range(1, 2 * devices):
        other = (me + step) % (2 * devices)
        pl.semaphore_signal(barrier, inc=1, device_id=(other // devices, other % devices), device_id_type=MESH)
    load_query = load(wq_hbm, wgate.at[:, pl.ds(0, 2048)], 1)
    load_key = load(wk_hbm, wgate.at[:, pl.ds(2048, 1024)], 2)
    load_value = load(wv_hbm.at[:, aligned(chip * 128, 128)], wup.at[:, pl.ds(0, 128)], 4)
    load_rope = load(rope_hbm, rope_ref, 5)
    load_out = load(wout_hbm, wout, 0)
    load_down = load(wd_hbm, wdown, 3)
    invert(order_ref, inverse_ref)
    pl.semaphore_wait(barrier, 2 * devices - 1)
    gather = RowGather(spot, tok_ref, tok_all, local_sems.at[8], send_sems, recv_sems)
    gather.start()

    load_query.wait()
    load_key.wait()
    own = tok_ref[...].reshape(128, tok_ref.shape[-1])
    sums = []
    for start, stop in ((0, 2048), (2048, 3072)):
        parts = [dot(own, wgate[:, first : first + 512]) for first in range(start, stop, 512)]
        sums.append(sum(jnp.sum(part * part, axis=-1, keepdims=True) for part in parts) / (stop - start))
    own_stats[pl.ds(seq, 1)] = lax.rsqrt(rows_of(sums[0], sums[1]) + EPSILON)[None]
    for step in range(1, devices):
        post.send(own_stats.at[seq], own_stats.at[seq], own_sems.at[seq], (dp, (seq + step) % devices))
    gather.forward()
    for step in range(1, devices):
        other = (seq + step) % devices
        arrived(spot, own_stats.at[other], own_sems.at[other], spare)
    gather.finish()

    first_length = docs_ref[core, 0, 0]
    load_value.wait()
    for part in range(4):
        rows = pl.ds(part * CHUNK, CHUNK)
        chunk = jnp.concatenate([tok_all[inverse_ref[part * 4 + piece]] for piece in range(4)], axis=0)
        hat[rows, :256] = dot(chunk, wgate[:, aligned(chip * 256, 256)])
        hat[rows, 256:] = dot(chunk, wgate[:, pl.ds(pl.multiple_of(2048 + chip * 128, 128), 128)])
        kv_nat[rows, 128:] = dot(chunk, wup[:, :128]).astype(LOW)
    load_gate = load(wg_hbm, wgate, 1)
    load_up = load(wu_hbm, wup, 7)
    for block in range(16):
        both = own_stats[inverse_ref[block]]
        both = jnp.where(core == 0, both, pltpu.roll(both, 64, axis=1))
        factors[:, block * 64 : (block + 1) * 64] = both[:, :64]
    load_rope.wait()
    qgain = qgain_ref[pl.ds(chip * 2, 2), :]
    kgain = kgain_ref[pl.ds(chip, 1), :]
    for part in range(8):
        rows = pl.ds(part * TILE, TILE)
        scale = columns_of(factors[:, rows])
        cos, sine = rope_part(rope_ref, part, first_length)
        for head in range(3):
            lanes = pl.ds(head * HD, HD)
            column = scale[:, 0:1] if head < 2 else scale[:, 1:2]
            gain = qgain[head : head + 1] if head < 2 else kgain
            normal = hat[rows, lanes] * column
            hat[rows, lanes] = normal
            normed = normal * gain
            turned = (normed * cos + swap_halves(normed) * sine).astype(LOW)
            if head < 2:
                q_pair[part, pl.ds(head * HD, HD), :] = turned
            else:
                kv_nat[rows, :HD] = turned
    k_turned[...] = kv_nat[:, HD:].T
    for tile in range(8):
        count = (tile + 1) * TILE
        scores = dot_nt(kv_nat[:count, :HD], q_pair[tile]) * HD ** (-0.5)
        masked = jnp.where(allowed_places(tile, count, first_length), scores, MASK_FILL)
        top = jnp.max(masked, axis=0, keepdims=True)
        terms = jnp.exp(masked - top)
        weight = jnp.sum(terms, axis=0, keepdims=True)
        lse[pl.ds(tile, 1), :] = top + jnp.log(weight)
        turned = dot(k_turned[:, :count], terms.astype(LOW)) / weight
        attended = turned.T.astype(LOW)
        grad_nat[pl.ds(tile * 2, 2), :, :HD] = attended[:TILE].reshape(2, 64, HD)
        grad_nat[pl.ds(tile * 2, 2), :, HD : 2 * HD] = attended[TILE:].reshape(2, 64, HD)
    att_recv[pl.ds(chip, 1), pl.ds(core, 1)] = grad_nat[order_ref[seq], :, : 2 * HD][None, None]
    for step in range(1, devices):
        other = (seq + step) % devices
        slot = (step % 2, slice(None), slice((step // 2) * 256, (step // 2 + 1) * 256))
        ag_own[slot] = grad_nat[order_ref[other], :, : 2 * HD]
        post.send(ag_own.at[slot], att_recv.at[chip, core], att_sems.at[seq], (dp, other))
    for step in range(1, devices):
        other = (seq + step) % devices
        arrived(spot, att_recv.at[other // 2, other % 2], att_sems.at[other], spare)
    post.finish()

    for group in range(8):
        attended = att_recv[group]
        ag_own[:, :, group * 256 : (group + 1) * 256] = attended
        block = attended.reshape(128, 256).T
        for piece in range(4):
            att_turned[(group // 4) * 4 + piece, pl.ds((group % 4) * 64, 64), :] = block[piece * 64 : (piece + 1) * 64]
    x_place, y_place, sib_place = (dp, spot.flip_x), (1 - dp, seq), (dp, spot.sibling)
    x_member = dp * 4 + (1 - spot.x) * 2 + core
    y_member = (1 - dp) * 4 + spot.x * 2 + core
    diagonal = (1 - dp) * 4 + (1 - spot.x) * 2 + core
    keeps = {}

    def spread(own, held, sems, index):
        keeps[index] = load(own, held.at[member], index)
        for place in (x_place, y_place, sib_place):
            post.send(own, held.at[member], sems.at[member], place)

    def pass_on(held, sems, across):
        turn = (x_member, y_place) if across == "y" else (y_member, x_place)
        straight = y_member if across == "y" else x_member
        for other, places in ((turn[0], (turn[1], sib_place)), (straight, (sib_place,))):
            arrived(spot, held.at[other], sems.at[other], spare)
            for place in places:
                post.send(held.at[other], held.at[other], sems.at[other], place)

    def pass_diagonal(held, sems):
        arrived(spot, held.at[diagonal], sems.at[diagonal], spare)
        post.send(held.at[diagonal], held.at[diagonal], sems.at[diagonal], sib_place)

    def whole(held, sems, index):
        keeps[index].wait()
        for y in range(2):
            for x in range(2):
                other = y * 4 + x * 2 + 1 - core
                arrived(spot, held.at[other], sems.at[other], spare)

    def deal(own, held, sems, index):
        keeps[index] = load(own.at[member], held.at[member], index)
        for step in range(1, 8):
            other = (member + step) % 8
            post.send(own.at[other], held.at[member], sems.at[member], (other // 4, z * 4 + other % 4))

    def dealt(held, sems, index):
        keeps[index].wait()
        for step in range(1, 8):
            other = (member + step) % 8
            arrived(spot, held.at[other], sems.at[other], spare)

    deal(att_turned, att_all, attp_sems, 10)
    load_out.wait()
    attn_proj = dot(ag_own[...].reshape(128, 2048), wout[...])
    att_factor = row_scale(attn_proj)
    normal = attn_proj * att_factor
    in_grad[...] = normal
    stream = tok_ref[...].reshape(128, 1024).astype(WIDE) + normal * again_ref[...]
    hidden[...] = stream
    hid_own[...] = stream.astype(LOW)
    spread(hid_own, hid_all, hid_sems, 9)

    load_gate.wait()
    load_up.wait()
    for group in range(8):
        lanes = slice(group * 384, (group + 1) * 384)
        gate = dot(hid_own[...], wgate[:, lanes])
        up = dot(hid_own[...], wup[:, lanes])
        gate_pre[group] = gate
        up_pre[group] = up
        block = (gate * jax.nn.sigmoid(gate) * up).astype(LOW)
        gu_own[group, :, :384] = block
        turned = block.T
        for piece in range(4):
            mix_turned[(group // 4) * 4 + piece, pl.ds((group % 4) * 96, 96), :] = turned[piece * 96 : (piece + 1) * 96]
    deal(mix_turned, mix_all, mix_sems, 11)
    pass_on(hid_all, hid_sems, "y")
    load_down.wait()
    down_pre = jnp.zeros((128, 1024), WIDE)
    for group in range(8):
        down_pre = down_pre + dot(gu_own[group, :, :384], wdown[group * 384 : (group + 1) * 384, :])
    factor = row_scale(down_pre)
    normal = down_pre * factor
    cot = cot_ref[...].reshape(128, 1024).astype(WIDE)
    layer_out[...] = (hidden[...] + normal * mgain_ref[...]).astype(LOW)
    down_own[...] = norm_back(cot, mgain_ref[...], normal, factor).astype(LOW)
    mlp_sum = jnp.sum(cot * normal, axis=0, keepdims=True)
    for piece in range(4):
        vec_own[4 + piece : 5 + piece, :] = mlp_sum[:, piece * 256 : (piece + 1) * 256]
    spread(down_own, down_all, dpl_sems, 12)

    for step in range(1, 9):
        group = (member + step) % 8
        grad = dot_nt(down_own[...], wdown[aligned(group * 384, 384), :])
        gate, up = gate_pre[group], up_pre[group]
        sigmoid = jax.nn.sigmoid(gate)
        gu_own[group, :, :384] = (grad * up * sigmoid * (1.0 + gate * (1.0 - sigmoid))).astype(LOW)
        gu_own[group, :, 384:] = (grad * gate * sigmoid).astype(LOW)
    hgrad = cot
    for group in range(8):
        lanes = slice(group * 384, (group + 1) * 384)
        hgrad = hgrad + dot_nt(gu_own[group, :, :384], wgate[:, lanes]) + dot_nt(gu_own[group, :, 384:], wup[:, lanes])
    hidden[...] = hgrad
    normal = in_grad[...]
    proj_own[...] = norm_back(hgrad, again_ref[...], normal, att_factor).astype(LOW)
    attn_sum = jnp.sum(hgrad * normal, axis=0, keepdims=True)
    for piece in range(4):
        vec_own[piece : piece + 1, :] = attn_sum[:, piece * 256 : (piece + 1) * 256]
    load_query = load(wq_hbm, wgate.at[:, pl.ds(0, 2048)], 1)
    load_key = load(wk_hbm, wgate.at[:, pl.ds(2048, 1024)], 2)
    load_value = load(wv_hbm, wup.at[:, pl.ds(0, 1024)], 3)

    att_grad = dot_nt(proj_own[...], wout[...]).astype(LOW)
    ag_own[...] = att_grad.reshape(2, 64, 2048)
    keep_ag = load(ag_own.at[core, :, aligned(chip * 256, 256)], ag_recv.at[seq], 14)
    for step in range(1, devices):
        other = (seq + step) % devices
        post.send(
            ag_own.at[other % 2, :, aligned((other // 2) * 256, 256)], ag_recv.at[seq], ag_sems.at[seq], (dp, other)
        )
    keep_vec = load(vec_own, vec_all.at[member], 16)
    for step in range(1, 8):
        other = (member + step) % 8
        post.send(vec_own, vec_all.at[member], vec_sems.at[member], (other // 4, z * 4 + other % 4))
    pass_diagonal(hid_all, hid_sems)
    pass_on(down_all, dpl_sems, "x")
    spread(proj_own, proj_all, proj_sems, 15)
    deal(gu_own, gu_all, gup_sems, 13)
    keep_ag.wait()
    for step in range(1, devices):
        other = (seq + step) % devices
        arrived(spot, ag_recv.at[other], ag_sems.at[other], spare)
    for tile in range(8):
        block = jnp.concatenate([ag_recv[inverse_ref[tile * 2 + piece]] for piece in range(2)], axis=0)
        ag_pair[tile, :TILE, :] = block[:, :HD]
        ag_pair[tile, TILE:, :] = block[:, HD:]
    k_turned[...] = kv_nat[:, :HD].T
    up_pre[:, :, :256] = jnp.zeros((8, TILE, 256), WIDE)
    down_part = wdown.at[pl.ds(0, 384)]
    for tile in range(7, -1, -1):
        if tile == 4:
            pass_diagonal(down_all, dpl_sems)
            dealt(mix_all, mix_sems, 11)
            whole(down_all, dpl_sems, 12)
            mixes = jnp.concatenate([mix_all[other] for other in range(8)], axis=1)
            down_part[...] = dot(mixes, down_all[...].reshape(1024, 1024)).astype(LOW)
            along.send(down_part, 96, down_land, down_transit, down_sems)
        count = (tile + 1) * TILE
        queries, grads = q_pair[tile], ag_pair[tile]
        scores = dot_nt(kv_nat[:count, :HD], queries) * HD ** (-0.5)
        masked = jnp.where(allowed_places(tile, count, first_length), scores, MASK_FILL)
        probs = jnp.exp(masked - lse[tile : tile + 1, :])
        prob_grad = dot_nt(kv_nat[:count, HD:], grads)
        row_dot = jnp.sum(probs * prob_grad, axis=0, keepdims=True)
        score_grad = (probs * (prob_grad - row_dot)).astype(LOW)
        up_pre[: tile + 1, :, :HD] += dot(score_grad, queries).reshape(tile + 1, TILE, HD)
        up_pre[: tile + 1, :, HD:256] += dot(probs.astype(LOW), grads).reshape(tile + 1, TILE, HD)
        turned = (dot(k_turned[:, :count], score_grad) * HD ** (-0.5)).T
        gate_pre[tile, :, :HD] = turned[:TILE]
        gate_pre[tile, :, HD:256] = turned[TILE:]

    pass_on(proj_all, proj_sems, "y")
    keep_vec.wait()
    for step in range(1, 8):
        other = (member + step) % 8
        arrived(spot, vec_all.at[other], vec_sems.at[other], spare)
    vec = vec_all[0]
    for other in range(1, 8):
        vec = vec + vec_all[other]
    vec_far[pl.ds(z, 1)] = vec[None]
    for far in spot.far_z:
        post.send(vec_far.at[z], vec_far.at[z], vec_sems.at[8 + z], along.place(far))

    gains = [jnp.zeros((1, HD), WIDE) for _ in range(3)]
    for part in range(8):
        rows = pl.ds(part * TILE, TILE)
        cos, sine = rope_part(rope_ref, part, first_length)
        dots = []
        for head in range(3):
            lanes = slice(head * HD, (head + 1) * HD)
            turned = gate_pre[part, :, lanes] if head < 2 else up_pre[part, :, :HD] * HD ** (-0.5)
            back = turned * cos - swap_halves(turned) * sine
            normal = hat[rows, lanes]
            gain = qgain[head : head + 1] if head < 2 else kgain
            gains[head] = gains[head] + jnp.sum(back * normal, axis=0, keepdims=True)
            weighted = back * gain
            if head < 2:
                gate_pre[part, :, lanes] = weighted
            else:
                up_pre[part, :, :HD] = weighted
            dots.append(jnp.sum(weighted * normal, axis=-1, keepdims=True))
        stat_all[pl.ds(chip, 1), :, rows] = rows_of(dots[0] + dots[1], dots[2])[None]
    for step in range(1, chips):
        other = (chip + step) % chips
        post.send(stat_all.at[chip], stat_all.at[chip], stat_sems.at[chip], (dp, other * 2 + core))
    gain_own[...] = jnp.concatenate([jnp.broadcast_to(gain, (8, HD)) for gain in gains], axis=1)
    for piece in range(4):
        target = chip * 4 + piece
        slot = gain_recv.at[dp * 2 + core]

        @pl.when(target == me)
        def _():
            gain_recv[pl.ds(dp * 2 + core, 1)] = gain_own[...][None]

        post.send(gain_own, slot, gain_sems.at[dp * 2 + core], (target // devices, target % devices), target != me)

    along.combine(down_part, 96, down_land, down_transit, down_sems)
    for step in range(1, chips):
        other = (chip + step) % chips
        arrived(spot, stat_all.at[other], stat_sems.at[other], spare)
    total = stat_all[0]
    for other in range(1, chips):
        total = total + stat_all[other]
    width = jnp.where(lax.broadcasted_iota(jnp.int32, total.shape, 0) == 0, 1.0 / 2048, 1.0 / 1024)
    means = total * width
    grad_send = wdown.at[pl.ds(1024, 1024), pl.ds(512, 512)]
    for part in range(8):
        rows = pl.ds(part * TILE, TILE)
        mean = columns_of(means[:, part * TILE : (part + 1) * TILE])
        scale = columns_of(factors[:, rows])
        for head in range(3):
            column = 0 if head < 2 else 1
            weighted = gate_pre[part, :, head * HD : (head + 1) * HD] if head < 2 else up_pre[part, :, :HD]
            normal = hat[rows, pl.ds(head * HD, HD)]
            grad = scale[:, column : column + 1] * (weighted - normal * mean[:, column : column + 1])
            grad_nat[pl.ds(part * 2, 2), :, head * HD : (head + 1) * HD] = grad.astype(LOW).reshape(2, 64, HD)
        grad_nat[pl.ds(part * 2, 2), :, 3 * HD :] = up_pre[part, :, HD:256].astype(LOW).reshape(2, 64, HD)
    for step in range(devices):
        other = (seq + step) % devices
        rows = aligned(other * 64, 64)
        block = grad_nat[order_ref[other]]
        grad_send[rows, :] = block
        if step > 0:
            post.send(grad_send.at[rows], grad_recv.at[chip, core], grad_sems.at[seq], (dp, other))
        else:
            grad_recv[pl.ds(chip, 1), pl.ds(core, 1)] = block[None, None]

    part_low = wdown.at[pl.ds(2048, 1024), pl.ds(0, 512)]
    for first in range(0, 1024, 256):
        part = dot_tn(tok_all[:, :, first : first + 256].reshape(1024, 256), grad_send[...])
        part_low[first : first + 256, :] = part.astype(LOW)
    post.send(part_low.at[aligned((1 - core) * 512, 512)], part_sib, sib_sem.at[0], sib_place)

    dealt(gu_all, gup_sems, 13)
    whole(hid_all, hid_sems, 9)
    gu_part = wout.at[pl.ds(1024, 1024), pl.ds(0, 768)]
    for first in range(0, 1024, 256):
        part = dot_tn(hid_all[:, :, first : first + 256].reshape(1024, 256), gu_all[...].reshape(1024, 768))
        gu_part[first : first + 256, :] = part.astype(LOW)
    for y in range(2):
        for slot, far in enumerate((along.far_inner, along.far_outer)):
            post.send(
                gu_part.at[aligned(y * 512 + far * 128, 128)], gu_transit.at[slot, y], gut_sems.at[slot, y],
                along.place(along.partner), along.outer,
            )
    arrived(spot, part_sib, sib_sem.at[0], spare)
    part_sum = wdown.at[pl.ds(2048, 512), pl.ds(512, 512)]
    part_sum[...] = (part_low[aligned(core * 512, 512), :].astype(WIDE) + part_sib[...].astype(WIDE)).astype(LOW)
    post.send(part_sum.at[aligned((1 - dp) * 256, 256)], part_far, sib_sem.at[1], y_place)
    for step in range(8):
        other = (member + step) % 8
        first = (other // 4) * 512 + (other % 4) * 32
        post.send(
            gu_part.at[aligned(first + along.partner * 128, 32)], gu_land.at[0, member], gu_sems.at[0, member],
            (other // 4, along.partner * 4 + other % 4),
        )
        if step > 0:
            post.send(
                gu_part.at[aligned(first + z * 128, 32)], gu_land.at[2, member], gu_sems.at[2, member],
                (other // 4, z * 4 + other % 4),
            )
    gu_land[2, pl.ds(member, 1)] = gu_part[aligned((member // 4) * 512 + z * 128 + (member % 4) * 32, 32), :][None]

    arrived(spot, part_far, sib_sem.at[1], spare)
    part_end = wdown.at[pl.ds(2560, 256), pl.ds(512, 512)]
    part_end[...] = (part_sum[aligned(dp * 256, 256), :].astype(WIDE) + part_far[...].astype(WIDE)).astype(LOW)
    for step in range(8):
        slot = (seq + step) % 8
        other = dp * 8 + slot
        rows = aligned(slot * 32, 32)

        @pl.when((core == dp) & (other == seq))
        def _():
            wqkv_recv[pl.ds(chip, 1)] = part_end[rows, :][None]

        post.send(
            part_end.at[rows], wqkv_recv.at[chip], wqkv_sems.at[chip], (core, other),
            (core != dp) | (other != seq),
        )

    pass_diagonal(proj_all, proj_sems)
    dealt(att_all, attp_sems, 10)
    whole(proj_all, proj_sems, 15)
    turned = jnp.concatenate([att_all[other] for other in range(8)], axis=1)
    wout_part = wdown.at[pl.ds(384, 256)]
    wout_part[...] = dot(turned, proj_all[...].reshape(1024, 1024)).astype(LOW)
    wout_land[pl.ds(z, 1)] = wout_part[aligned(z * 64, 64), :][None]
    for far in spot.far_z:
        post.send(wout_part.at[aligned(far * 64, 64)], wout_land.at[z], wout_sems.at[z], along.place(far))
    for step in range(1, devices):
        other = (seq + step) % devices
        arrived(spot, grad_recv.at[other // 2, other % 2], grad_sems.at[other], spare)
    load_query.wait()
    load_key.wait()
    load_value.wait()
    grad_k, grad_v = [], []
    gradient = hidden[...]
    for piece in range(chips):
        block = grad_recv[piece].reshape(128, 512)
        gradient = gradient + dot_nt(block[:, :256], wgate[:, piece * 256 : (piece + 1) * 256])
        grad_k.append(block[:, 256:384])
        grad_v.append(block[:, 384:])
    gradient = gradient + dot_nt(jnp.concatenate(grad_k, axis=1), wgate[:, 2048:])
    in_grad[...] = gradient + dot_nt(jnp.concatenate(grad_v, axis=1), wup[:, :1024])

    for slot, far in enumerate((along.far_inner, along.far_outer)):
        for y in range(2):

            @pl.when(along.inner)
            def _():
                arrived(spot, gu_transit.at[slot, y], gut_sems.at[slot, y], spare)
                added = gu_transit[slot, y].astype(WIDE) + gu_part[aligned(y * 512 + far * 128, 128), :].astype(WIDE)
                gu_transit[slot, y] = added.astype(LOW)

            for piece in range(4):
                post.send(
                    gu_transit.at[slot, y, pl.ds(piece * 32, 32)], gu_land.at[1, member], gu_sems.at[1, member],
                    (y, far * 4 + piece), along.inner,
                )

    for y in range(2):
        for micro in range(2):
            source = y * 2 + micro
            sender = y * devices + (me // 4) * 2 + micro

            @pl.when(sender != me)
            def _():
                arrived(spot, gain_recv.at[source], gain_sems.at[source], spare)

    gain_out[...] = sum(gain_recv[source] for source in range(4))
    for source in range(chips):
        sender = (seq // 8) * devices + source * 2 + dp

        @pl.when(sender != me)
        def _():
            arrived(spot, wqkv_recv.at[source], wqkv_sems.at[source], spare)

    for piece in range(chips):
        block = wqkv_recv[piece].astype(WIDE)
        g_query[:, piece * 256 : (piece + 1) * 256] = block[:, :256]
        g_key[:, piece * 128 : (piece + 1) * 128] = block[:, 256:384]
        g_value[:, piece * 128 : (piece + 1) * 128] = block[:, 384:]
    for far in spot.far_z:
        arrived(spot, vec_far.at[far], vec_sems.at[8 + far], spare)
    vec_out[...] = sum(vec_far[far] for far in range(4))
    g_down[...] = along.total(down_land, down_sems)
    for step in range(8):
        other = (member + step) % 8
        for kind in range(3):
            if kind < 2 or step > 0:
                arrived(spot, gu_land.at[kind, other], gu_sems.at[kind, other], spare)
    for slot in range(8):
        block = sum(gu_land[kind, slot].astype(WIDE) for kind in range(3))
        g_gate[:, slot * 384 : (slot + 1) * 384] = block[:, :384]
        g_up[:, slot * 384 : (slot + 1) * 384] = block[:, 384:]
    for far in spot.far_z:
        arrived(spot, wout_land.at[far], wout_sems.at[far], spare)
    g_out[...] = sum(wout_land[far].astype(WIDE) for far in range(4))
    post.finish()
    gather.drain()


POST_SENDS = 256


def whole_layer(*operands):
    length, width = 1024, 1024
    any_spec = pl.BlockSpec(memory_space=pl.ANY)
    vmem = pl.BlockSpec(memory_space=pltpu.VMEM)
    smem = pl.BlockSpec(memory_space=pltpu.SMEM)
    shape = jax.ShapeDtypeStruct
    dma = pltpu.SemaphoreType.DMA
    return pl.pallas_call(
        layer_kernel,
        out_shape=(
            shape((128, width), LOW),
            shape((128, width), WIDE),
            shape((32, 2048), WIDE),
            shape((32, 1024), WIDE),
            shape((32, 1024), WIDE),
            shape((64, 1024), WIDE),
            shape((8, 256), WIDE),
            shape((8, 384), WIDE),
            shape((32, 3072), WIDE),
            shape((32, 3072), WIDE),
            shape((96, 1024), WIDE),
        ),
        in_specs=[vmem] * 6 + [any_spec] * 8 + [smem] * 2,
        out_specs=(vmem,) * 11,
        scratch_shapes=[
            pltpu.VMEM((16, 64, width), LOW),
            pltpu.VMEM((16, 8, HD), WIDE),
            pltpu.VMEM((8, length), WIDE),
            pltpu.VMEM((8, 2 * TILE), WIDE),
            pltpu.VMEM((8, 2, 64, 2 * HD), LOW),
            pltpu.VMEM((2048, width), LOW),
            pltpu.VMEM((width, 3072), LOW),
            pltpu.VMEM((width, 3072), LOW),
            pltpu.VMEM((3072, width), LOW),
            pltpu.VMEM((8, 2 * TILE, HD), LOW),
            pltpu.VMEM((length, 2 * HD), LOW),
            pltpu.VMEM((length, 3 * HD), WIDE),
            pltpu.VMEM((length + 64, HD), WIDE),
            pltpu.VMEM((128, width), WIDE),
            pltpu.VMEM((128, width), LOW),
            pltpu.VMEM((8, 128, 384), WIDE),
            pltpu.VMEM((8, 128, 384), WIDE),
            pltpu.VMEM((8, 384, 128), LOW),
            pltpu.VMEM((8, 256, 128), LOW),
            pltpu.VMEM((128, width), LOW),
            pltpu.VMEM((8, 128, 768), LOW),
            pltpu.VMEM((128, width), LOW),
            pltpu.VMEM((2, 64, 2048), LOW),
            pltpu.VMEM((8, 256), WIDE),
            pltpu.VMEM((8, 128, width), LOW),
            pltpu.VMEM((8, 128, width), LOW),
            pltpu.VMEM((8, 128, width), LOW),
            pltpu.VMEM((8, 128, 768), LOW),
            pltpu.VMEM((8, 384, 128), LOW),
            pltpu.VMEM((8, 256, 128), LOW),
            pltpu.VMEM((8, 8, 256), WIDE),
            pltpu.VMEM((4, 8, 256), WIDE),
            pltpu.VMEM((3, 96, width), LOW),
            pltpu.VMEM((2, 96, width), LOW),
            pltpu.VMEM((4, 64, width), LOW),
            pltpu.VMEM((3, 8, 32, 768), LOW),
            pltpu.VMEM((2, 2, 128, 768), LOW),
            pltpu.VMEM((16, 64, 256), LOW),
            pltpu.VMEM((8, 2 * TILE, HD), LOW),
            pltpu.VMEM((HD, length), LOW),
            pltpu.VMEM((8, 8, length), WIDE),
            pltpu.VMEM((16, 64, 512), LOW),
            pltpu.VMEM((8, 2, 64, 512), LOW),
            pltpu.VMEM((512, 512), LOW),
            pltpu.VMEM((256, 512), LOW),
            pltpu.VMEM((8, 32, 512), LOW),
            pltpu.VMEM((8, 384), WIDE),
            pltpu.VMEM((4, 8, 384), WIDE),
            pltpu.SMEM((16,), jnp.int32),
            dma((GATHER_SENDS,)),
            dma((GATHER_RECVS,)),
            dma((16,)),
            dma((16,)),
            dma((17,)),
            dma((POST_SENDS,)),
            dma((8,)),
            dma((8,)),
            dma((8,)),
            dma((8,)),
            dma((8,)),
            dma((8,)),
            dma((12,)),
            dma((4,)),
            dma((4,)),
            dma((3, 8)),
            dma((2, 2)),
            dma((16,)),
            dma((8,)),
            dma((16,)),
            dma((2,)),
            dma((16,)),
            dma((4,)),
        ],
        compiler_params=pltpu.CompilerParams(
            collective_id=0, has_side_effects=True, vmem_limit_bytes=63 * 2**20
        ),
        name="whole_layer",
    )(*operands)


def rope_constant(length):
    frequency = np.power(np.float32(ROPE_BASE), -np.arange(0, HD, 2).astype(np.float32) / np.float32(HD)).astype(np.float32)
    angles = (np.arange(length, dtype=np.float32)[:, None] * frequency[None, :]).astype(np.float32).astype(np.float64)
    table = np.concatenate([np.cos(angles), np.sin(angles)], axis=1)
    return jnp.asarray(np.concatenate([np.zeros((64, HD)), table], axis=0), WIDE)


def finish_kernel(*refs):
    count = 9
    sources, vec_ref, gain_ref = refs[:count], refs[count], refs[count + 1]
    targets, small = refs[count + 2 : 2 * count + 2], refs[2 * count + 2 :]
    for source, target in zip(sources, targets):
        target[...] = source[...]
    seq = lax.axis_index("seq")
    me = lax.axis_index("dp") * 16 + seq
    part = seq % 4
    gains = gain_ref[...]
    q_out, k_out, attn_out, mlp_out = small
    q_all = pltpu.roll(gains[:, :256], (256 - part * 64) % 256, axis=1)
    k_all = pltpu.roll(gains[:, 256:], (128 - part * 32) % 128, axis=1)
    turn = (256 - (me % 8) * 32) % 256
    attn_all = pltpu.roll(jnp.broadcast_to(vec_ref[pl.ds(me // 8, 1), :], (8, 256)), turn, axis=1)
    mlp_all = pltpu.roll(jnp.broadcast_to(vec_ref[pl.ds(4 + me // 8, 1), :], (8, 256)), turn, axis=1)
    q_out[...] = q_all[0:1, :64]
    k_out[...] = k_all[0:1, :32]
    attn_out[...] = attn_all[0:1, :32]
    mlp_out[...] = mlp_all[0:1, :32]


def finish(arrays, vec, gains):
    vmem = pl.BlockSpec(memory_space=pltpu.VMEM)
    shape = jax.ShapeDtypeStruct
    count = len(arrays)
    return pl.pallas_call(
        finish_kernel,
        out_shape=tuple(shape(a.shape, a.dtype) for a in arrays)
        + (shape((1, 64), WIDE), shape((1, 32), WIDE), shape((1, 32), WIDE), shape((1, 32), WIDE)),
        in_specs=[vmem] * (count + 2),
        out_specs=(vmem,) * (count + 4),
        name="finish",
    )(*arrays, vec, gains)


def rms_forward(inputs, gain_vec):
    factor = lax.rsqrt(jnp.mean(inputs * inputs, axis=-1, keepdims=True) + EPSILON)
    normal = inputs * factor
    return (normal * gain_vec, normal, factor)


def rms_backward(grad_in, gain_vec, normal, factor):
    weighted = grad_in * gain_vec
    gain_grad = jnp.sum(grad_in * normal, axis=0)
    inner_mean = jnp.mean(weighted * normal, axis=-1, keepdims=True)
    return (factor * (weighted - normal * inner_mean), gain_grad)


def rope_tables(rot_places, head_size):
    frequency = jnp.power(ROPE_BASE, -jnp.arange(0, head_size, 2).astype(jnp.float32) / head_size)
    angles = rot_places.astype(jnp.float32)[:, None] * frequency[None, :]
    return (jnp.cos(angles), jnp.sin(angles))


def rotate(inputs, cos_table, sine_table, head_count, direction):
    row_count = inputs.shape[0]
    halves = inputs.reshape(row_count, head_count, 2, -1)
    first_half = halves[:, :, 0]
    second = halves[:, :, 1]
    cos_part = cos_table[:, None, :]
    sine_part = sine_table[:, None, :] * direction
    turned = jnp.stack(
        [first_half * cos_part - second * sine_part, second * cos_part + first_half * sine_part],
        axis=2,
    )
    return turned.reshape(row_count, -1)


def product(left, right):
    return jnp.dot(left, right, preferred_element_type=jnp.float32)


def weight_grad(left, right):
    return lax.dot_general(
        left, right, (((0,), (0,)), ((), ())), preferred_element_type=jnp.float32
    )


def back_product(left, right):
    return lax.dot_general(
        left, right, (((1,), (1,)), ((), ())), preferred_element_type=jnp.float32
    )


def heads_first(rows, group_count, head_size):
    shaped = rows.reshape(rows.shape[0], group_count, -1, head_size)
    return jnp.moveaxis(shaped, 1, 0)


def kv_first(rows, group_count, head_size):
    return jnp.moveaxis(rows.reshape(rows.shape[0], group_count, head_size), 1, 0)


def score_block(q_group, k_group, mask_rows, score_scale):
    raw_scores = (
        jnp.einsum("trd,ud->rtu", q_group, k_group, preferred_element_type=jnp.float32)
        * score_scale
    )
    return jnp.where(mask_rows[None], raw_scores, MASK_FILL)


def attend(pieces, score_scale, group_count, head_size):
    q_rows, key_rows, value_rows, mask_rows = pieces

    def attend_one_group(parts):
        q_group, k_group, v_group = parts
        masked = score_block(q_group, k_group, mask_rows, score_scale)
        row_max = jnp.max(masked, axis=-1)
        exp_terms = jnp.exp(masked - row_max[..., None])
        row_sum = jnp.sum(exp_terms, axis=-1)
        attn_prob = (exp_terms / row_sum[..., None]).astype(jnp.bfloat16)
        attended = jnp.einsum("rtu,ud->trd", attn_prob, v_group, preferred_element_type=jnp.float32)
        return (attended, row_max, row_sum)

    attended, row_max, row_sum = lax.map(
        attend_one_group,
        (
            heads_first(q_rows, group_count, head_size),
            kv_first(key_rows, group_count, head_size),
            kv_first(value_rows, group_count, head_size),
        ),
    )
    attended = jnp.moveaxis(attended, 0, 1)
    return (attended.reshape(q_rows.shape[0], -1), row_max, row_sum)


def score_grads(
    q_group, grad_group, k_group, v_group, mask_rows, row_max, row_sum, row_dot, score_scale
):
    masked = score_block(q_group, k_group, mask_rows, score_scale)
    attn_prob = jnp.exp(masked - row_max[..., None]) / row_sum[..., None]
    prob_grad = jnp.einsum("trd,ud->rtu", grad_group, v_group, preferred_element_type=jnp.float32)
    row_dot = jnp.sum(attn_prob * prob_grad, axis=-1)
    score_grad = (attn_prob * (prob_grad - row_dot[..., None])).astype(jnp.bfloat16)
    return (attn_prob.astype(jnp.bfloat16), score_grad, row_dot)


def on_device(
    tokens,
    cotangent,
    w_query,
    w_key,
    w_value,
    w_out,
    q_gain,
    k_gain,
    attn_gain,
    w_gate,
    w_up,
    w_down,
    mlp_gain,
    doc_lengths,
    block_order,
):
    micro_count = tokens.shape[0]
    block_len = tokens.shape[2]
    model_width = tokens.shape[3]
    seq_length = lax.axis_size("seq") * block_len
    head_count = w_query.shape[1] // HD
    group_count = w_key.shape[1] // HD
    score_scale = HD ** (-0.5)
    flat_tokens = tokens.reshape(micro_count * block_len, model_width)
    out_grad = cotangent.reshape(micro_count * block_len, model_width).astype(jnp.float32)
    first_lengths = doc_lengths[:, 0, 0]
    offsets = jnp.arange(block_len, dtype=jnp.int32)
    own_places = block_order[lax.axis_index("seq")] * block_len + offsets
    key_places = (block_order[:, None] * block_len + offsets[None, :]).reshape(seq_length)
    own_segments = (own_places[None, :] >= first_lengths[:, None]).astype(jnp.int32)
    all_segments = (key_places[None, :] >= first_lengths[:, None]).astype(jnp.int32)
    rot_places = (own_places[None, :] - own_segments * first_lengths[:, None]).reshape(-1)
    allowed = (own_segments[:, :, None] == all_segments[:, None, :]) & (
        key_places[None, None, :] <= own_places[None, :, None]
    )
    cos_table, sine_table = rope_tables(rot_places, HD)
    q_pre = product(flat_tokens, w_query)
    k_pre = product(flat_tokens, w_key)
    v_pre = product(flat_tokens, w_value)
    q_norm, q_hat, q_factor = rms_forward(q_pre, q_gain)
    k_norm, k_hat, k_factor = rms_forward(k_pre, k_gain)
    q_low = rotate(q_norm, cos_table, sine_table, head_count, 1.0).astype(jnp.bfloat16)
    k_low = rotate(k_norm, cos_table, sine_table, group_count, 1.0).astype(jnp.bfloat16)
    v_low = v_pre.astype(jnp.bfloat16)
    q_blocks = q_low.reshape(micro_count, block_len, -1)
    k_blocks = k_low.reshape(micro_count, block_len, -1)
    v_blocks = v_low.reshape(micro_count, block_len, -1)
    key_all, value_all = (
        lax.all_gather(k_blocks, "seq", axis=1, tiled=True),
        lax.all_gather(v_blocks, "seq", axis=1, tiled=True),
    )

    def forward_block(pieces):
        return attend(pieces, score_scale, group_count, HD)

    attended, row_max, row_sum = lax.map(forward_block, (q_blocks, key_all, value_all, allowed))
    att_low = attended.reshape(micro_count * block_len, -1).astype(jnp.bfloat16)
    attn_proj = product(att_low, w_out)
    attn_normed, attn_hat, attn_factor = rms_forward(attn_proj, attn_gain)
    hidden = flat_tokens.astype(jnp.float32) + attn_normed
    hidden_low = hidden.astype(jnp.bfloat16)
    gate_pre = product(hidden_low, w_gate)
    up_pre = product(hidden_low, w_up)
    mixed_low = (jax.nn.silu(gate_pre) * up_pre).astype(jnp.bfloat16)
    down_pre = product(mixed_low, w_down)
    down_normed, down_hat, down_factor = rms_forward(down_pre, mlp_gain)
    layer_out = (hidden + down_normed).astype(jnp.bfloat16).reshape(tokens.shape)
    down_grad, grad_mlp_gain = rms_backward(out_grad, mlp_gain, down_hat, down_factor)
    down_grad = down_grad.astype(jnp.bfloat16)
    grad_w_down = weight_grad(mixed_low, down_grad)
    mixed_grad = back_product(down_grad, w_down)
    sigmoid_gate = jax.nn.sigmoid(gate_pre)
    gate_grad = (
        mixed_grad * up_pre * sigmoid_gate * (1.0 + gate_pre * (1.0 - sigmoid_gate))
    ).astype(jnp.bfloat16)
    up_grad = (mixed_grad * gate_pre * sigmoid_gate).astype(jnp.bfloat16)
    grad_w_gate = weight_grad(hidden_low, gate_grad)
    grad_w_up = weight_grad(hidden_low, up_grad)
    hidden_grad = out_grad + back_product(gate_grad, w_gate) + back_product(up_grad, w_up)
    proj_grad, grad_attn_gain = rms_backward(hidden_grad, attn_gain, attn_hat, attn_factor)
    proj_grad = proj_grad.astype(jnp.bfloat16)
    grad_w_out = weight_grad(att_low, proj_grad)
    att_grad = back_product(proj_grad, w_out).astype(jnp.bfloat16)
    grad_blocks = att_grad.reshape(micro_count, block_len, -1)
    key_back, value_back = (key_all, value_all)

    def query_pass(pieces):
        q_rows, grad_rows, key_rows, value_rows, mask_rows, max_rows, sum_rows = pieces

        def query_one_group(parts):
            q_group, grad_group, k_group, v_group, max_group, sum_group = parts
            prob_low, score_grad, unused = score_grads(
                q_group,
                grad_group,
                k_group,
                v_group,
                mask_rows,
                max_group,
                sum_group,
                None,
                score_scale,
            )
            q_grad = (
                jnp.einsum("rtu,ud->trd", score_grad, k_group, preferred_element_type=jnp.float32)
                * score_scale
            )
            key_terms = (
                jnp.einsum("rtu,trd->ud", score_grad, q_group, preferred_element_type=jnp.float32)
                * score_scale
            )
            value_terms = jnp.einsum(
                "rtu,trd->ud", prob_low, grad_group, preferred_element_type=jnp.float32
            )
            return (q_grad, key_terms, value_terms)

        q_grad, key_terms, value_terms = lax.map(
            query_one_group,
            (
                heads_first(q_rows, group_count, HD),
                heads_first(grad_rows, group_count, HD),
                kv_first(key_rows, group_count, HD),
                kv_first(value_rows, group_count, HD),
                max_rows,
                sum_rows,
            ),
        )
        q_grad = jnp.moveaxis(q_grad, 0, 1).reshape(block_len, -1)
        key_terms = jnp.moveaxis(key_terms, 0, 1).reshape(seq_length, -1)
        value_terms = jnp.moveaxis(value_terms, 0, 1).reshape(seq_length, -1)
        key_own, value_own = (
            lax.psum_scatter(key_terms, "seq", scatter_dimension=0, tiled=True),
            lax.psum_scatter(value_terms, "seq", scatter_dimension=0, tiled=True),
        )
        return (q_grad, key_own, value_own)

    q_rot_grad, k_rot_grad, value_grad = lax.map(
        query_pass, (q_blocks, grad_blocks, key_back, value_back, allowed, row_max, row_sum)
    )
    q_rot_grad = q_rot_grad.reshape(micro_count * block_len, -1)
    k_rot_grad = k_rot_grad.reshape(micro_count * block_len, -1)
    v_grad = value_grad.reshape(micro_count * block_len, -1).astype(jnp.bfloat16)
    q_norm_grad = rotate(q_rot_grad, cos_table, sine_table, head_count, -1.0)
    k_norm_grad = rotate(k_rot_grad, cos_table, sine_table, group_count, -1.0)
    q_grad, grad_q_gain = rms_backward(q_norm_grad, q_gain, q_hat, q_factor)
    k_grad, grad_k_gain = rms_backward(k_norm_grad, k_gain, k_hat, k_factor)
    q_grad = q_grad.astype(jnp.bfloat16)
    k_grad = k_grad.astype(jnp.bfloat16)
    grad_w_query = weight_grad(flat_tokens, q_grad)
    grad_w_key = weight_grad(flat_tokens, k_grad)
    grad_w_value = weight_grad(flat_tokens, v_grad)
    input_grad = (
        hidden_grad
        + back_product(q_grad, w_query)
        + back_product(k_grad, w_key)
        + back_product(v_grad, w_value)
    )
    input_grad = input_grad.reshape(tokens.shape)
    summed = (
        lax.psum_scatter(grad_w_query, ("dp", "seq"), scatter_dimension=0, tiled=True),
        lax.psum_scatter(grad_w_key, ("dp", "seq"), scatter_dimension=0, tiled=True),
        lax.psum_scatter(grad_w_value, ("dp", "seq"), scatter_dimension=0, tiled=True),
        lax.psum_scatter(grad_w_out, ("dp", "seq"), scatter_dimension=0, tiled=True),
        lax.psum_scatter(grad_q_gain, ("dp", "seq"), scatter_dimension=0, tiled=True),
        lax.psum_scatter(grad_k_gain, ("dp", "seq"), scatter_dimension=0, tiled=True),
        lax.psum_scatter(grad_attn_gain, ("dp", "seq"), scatter_dimension=0, tiled=True),
        lax.psum_scatter(grad_w_gate, ("dp", "seq"), scatter_dimension=0, tiled=True),
        lax.psum_scatter(grad_w_up, ("dp", "seq"), scatter_dimension=0, tiled=True),
        lax.psum_scatter(grad_w_down, ("dp", "seq"), scatter_dimension=0, tiled=True),
        lax.psum_scatter(grad_mlp_gain, ("dp", "seq"), scatter_dimension=0, tiled=True),
    )
    return (
        layer_out,
        input_grad,
        summed[0],
        summed[1],
        summed[2],
        summed[3],
        summed[4],
        summed[5],
        summed[6],
        summed[7],
        summed[8],
        summed[9],
        summed[10],
    )


def split_by_heads(
    tokens, cotangent, w_query, w_key, w_value, w_out, q_gain, k_gain, attn_gain,
    w_gate, w_up, w_down, mlp_gain, doc_lengths, block_order,
):
    rope = rope_constant(1024)
    q_gain_rows, k_gain_rows = q_gain.reshape(16, HD), k_gain.reshape(8, HD)
    own_tokens = tokens[:, 0]
    layer_out, in_grad, g_query, g_key, g_value, g_out, vec, gains, g_gate, g_up, g_down = whole_layer(
        own_tokens, cotangent[:, 0], attn_gain[None], mlp_gain[None], q_gain_rows, k_gain_rows,
        rope, w_out, w_gate, w_up, w_down, w_query, w_key, w_value, block_order, doc_lengths,
    )
    (
        layer_out, in_grad, g_query, g_key, g_value, g_out, g_gate, g_up, g_down,
        g_q_gain, g_k_gain, g_attn_gain, g_mlp_gain,
    ) = finish((layer_out, in_grad, g_query, g_key, g_value, g_out, g_gate, g_up, g_down), vec, gains)
    return (
        layer_out.reshape(tokens.shape),
        in_grad.reshape(tokens.shape),
        g_query,
        g_key,
        g_value,
        g_out,
        g_q_gain[0],
        g_k_gain[0],
        g_attn_gain[0],
        g_gate,
        g_up,
        g_down,
        g_mlp_gain[0],
    )


SPECS_IN = (
    P(None, "dp", "seq", None), P(None, "dp", "seq", None),
    P(), P(), P(), P(), P(), P(), P(), P(), P(), P(), P(),
    P(None, "dp", None), P(),
)
SPECS_OUT = (
    P(None, "dp", "seq", None), P(None, "dp", "seq", None),
    P(("dp", "seq"), None), P(("dp", "seq"), None), P(("dp", "seq"), None), P(("dp", "seq"), None),
    P(("dp", "seq")), P(("dp", "seq")), P(("dp", "seq")),
    P(("dp", "seq"), None), P(("dp", "seq"), None), P(("dp", "seq"), None),
    P(("dp", "seq")),
)


def solution(mesh):
    body = split_by_heads if mesh.shape["seq"] == 16 and mesh.shape["dp"] == 2 else on_device
    return jax.shard_map(body, mesh=mesh, in_specs=SPECS_IN, out_specs=SPECS_OUT, check_vma=False)
```

```python
import functools

import jax
import jax.numpy as jnp
import numpy as np
from jax import lax
from jax.experimental import pallas as pl
from jax.experimental.pallas import tpu as pltpu
from jax.sharding import PartitionSpec as P

HD = 128
EPSILON = 1e-06
ROPE_BASE = 500000.0
MASK_FILL = -1e30
MESH = pl.DeviceIdType.MESH
LOW = jnp.bfloat16
WIDE = jnp.float32
TILE = 128
CHUNK = 256


def remote(source, target, send_sem, recv_sem, place):
    return pltpu.make_async_remote_copy(
        src_ref=source,
        dst_ref=target,
        send_sem=send_sem,
        recv_sem=recv_sem,
        device_id=place,
        device_id_type=MESH,
    )


def dot(left, right):
    return jnp.dot(left, right, preferred_element_type=WIDE)


def dot_nt(left, right):
    return lax.dot_general(left, right, (((1,), (1,)), ((), ())), preferred_element_type=WIDE)


def dot_tn(left, right):
    return lax.dot_general(left, right, (((0,), (0,)), ((), ())), preferred_element_type=WIDE)


class Spot:
    def __init__(self):
        self.dp = lax.axis_index("dp")
        self.seq = lax.axis_index("seq")
        self.core = self.seq % 2
        self.chip = self.seq // 2
        self.x = self.chip % 2
        self.z = self.chip // 2
        self.sibling = self.seq + 1 - 2 * self.core
        self.flip_x = self.seq + 2 - 4 * self.x
        self.far_z = (
            self.z + 1 - 2 * (self.z % 2),
            self.z + 2 - 4 * (self.z // 2),
            3 - self.z,
        )


class RowGather:
    def __init__(self, spot, own, held, local_sem, send_sems, recv_sems):
        self.spot, self.own, self.held = spot, own, held
        self.send_sems, self.recv_sems = send_sems, recv_sems
        self.sent = []
        self.local = pltpu.make_async_copy(own.at[spot.core], held.at[spot.seq], local_sem)

    def send(self, source, slots, recv_sem, target):
        copy = remote(
            source, slots, self.send_sems.at[len(self.sent)], recv_sem, (self.spot.dp, target)
        )
        copy.start()
        self.sent.append(copy)

    def start(self):
        spot = self.spot
        own_slot = self.held.at[spot.seq]
        own_sem = self.recv_sems.at[spot.seq]
        for far in spot.far_z:
            for micro in range(2):
                self.send(self.own.at[micro], own_slot, own_sem, far * 4 + spot.x * 2 + micro)
        for micro in range(2):
            self.send(
                self.own.at[micro], own_slot, own_sem, spot.z * 4 + (1 - spot.x) * 2 + micro
            )
        self.send(self.own.at[1 - spot.core], own_slot, own_sem, spot.sibling)
        self.local.start()

    def arrived(self, slots, recv_sem):
        remote(slots, slots, self.send_sems.at[0], recv_sem, (self.spot.dp, self.spot.sibling)).wait_recv()

    def forward(self):
        spot = self.spot
        for far in spot.far_z:
            first = far * 4 + spot.x * 2
            for core in range(2):
                self.arrived(self.held.at[first + core], self.recv_sems.at[first + core])
            pair = self.held.at[pl.ds(first, 2)]
            self.send(pair, pair, self.recv_sems.at[16 + far], spot.flip_x)

    def finish(self):
        spot = self.spot
        self.arrived(self.held.at[spot.sibling], self.recv_sems.at[spot.sibling])
        for core in range(2):
            slot = spot.z * 4 + (1 - spot.x) * 2 + core
            self.arrived(self.held.at[slot], self.recv_sems.at[slot])
        for far in spot.far_z:
            first = far * 4 + (1 - spot.x) * 2
            self.arrived(self.held.at[pl.ds(first, 2)], self.recv_sems.at[16 + far])
        self.local.wait()

    def drain(self):
        for copy in self.sent:
            copy.wait_send()


GATHER_SENDS = 12
GATHER_RECVS = 20


def rope_rows(table, block, first_length):
    start = block * 64
    inside = table[pl.ds(64 + start, 64), :]
    shifted = table[pl.ds(64 + jnp.maximum(start - first_length, -64), 64), :]
    places = start + lax.broadcasted_iota(jnp.int32, (64, HD), 0)
    both = jnp.where(places < first_length, inside, shifted)
    swapped = swap_halves(both)
    low_half = lax.broadcasted_iota(jnp.int32, (64, HD), 1) < HD // 2
    return jnp.where(low_half, both, swapped), jnp.where(low_half, -swapped, both)


def rope_part(table, part, first_length):
    first, second = (rope_rows(table, part * 2 + piece, first_length) for piece in range(2))
    return jnp.concatenate([first[0], second[0]], axis=0), jnp.concatenate([first[1], second[1]], axis=0)


def swap_halves(head):
    return pltpu.roll(head, HD // 2, axis=1)


def columns_of(rows):
    return jnp.concatenate([rows] * 16, axis=0).T[:, :8]


def rows_of(first, second):
    lane = lax.broadcasted_iota(jnp.int32, (first.shape[0], HD), 1)
    return jnp.where(lane == 0, first, second).T[:8]


def allowed_places(tile, count, first_length):
    keys = lax.broadcasted_iota(jnp.int32, (count, 2 * TILE), 0)
    lanes = lax.broadcasted_iota(jnp.int32, (1, 2 * TILE), 1)
    queries = tile * TILE + lanes % TILE
    earliest = jnp.where(queries < first_length, 0, first_length)
    return (keys >= earliest) & (keys <= queries)


def invert(order_ref, inverse_ref):
    def fill(block, carry):
        place = jnp.int32(0)
        for slot in range(16):
            place = jnp.maximum(place, jnp.where(order_ref[slot] == block, slot, 0))
        inverse_ref[block] = place
        return carry

    lax.fori_loop(0, 16, fill, 0)


class Post:
    def __init__(self, sems):
        self.sems, self.started, self.used = sems, [], 0

    def send(self, source, target, recv_sem, place, when=None):
        copy = remote(source, target, self.sems.at[self.used], recv_sem, place)
        self.used += 1
        self.started.append((copy, when))
        if when is None:
            copy.start()
        else:
            pl.when(when)(copy.start)

    def finish(self):
        started, self.started = self.started, []
        for copy, when in started:
            if when is None:
                copy.wait_send()
            else:
                pl.when(when)(copy.wait_send)


def arrived(spot, slot, recv_sem, spare_sem):
    remote(slot, slot, spare_sem, recv_sem, (spot.dp, spot.sibling)).wait_recv()


def aligned(start, size):
    return pl.ds(pl.multiple_of(start, size), size)


class AlongZ:
    def __init__(self, spot, post, spare):
        self.spot, self.post, self.spare = spot, post, spare
        half = spot.z // 2
        self.partner = spot.far_z[0]
        self.far_inner = 2 - half
        self.far_outer = 3 - 3 * half
        self.inner = ((spot.z + 1) // 2) % 2 == 1
        self.outer = ((spot.z + 1) // 2) % 2 == 0

    def place(self, z):
        return (self.spot.dp, z * 4 + self.spot.x * 2 + self.spot.core)

    def send(self, part, size, landing, transit, sems):
        spot, post = self.spot, self.post
        landing[2] = part[aligned(spot.z * size, size), :]
        for slot, far in enumerate((self.far_inner, self.far_outer)):
            post.send(
                part.at[aligned(far * size, size)], transit.at[slot], sems.at[2 + slot], self.place(self.partner),
                self.outer,
            )
        post.send(part.at[aligned(self.partner * size, size)], landing.at[0], sems.at[0], self.place(self.partner))

    def combine(self, part, size, landing, transit, sems):
        for slot, far in enumerate((self.far_inner, self.far_outer)):

            @pl.when(self.inner)
            def _():
                arrived(self.spot, transit.at[slot], sems.at[2 + slot], self.spare)
                added = transit[slot].astype(WIDE) + part[aligned(far * size, size), :].astype(WIDE)
                transit[slot] = added.astype(LOW)

            self.post.send(transit.at[slot], landing.at[1], sems.at[1], self.place(far), self.inner)

    def total(self, landing, sems):
        arrived(self.spot, landing.at[0], sems.at[0], self.spare)
        arrived(self.spot, landing.at[1], sems.at[1], self.spare)
        return landing[0].astype(WIDE) + landing[1].astype(WIDE) + landing[2].astype(WIDE)


def row_scale(values):
    return lax.rsqrt(jnp.mean(values * values, axis=-1, keepdims=True) + EPSILON)


def norm_back(grad, gain, normal, factor):
    weighted = grad * gain
    return factor * (weighted - normal * jnp.mean(weighted * normal, axis=-1, keepdims=True))


def layer_kernel(
    tok_ref, cot_ref, again_ref, mgain_ref, qgain_ref, kgain_ref,
    rope_hbm, wout_hbm, wg_hbm, wu_hbm, wd_hbm, wq_hbm, wk_hbm, wv_hbm, order_ref, docs_ref,
    layer_out, in_grad, g_query, g_key, g_value, g_out, vec_out, gain_out, g_gate, g_up, g_down,
    tok_all, own_stats, factors, lse, att_recv,
    wout, wgate, wup, wdown, q_pair, kv_nat, hat, rope_ref,
    hidden, hid_own, gate_pre, up_pre, mix_turned, att_turned, down_own, gu_own, proj_own, ag_own, vec_own,
    hid_all, down_all, proj_all, gu_all, mix_all, att_all, vec_all, vec_far,
    down_land, down_transit, wout_land, gu_land, gu_transit,
    ag_recv, ag_pair, k_turned, stat_all, grad_nat, grad_recv, part_sib, part_far, wqkv_recv, gain_own, gain_recv,
    inverse_ref, send_sems, recv_sems, own_sems, att_sems,
    local_sems, post_sems, hid_sems, dpl_sems, proj_sems, attp_sems, mix_sems, gup_sems,
    vec_sems, down_sems, wout_sems, gu_sems, gut_sems, ag_sems, stat_sems, grad_sems, sib_sem, wqkv_sems, gain_sems,
):
    spot = Spot()
    devices, chips = 16, 8
    dp, seq, core, chip, z = spot.dp, spot.seq, spot.core, spot.chip, spot.z
    me = dp * devices + seq
    member = dp * 4 + spot.x * 2 + core
    spare = post_sems.at[0]
    post = Post(post_sems)
    along = AlongZ(spot, post, spare)

    def load(source, target, index):
        copy = pltpu.make_async_copy(source, target, local_sems.at[index])
        copy.start()
        return copy

    barrier = pltpu.get_barrier_semaphore()
    for step in range(1, 2 * devices):
        other = (me + step) % (2 * devices)
        pl.semaphore_signal(barrier, inc=1, device_id=(other // devices, other % devices), device_id_type=MESH)
    load_query = load(wq_hbm, wgate.at[:, pl.ds(0, 2048)], 1)
    load_key = load(wk_hbm, wgate.at[:, pl.ds(2048, 1024)], 2)
    load_value = load(wv_hbm.at[:, aligned(chip * 128, 128)], wup.at[:, pl.ds(0, 128)], 4)
    load_rope = load(rope_hbm, rope_ref, 5)
    load_out = load(wout_hbm, wout, 0)
    load_down = load(wd_hbm, wdown, 3)
    invert(order_ref, inverse_ref)
    pl.semaphore_wait(barrier, 2 * devices - 1)
    gather = RowGather(spot, tok_ref, tok_all, local_sems.at[8], send_sems, recv_sems)
    gather.start()

    load_query.wait()
    load_key.wait()
    own = tok_ref[...].reshape(128, tok_ref.shape[-1])
    sums = []
    for start, stop in ((0, 2048), (2048, 3072)):
        parts = [dot(own, wgate[:, first : first + 512]) for first in range(start, stop, 512)]
        sums.append(sum(jnp.sum(part * part, axis=-1, keepdims=True) for part in parts) / (stop - start))
    own_stats[pl.ds(seq, 1)] = lax.rsqrt(rows_of(sums[0], sums[1]) + EPSILON)[None]
    for step in range(1, devices):
        post.send(own_stats.at[seq], own_stats.at[seq], own_sems.at[seq], (dp, (seq + step) % devices))
    gather.forward()
    for step in range(1, devices):
        other = (seq + step) % devices
        arrived(spot, own_stats.at[other], own_sems.at[other], spare)
    gather.finish()

    first_length = docs_ref[core, 0, 0]
    load_value.wait()
    for part in range(4):
        rows = pl.ds(part * CHUNK, CHUNK)
        chunk = jnp.concatenate([tok_all[inverse_ref[part * 4 + piece]] for piece in range(4)], axis=0)
        hat[rows, :256] = dot(chunk, wgate[:, aligned(chip * 256, 256)])
        hat[rows, 256:] = dot(chunk, wgate[:, pl.ds(pl.multiple_of(2048 + chip * 128, 128), 128)])
        kv_nat[rows, 128:] = dot(chunk, wup[:, :128]).astype(LOW)
    load_gate = load(wg_hbm, wgate, 1)
    load_up = load(wu_hbm, wup, 7)
    for block in range(16):
        both = own_stats[inverse_ref[block]]
        both = jnp.where(core == 0, both, pltpu.roll(both, 64, axis=1))
        factors[:, block * 64 : (block + 1) * 64] = both[:, :64]
    load_rope.wait()
    qgain = qgain_ref[pl.ds(chip * 2, 2), :]
    kgain = kgain_ref[pl.ds(chip, 1), :]
    for part in range(8):
        rows = pl.ds(part * TILE, TILE)
        scale = columns_of(factors[:, rows])
        cos, sine = rope_part(rope_ref, part, first_length)
        for head in range(3):
            lanes = pl.ds(head * HD, HD)
            column = scale[:, 0:1] if head < 2 else scale[:, 1:2]
            gain = qgain[head : head + 1] if head < 2 else kgain
            normal = hat[rows, lanes] * column
            hat[rows, lanes] = normal
            normed = normal * gain
            turned = (normed * cos + swap_halves(normed) * sine).astype(LOW)
            if head < 2:
                q_pair[part, pl.ds(head * HD, HD), :] = turned
            else:
                kv_nat[rows, :HD] = turned
    k_turned[...] = kv_nat[:, HD:].T
    for tile in range(8):
        count = (tile + 1) * TILE
        scores = dot_nt(kv_nat[:count, :HD], q_pair[tile]) * HD ** (-0.5)
        masked = jnp.where(allowed_places(tile, count, first_length), scores, MASK_FILL)
        top = jnp.max(masked, axis=0, keepdims=True)
        terms = jnp.exp(masked - top)
        weight = jnp.sum(terms, axis=0, keepdims=True)
        lse[pl.ds(tile, 1), :] = top + jnp.log(weight)
        turned = dot(k_turned[:, :count], terms.astype(LOW)) / weight
        attended = turned.T.astype(LOW)
        grad_nat[pl.ds(tile * 2, 2), :, :HD] = attended[:TILE].reshape(2, 64, HD)
        grad_nat[pl.ds(tile * 2, 2), :, HD : 2 * HD] = attended[TILE:].reshape(2, 64, HD)
    att_recv[pl.ds(chip, 1), pl.ds(core, 1)] = grad_nat[order_ref[seq], :, : 2 * HD][None, None]
    for step in range(1, devices):
        other = (seq + step) % devices
        slot = (step % 2, slice(None), slice((step // 2) * 256, (step // 2 + 1) * 256))
        ag_own[slot] = grad_nat[order_ref[other], :, : 2 * HD]
        post.send(ag_own.at[slot], att_recv.at[chip, core], att_sems.at[seq], (dp, other))
    for step in range(1, devices):
        other = (seq + step) % devices
        arrived(spot, att_recv.at[other // 2, other % 2], att_sems.at[other], spare)
    post.finish()

    for group in range(8):
        attended = att_recv[group]
        ag_own[:, :, group * 256 : (group + 1) * 256] = attended
        block = attended.reshape(128, 256).T
        for piece in range(4):
            att_turned[(group // 4) * 4 + piece, pl.ds((group % 4) * 64, 64), :] = block[piece * 64 : (piece + 1) * 64]
    x_place, y_place, sib_place = (dp, spot.flip_x), (1 - dp, seq), (dp, spot.sibling)
    x_member = dp * 4 + (1 - spot.x) * 2 + core
    y_member = (1 - dp) * 4 + spot.x * 2 + core
    diagonal = (1 - dp) * 4 + (1 - spot.x) * 2 + core
    keeps = {}

    def spread(own, held, sems, index):
        keeps[index] = load(own, held.at[member], index)
        for place in (x_place, y_place, sib_place):
            post.send(own, held.at[member], sems.at[member], place)

    def pass_on(held, sems, across):
        turn = (x_member, y_place) if across == "y" else (y_member, x_place)
        straight = y_member if across == "y" else x_member
        for other, places in ((turn[0], (turn[1], sib_place)), (straight, (sib_place,))):
            arrived(spot, held.at[other], sems.at[other], spare)
            for place in places:
                post.send(held.at[other], held.at[other], sems.at[other], place)

    def pass_diagonal(held, sems):
        arrived(spot, held.at[diagonal], sems.at[diagonal], spare)
        post.send(held.at[diagonal], held.at[diagonal], sems.at[diagonal], sib_place)

    def whole(held, sems, index):
        keeps[index].wait()
        for y in range(2):
            for x in range(2):
                other = y * 4 + x * 2 + 1 - core
                arrived(spot, held.at[other], sems.at[other], spare)

    def deal(own, held, sems, index):
        keeps[index] = load(own.at[member], held.at[member], index)
        for step in range(1, 8):
            other = (member + step) % 8
            post.send(own.at[other], held.at[member], sems.at[member], (other // 4, z * 4 + other % 4))

    def dealt(held, sems, index):
        keeps[index].wait()
        for step in range(1, 8):
            other = (member + step) % 8
            arrived(spot, held.at[other], sems.at[other], spare)

    deal(att_turned, att_all, attp_sems, 10)
    load_out.wait()
    attn_proj = dot(ag_own[...].reshape(128, 2048), wout[...])
    att_factor = row_scale(attn_proj)
    normal = attn_proj * att_factor
    in_grad[...] = normal
    stream = tok_ref[...].reshape(128, 1024).astype(WIDE) + normal * again_ref[...]
    hidden[...] = stream
    hid_own[...] = stream.astype(LOW)
    spread(hid_own, hid_all, hid_sems, 9)

    load_gate.wait()
    load_up.wait()
    for group in range(8):
        lanes = slice(group * 384, (group + 1) * 384)
        gate = dot(hid_own[...], wgate[:, lanes])
        up = dot(hid_own[...], wup[:, lanes])
        gate_pre[group] = gate
        up_pre[group] = up
        block = (gate * jax.nn.sigmoid(gate) * up).astype(LOW)
        gu_own[group, :, :384] = block
        turned = block.T
        for piece in range(4):
            mix_turned[(group // 4) * 4 + piece, pl.ds((group % 4) * 96, 96), :] = turned[piece * 96 : (piece + 1) * 96]
    deal(mix_turned, mix_all, mix_sems, 11)
    pass_on(hid_all, hid_sems, "y")
    load_down.wait()
    down_pre = jnp.zeros((128, 1024), WIDE)
    for group in range(8):
        down_pre = down_pre + dot(gu_own[group, :, :384], wdown[group * 384 : (group + 1) * 384, :])
    factor = row_scale(down_pre)
    normal = down_pre * factor
    cot = cot_ref[...].reshape(128, 1024).astype(WIDE)
    layer_out[...] = (hidden[...] + normal * mgain_ref[...]).astype(LOW)
    down_own[...] = norm_back(cot, mgain_ref[...], normal, factor).astype(LOW)
    mlp_sum = jnp.sum(cot * normal, axis=0, keepdims=True)
    for piece in range(4):
        vec_own[4 + piece : 5 + piece, :] = mlp_sum[:, piece * 256 : (piece + 1) * 256]

    for step in range(1, 9):
        group = (member + step) % 8
        grad = dot_nt(down_own[...], wdown[aligned(group * 384, 384), :])
        gate, up = gate_pre[group], up_pre[group]
        sigmoid = jax.nn.sigmoid(gate)
        gu_own[group, :, :384] = (grad * up * sigmoid * (1.0 + gate * (1.0 - sigmoid))).astype(LOW)
        gu_own[group, :, 384:] = (grad * gate * sigmoid).astype(LOW)
    hgrad = cot
    for group in range(8):
        lanes = slice(group * 384, (group + 1) * 384)
        hgrad = hgrad + dot_nt(gu_own[group, :, :384], wgate[:, lanes]) + dot_nt(gu_own[group, :, 384:], wup[:, lanes])
    hidden[...] = hgrad
    normal = in_grad[...]
    proj_own[...] = norm_back(hgrad, again_ref[...], normal, att_factor).astype(LOW)
    attn_sum = jnp.sum(hgrad * normal, axis=0, keepdims=True)
    for piece in range(4):
        vec_own[piece : piece + 1, :] = attn_sum[:, piece * 256 : (piece + 1) * 256]
    load_query = load(wq_hbm, wgate.at[:, pl.ds(0, 2048)], 1)
    load_key = load(wk_hbm, wgate.at[:, pl.ds(2048, 1024)], 2)
    load_value = load(wv_hbm, wup.at[:, pl.ds(0, 1024)], 3)

    att_grad = dot_nt(proj_own[...], wout[...]).astype(LOW)
    ag_own[...] = att_grad.reshape(2, 64, 2048)
    keep_ag = load(ag_own.at[core, :, aligned(chip * 256, 256)], ag_recv.at[seq], 14)
    for step in range(1, devices):
        other = (seq + step) % devices
        post.send(
            ag_own.at[other % 2, :, aligned((other // 2) * 256, 256)], ag_recv.at[seq], ag_sems.at[seq], (dp, other)
        )
    keep_vec = load(vec_own, vec_all.at[member], 16)
    for step in range(1, 8):
        other = (member + step) % 8
        post.send(vec_own, vec_all.at[member], vec_sems.at[member], (other // 4, z * 4 + other % 4))
    spread(down_own, down_all, dpl_sems, 12)
    pass_diagonal(hid_all, hid_sems)
    pass_on(down_all, dpl_sems, "x")
    spread(proj_own, proj_all, proj_sems, 15)
    deal(gu_own, gu_all, gup_sems, 13)
    keep_ag.wait()
    for step in range(1, devices):
        other = (seq + step) % devices
        arrived(spot, ag_recv.at[other], ag_sems.at[other], spare)
    for tile in range(8):
        block = jnp.concatenate([ag_recv[inverse_ref[tile * 2 + piece]] for piece in range(2)], axis=0)
        ag_pair[tile, :TILE, :] = block[:, :HD]
        ag_pair[tile, TILE:, :] = block[:, HD:]
    k_turned[...] = kv_nat[:, :HD].T
    up_pre[:, :, :256] = jnp.zeros((8, TILE, 256), WIDE)
    down_part = wdown.at[pl.ds(0, 384)]
    for tile in range(7, -1, -1):
        if tile == 1:
            pass_diagonal(down_all, dpl_sems)
            dealt(mix_all, mix_sems, 11)
            whole(down_all, dpl_sems, 12)
            mixes = jnp.concatenate([mix_all[other] for other in range(8)], axis=1)
            down_part[...] = dot(mixes, down_all[...].reshape(1024, 1024)).astype(LOW)
            along.send(down_part, 96, down_land, down_transit, down_sems)
        count = (tile + 1) * TILE
        queries, grads = q_pair[tile], ag_pair[tile]
        scores = dot_nt(kv_nat[:count, :HD], queries) * HD ** (-0.5)
        masked = jnp.where(allowed_places(tile, count, first_length), scores, MASK_FILL)
        probs = jnp.exp(masked - lse[tile : tile + 1, :])
        prob_grad = dot_nt(kv_nat[:count, HD:], grads)
        row_dot = jnp.sum(probs * prob_grad, axis=0, keepdims=True)
        score_grad = (probs * (prob_grad - row_dot)).astype(LOW)
        up_pre[: tile + 1, :, :HD] += dot(score_grad, queries).reshape(tile + 1, TILE, HD)
        up_pre[: tile + 1, :, HD:256] += dot(probs.astype(LOW), grads).reshape(tile + 1, TILE, HD)
        turned = (dot(k_turned[:, :count], score_grad) * HD ** (-0.5)).T
        gate_pre[tile, :, :HD] = turned[:TILE]
        gate_pre[tile, :, HD:256] = turned[TILE:]

    pass_on(proj_all, proj_sems, "y")
    keep_vec.wait()
    for step in range(1, 8):
        other = (member + step) % 8
        arrived(spot, vec_all.at[other], vec_sems.at[other], spare)
    vec = vec_all[0]
    for other in range(1, 8):
        vec = vec + vec_all[other]
    vec_far[pl.ds(z, 1)] = vec[None]
    for far in spot.far_z:
        post.send(vec_far.at[z], vec_far.at[z], vec_sems.at[8 + z], along.place(far))

    gains = [jnp.zeros((1, HD), WIDE) for _ in range(3)]
    for part in range(8):
        rows = pl.ds(part * TILE, TILE)
        cos, sine = rope_part(rope_ref, part, first_length)
        dots = []
        for head in range(3):
            lanes = slice(head * HD, (head + 1) * HD)
            turned = gate_pre[part, :, lanes] if head < 2 else up_pre[part, :, :HD] * HD ** (-0.5)
            back = turned * cos - swap_halves(turned) * sine
            normal = hat[rows, lanes]
            gain = qgain[head : head + 1] if head < 2 else kgain
            gains[head] = gains[head] + jnp.sum(back * normal, axis=0, keepdims=True)
            weighted = back * gain
            if head < 2:
                gate_pre[part, :, lanes] = weighted
            else:
                up_pre[part, :, :HD] = weighted
            dots.append(jnp.sum(weighted * normal, axis=-1, keepdims=True))
        stat_all[pl.ds(chip, 1), :, rows] = rows_of(dots[0] + dots[1], dots[2])[None]
    for step in range(1, chips):
        other = (chip + step) % chips
        post.send(stat_all.at[chip], stat_all.at[chip], stat_sems.at[chip], (dp, other * 2 + core))
    gain_own[...] = jnp.concatenate([jnp.broadcast_to(gain, (8, HD)) for gain in gains], axis=1)
    for piece in range(4):
        target = chip * 4 + piece
        slot = gain_recv.at[dp * 2 + core]

        @pl.when(target == me)
        def _():
            gain_recv[pl.ds(dp * 2 + core, 1)] = gain_own[...][None]

        post.send(gain_own, slot, gain_sems.at[dp * 2 + core], (target // devices, target % devices), target != me)

    along.combine(down_part, 96, down_land, down_transit, down_sems)
    for step in range(1, chips):
        other = (chip + step) % chips
        arrived(spot, stat_all.at[other], stat_sems.at[other], spare)
    total = stat_all[0]
    for other in range(1, chips):
        total = total + stat_all[other]
    width = jnp.where(lax.broadcasted_iota(jnp.int32, total.shape, 0) == 0, 1.0 / 2048, 1.0 / 1024)
    means = total * width
    grad_send = wdown.at[pl.ds(1024, 1024), pl.ds(512, 512)]
    for part in range(8):
        rows = pl.ds(part * TILE, TILE)
        mean = columns_of(means[:, part * TILE : (part + 1) * TILE])
        scale = columns_of(factors[:, rows])
        for head in range(3):
            column = 0 if head < 2 else 1
            weighted = gate_pre[part, :, head * HD : (head + 1) * HD] if head < 2 else up_pre[part, :, :HD]
            normal = hat[rows, pl.ds(head * HD, HD)]
            grad = scale[:, column : column + 1] * (weighted - normal * mean[:, column : column + 1])
            grad_nat[pl.ds(part * 2, 2), :, head * HD : (head + 1) * HD] = grad.astype(LOW).reshape(2, 64, HD)
        grad_nat[pl.ds(part * 2, 2), :, 3 * HD :] = up_pre[part, :, HD:256].astype(LOW).reshape(2, 64, HD)
    for step in range(devices):
        other = (seq + step) % devices
        rows = aligned(other * 64, 64)
        block = grad_nat[order_ref[other]]
        grad_send[rows, :] = block
        if step > 0:
            post.send(grad_send.at[rows], grad_recv.at[chip, core], grad_sems.at[seq], (dp, other))
        else:
            grad_recv[pl.ds(chip, 1), pl.ds(core, 1)] = block[None, None]

    part_low = wdown.at[pl.ds(2048, 1024), pl.ds(0, 512)]
    for first in range(0, 1024, 256):
        part = dot_tn(tok_all[:, :, first : first + 256].reshape(1024, 256), grad_send[...])
        part_low[first : first + 256, :] = part.astype(LOW)
    post.send(part_low.at[aligned((1 - core) * 512, 512)], part_sib, sib_sem.at[0], sib_place)

    dealt(gu_all, gup_sems, 13)
    whole(hid_all, hid_sems, 9)
    gu_part = wout.at[pl.ds(1024, 1024), pl.ds(0, 768)]
    for first in range(0, 1024, 256):
        part = dot_tn(hid_all[:, :, first : first + 256].reshape(1024, 256), gu_all[...].reshape(1024, 768))
        gu_part[first : first + 256, :] = part.astype(LOW)
    for y in range(2):
        for slot, far in enumerate((along.far_inner, along.far_outer)):
            post.send(
                gu_part.at[aligned(y * 512 + far * 128, 128)], gu_transit.at[slot, y], gut_sems.at[slot, y],
                along.place(along.partner), along.outer,
            )
    arrived(spot, part_sib, sib_sem.at[0], spare)
    part_sum = wdown.at[pl.ds(2048, 512), pl.ds(512, 512)]
    part_sum[...] = (part_low[aligned(core * 512, 512), :].astype(WIDE) + part_sib[...].astype(WIDE)).astype(LOW)
    post.send(part_sum.at[aligned((1 - dp) * 256, 256)], part_far, sib_sem.at[1], y_place)
    for step in range(8):
        other = (member + step) % 8
        first = (other // 4) * 512 + (other % 4) * 32
        post.send(
            gu_part.at[aligned(first + along.partner * 128, 32)], gu_land.at[0, member], gu_sems.at[0, member],
            (other // 4, along.partner * 4 + other % 4),
        )
        if step > 0:
            post.send(
                gu_part.at[aligned(first + z * 128, 32)], gu_land.at[2, member], gu_sems.at[2, member],
                (other // 4, z * 4 + other % 4),
            )
    gu_land[2, pl.ds(member, 1)] = gu_part[aligned((member // 4) * 512 + z * 128 + (member % 4) * 32, 32), :][None]

    arrived(spot, part_far, sib_sem.at[1], spare)
    part_end = wdown.at[pl.ds(2560, 256), pl.ds(512, 512)]
    part_end[...] = (part_sum[aligned(dp * 256, 256), :].astype(WIDE) + part_far[...].astype(WIDE)).astype(LOW)
    for step in range(8):
        slot = (seq + step) % 8
        other = dp * 8 + slot
        rows = aligned(slot * 32, 32)

        @pl.when((core == dp) & (other == seq))
        def _():
            wqkv_recv[pl.ds(chip, 1)] = part_end[rows, :][None]

        post.send(
            part_end.at[rows], wqkv_recv.at[chip], wqkv_sems.at[chip], (core, other),
            (core != dp) | (other != seq),
        )

    for slot, far in enumerate((along.far_inner, along.far_outer)):
        for y in range(2):

            @pl.when(along.inner)
            def _():
                arrived(spot, gu_transit.at[slot, y], gut_sems.at[slot, y], spare)
                added = gu_transit[slot, y].astype(WIDE) + gu_part[aligned(y * 512 + far * 128, 128), :].astype(WIDE)
                gu_transit[slot, y] = added.astype(LOW)

            for piece in range(4):
                post.send(
                    gu_transit.at[slot, y, pl.ds(piece * 32, 32)], gu_land.at[1, member], gu_sems.at[1, member],
                    (y, far * 4 + piece), along.inner,
                )

    pass_diagonal(proj_all, proj_sems)
    dealt(att_all, attp_sems, 10)
    whole(proj_all, proj_sems, 15)
    turned = jnp.concatenate([att_all[other] for other in range(8)], axis=1)
    wout_part = wdown.at[pl.ds(384, 256)]
    wout_part[...] = dot(turned, proj_all[...].reshape(1024, 1024)).astype(LOW)
    wout_land[pl.ds(z, 1)] = wout_part[aligned(z * 64, 64), :][None]
    for far in spot.far_z:
        post.send(wout_part.at[aligned(far * 64, 64)], wout_land.at[z], wout_sems.at[z], along.place(far))
    for step in range(1, devices):
        other = (seq + step) % devices
        arrived(spot, grad_recv.at[other // 2, other % 2], grad_sems.at[other], spare)
    load_query.wait()
    load_key.wait()
    load_value.wait()
    grad_k, grad_v = [], []
    gradient = hidden[...]
    for piece in range(chips):
        block = grad_recv[piece].reshape(128, 512)
        gradient = gradient + dot_nt(block[:, :256], wgate[:, piece * 256 : (piece + 1) * 256])
        grad_k.append(block[:, 256:384])
        grad_v.append(block[:, 384:])
    gradient = gradient + dot_nt(jnp.concatenate(grad_k, axis=1), wgate[:, 2048:])
    in_grad[...] = gradient + dot_nt(jnp.concatenate(grad_v, axis=1), wup[:, :1024])

    for y in range(2):
        for micro in range(2):
            source = y * 2 + micro
            sender = y * devices + (me // 4) * 2 + micro

            @pl.when(sender != me)
            def _():
                arrived(spot, gain_recv.at[source], gain_sems.at[source], spare)

    gain_out[...] = sum(gain_recv[source] for source in range(4))
    for source in range(chips):
        sender = (seq // 8) * devices + source * 2 + dp

        @pl.when(sender != me)
        def _():
            arrived(spot, wqkv_recv.at[source], wqkv_sems.at[source], spare)

    for piece in range(chips):
        block = wqkv_recv[piece].astype(WIDE)
        g_query[:, piece * 256 : (piece + 1) * 256] = block[:, :256]
        g_key[:, piece * 128 : (piece + 1) * 128] = block[:, 256:384]
        g_value[:, piece * 128 : (piece + 1) * 128] = block[:, 384:]
    for far in spot.far_z:
        arrived(spot, vec_far.at[far], vec_sems.at[8 + far], spare)
    vec_out[...] = sum(vec_far[far] for far in range(4))
    g_down[...] = along.total(down_land, down_sems)
    for step in range(8):
        other = (member + step) % 8
        for kind in range(3):
            if kind < 2 or step > 0:
                arrived(spot, gu_land.at[kind, other], gu_sems.at[kind, other], spare)
    for slot in range(8):
        block = sum(gu_land[kind, slot].astype(WIDE) for kind in range(3))
        g_gate[:, slot * 384 : (slot + 1) * 384] = block[:, :384]
        g_up[:, slot * 384 : (slot + 1) * 384] = block[:, 384:]
    for far in spot.far_z:
        arrived(spot, wout_land.at[far], wout_sems.at[far], spare)
    g_out[...] = sum(wout_land[far].astype(WIDE) for far in range(4))
    post.finish()
    gather.drain()


POST_SENDS = 256


def whole_layer(*operands):
    length, width = 1024, 1024
    any_spec = pl.BlockSpec(memory_space=pl.ANY)
    vmem = pl.BlockSpec(memory_space=pltpu.VMEM)
    smem = pl.BlockSpec(memory_space=pltpu.SMEM)
    shape = jax.ShapeDtypeStruct
    dma = pltpu.SemaphoreType.DMA
    return pl.pallas_call(
        layer_kernel,
        out_shape=(
            shape((128, width), LOW),
            shape((128, width), WIDE),
            shape((32, 2048), WIDE),
            shape((32, 1024), WIDE),
            shape((32, 1024), WIDE),
            shape((64, 1024), WIDE),
            shape((8, 256), WIDE),
            shape((8, 384), WIDE),
            shape((32, 3072), WIDE),
            shape((32, 3072), WIDE),
            shape((96, 1024), WIDE),
        ),
        in_specs=[vmem] * 6 + [any_spec] * 8 + [smem] * 2,
        out_specs=(vmem,) * 11,
        scratch_shapes=[
            pltpu.VMEM((16, 64, width), LOW),
            pltpu.VMEM((16, 8, HD), WIDE),
            pltpu.VMEM((8, length), WIDE),
            pltpu.VMEM((8, 2 * TILE), WIDE),
            pltpu.VMEM((8, 2, 64, 2 * HD), LOW),
            pltpu.VMEM((2048, width), LOW),
            pltpu.VMEM((width, 3072), LOW),
            pltpu.VMEM((width, 3072), LOW),
            pltpu.VMEM((3072, width), LOW),
            pltpu.VMEM((8, 2 * TILE, HD), LOW),
            pltpu.VMEM((length, 2 * HD), LOW),
            pltpu.VMEM((length, 3 * HD), WIDE),
            pltpu.VMEM((length + 64, HD), WIDE),
            pltpu.VMEM((128, width), WIDE),
            pltpu.VMEM((128, width), LOW),
            pltpu.VMEM((8, 128, 384), WIDE),
            pltpu.VMEM((8, 128, 384), WIDE),
            pltpu.VMEM((8, 384, 128), LOW),
            pltpu.VMEM((8, 256, 128), LOW),
            pltpu.VMEM((128, width), LOW),
            pltpu.VMEM((8, 128, 768), LOW),
            pltpu.VMEM((128, width), LOW),
            pltpu.VMEM((2, 64, 2048), LOW),
            pltpu.VMEM((8, 256), WIDE),
            pltpu.VMEM((8, 128, width), LOW),
            pltpu.VMEM((8, 128, width), LOW),
            pltpu.VMEM((8, 128, width), LOW),
            pltpu.VMEM((8, 128, 768), LOW),
            pltpu.VMEM((8, 384, 128), LOW),
            pltpu.VMEM((8, 256, 128), LOW),
            pltpu.VMEM((8, 8, 256), WIDE),
            pltpu.VMEM((4, 8, 256), WIDE),
            pltpu.VMEM((3, 96, width), LOW),
            pltpu.VMEM((2, 96, width), LOW),
            pltpu.VMEM((4, 64, width), LOW),
            pltpu.VMEM((3, 8, 32, 768), LOW),
            pltpu.VMEM((2, 2, 128, 768), LOW),
            pltpu.VMEM((16, 64, 256), LOW),
            pltpu.VMEM((8, 2 * TILE, HD), LOW),
            pltpu.VMEM((HD, length), LOW),
            pltpu.VMEM((8, 8, length), WIDE),
            pltpu.VMEM((16, 64, 512), LOW),
            pltpu.VMEM((8, 2, 64, 512), LOW),
            pltpu.VMEM((512, 512), LOW),
            pltpu.VMEM((256, 512), LOW),
            pltpu.VMEM((8, 32, 512), LOW),
            pltpu.VMEM((8, 384), WIDE),
            pltpu.VMEM((4, 8, 384), WIDE),
            pltpu.SMEM((16,), jnp.int32),
            dma((GATHER_SENDS,)),
            dma((GATHER_RECVS,)),
            dma((16,)),
            dma((16,)),
            dma((17,)),
            dma((POST_SENDS,)),
            dma((8,)),
            dma((8,)),
            dma((8,)),
            dma((8,)),
            dma((8,)),
            dma((8,)),
            dma((12,)),
            dma((4,)),
            dma((4,)),
            dma((3, 8)),
            dma((2, 2)),
            dma((16,)),
            dma((8,)),
            dma((16,)),
            dma((2,)),
            dma((16,)),
            dma((4,)),
        ],
        compiler_params=pltpu.CompilerParams(
            collective_id=0, has_side_effects=True, vmem_limit_bytes=63 * 2**20
        ),
        name="whole_layer",
    )(*operands)


def rope_constant(length):
    frequency = np.power(np.float32(ROPE_BASE), -np.arange(0, HD, 2).astype(np.float32) / np.float32(HD)).astype(np.float32)
    angles = (np.arange(length, dtype=np.float32)[:, None] * frequency[None, :]).astype(np.float32).astype(np.float64)
    table = np.concatenate([np.cos(angles), np.sin(angles)], axis=1)
    return jnp.asarray(np.concatenate([np.zeros((64, HD)), table], axis=0), WIDE)


def finish_kernel(*refs):
    count = 9
    sources, vec_ref, gain_ref = refs[:count], refs[count], refs[count + 1]
    targets, small = refs[count + 2 : 2 * count + 2], refs[2 * count + 2 :]
    for source, target in zip(sources, targets):
        target[...] = source[...]
    seq = lax.axis_index("seq")
    me = lax.axis_index("dp") * 16 + seq
    part = seq % 4
    gains = gain_ref[...]
    q_out, k_out, attn_out, mlp_out = small
    q_all = pltpu.roll(gains[:, :256], (256 - part * 64) % 256, axis=1)
    k_all = pltpu.roll(gains[:, 256:], (128 - part * 32) % 128, axis=1)
    turn = (256 - (me % 8) * 32) % 256
    attn_all = pltpu.roll(jnp.broadcast_to(vec_ref[pl.ds(me // 8, 1), :], (8, 256)), turn, axis=1)
    mlp_all = pltpu.roll(jnp.broadcast_to(vec_ref[pl.ds(4 + me // 8, 1), :], (8, 256)), turn, axis=1)
    q_out[...] = q_all[0:1, :64]
    k_out[...] = k_all[0:1, :32]
    attn_out[...] = attn_all[0:1, :32]
    mlp_out[...] = mlp_all[0:1, :32]


def finish(arrays, vec, gains):
    vmem = pl.BlockSpec(memory_space=pltpu.VMEM)
    shape = jax.ShapeDtypeStruct
    count = len(arrays)
    return pl.pallas_call(
        finish_kernel,
        out_shape=tuple(shape(a.shape, a.dtype) for a in arrays)
        + (shape((1, 64), WIDE), shape((1, 32), WIDE), shape((1, 32), WIDE), shape((1, 32), WIDE)),
        in_specs=[vmem] * (count + 2),
        out_specs=(vmem,) * (count + 4),
        name="finish",
    )(*arrays, vec, gains)


def rms_forward(inputs, gain_vec):
    factor = lax.rsqrt(jnp.mean(inputs * inputs, axis=-1, keepdims=True) + EPSILON)
    normal = inputs * factor
    return (normal * gain_vec, normal, factor)


def rms_backward(grad_in, gain_vec, normal, factor):
    weighted = grad_in * gain_vec
    gain_grad = jnp.sum(grad_in * normal, axis=0)
    inner_mean = jnp.mean(weighted * normal, axis=-1, keepdims=True)
    return (factor * (weighted - normal * inner_mean), gain_grad)


def rope_tables(rot_places, head_size):
    frequency = jnp.power(ROPE_BASE, -jnp.arange(0, head_size, 2).astype(jnp.float32) / head_size)
    angles = rot_places.astype(jnp.float32)[:, None] * frequency[None, :]
    return (jnp.cos(angles), jnp.sin(angles))


def rotate(inputs, cos_table, sine_table, head_count, direction):
    row_count = inputs.shape[0]
    halves = inputs.reshape(row_count, head_count, 2, -1)
    first_half = halves[:, :, 0]
    second = halves[:, :, 1]
    cos_part = cos_table[:, None, :]
    sine_part = sine_table[:, None, :] * direction
    turned = jnp.stack(
        [first_half * cos_part - second * sine_part, second * cos_part + first_half * sine_part],
        axis=2,
    )
    return turned.reshape(row_count, -1)


def product(left, right):
    return jnp.dot(left, right, preferred_element_type=jnp.float32)


def weight_grad(left, right):
    return lax.dot_general(
        left, right, (((0,), (0,)), ((), ())), preferred_element_type=jnp.float32
    )


def back_product(left, right):
    return lax.dot_general(
        left, right, (((1,), (1,)), ((), ())), preferred_element_type=jnp.float32
    )


def heads_first(rows, group_count, head_size):
    shaped = rows.reshape(rows.shape[0], group_count, -1, head_size)
    return jnp.moveaxis(shaped, 1, 0)


def kv_first(rows, group_count, head_size):
    return jnp.moveaxis(rows.reshape(rows.shape[0], group_count, head_size), 1, 0)


def score_block(q_group, k_group, mask_rows, score_scale):
    raw_scores = (
        jnp.einsum("trd,ud->rtu", q_group, k_group, preferred_element_type=jnp.float32)
        * score_scale
    )
    return jnp.where(mask_rows[None], raw_scores, MASK_FILL)


def attend(pieces, score_scale, group_count, head_size):
    q_rows, key_rows, value_rows, mask_rows = pieces

    def attend_one_group(parts):
        q_group, k_group, v_group = parts
        masked = score_block(q_group, k_group, mask_rows, score_scale)
        row_max = jnp.max(masked, axis=-1)
        exp_terms = jnp.exp(masked - row_max[..., None])
        row_sum = jnp.sum(exp_terms, axis=-1)
        attn_prob = (exp_terms / row_sum[..., None]).astype(jnp.bfloat16)
        attended = jnp.einsum("rtu,ud->trd", attn_prob, v_group, preferred_element_type=jnp.float32)
        return (attended, row_max, row_sum)

    attended, row_max, row_sum = lax.map(
        attend_one_group,
        (
            heads_first(q_rows, group_count, head_size),
            kv_first(key_rows, group_count, head_size),
            kv_first(value_rows, group_count, head_size),
        ),
    )
    attended = jnp.moveaxis(attended, 0, 1)
    return (attended.reshape(q_rows.shape[0], -1), row_max, row_sum)


def score_grads(
    q_group, grad_group, k_group, v_group, mask_rows, row_max, row_sum, row_dot, score_scale
):
    masked = score_block(q_group, k_group, mask_rows, score_scale)
    attn_prob = jnp.exp(masked - row_max[..., None]) / row_sum[..., None]
    prob_grad = jnp.einsum("trd,ud->rtu", grad_group, v_group, preferred_element_type=jnp.float32)
    row_dot = jnp.sum(attn_prob * prob_grad, axis=-1)
    score_grad = (attn_prob * (prob_grad - row_dot[..., None])).astype(jnp.bfloat16)
    return (attn_prob.astype(jnp.bfloat16), score_grad, row_dot)


def on_device(
    tokens,
    cotangent,
    w_query,
    w_key,
    w_value,
    w_out,
    q_gain,
    k_gain,
    attn_gain,
    w_gate,
    w_up,
    w_down,
    mlp_gain,
    doc_lengths,
    block_order,
):
    micro_count = tokens.shape[0]
    block_len = tokens.shape[2]
    model_width = tokens.shape[3]
    seq_length = lax.axis_size("seq") * block_len
    head_count = w_query.shape[1] // HD
    group_count = w_key.shape[1] // HD
    score_scale = HD ** (-0.5)
    flat_tokens = tokens.reshape(micro_count * block_len, model_width)
    out_grad = cotangent.reshape(micro_count * block_len, model_width).astype(jnp.float32)
    first_lengths = doc_lengths[:, 0, 0]
    offsets = jnp.arange(block_len, dtype=jnp.int32)
    own_places = block_order[lax.axis_index("seq")] * block_len + offsets
    key_places = (block_order[:, None] * block_len + offsets[None, :]).reshape(seq_length)
    own_segments = (own_places[None, :] >= first_lengths[:, None]).astype(jnp.int32)
    all_segments = (key_places[None, :] >= first_lengths[:, None]).astype(jnp.int32)
    rot_places = (own_places[None, :] - own_segments * first_lengths[:, None]).reshape(-1)
    allowed = (own_segments[:, :, None] == all_segments[:, None, :]) & (
        key_places[None, None, :] <= own_places[None, :, None]
    )
    cos_table, sine_table = rope_tables(rot_places, HD)
    q_pre = product(flat_tokens, w_query)
    k_pre = product(flat_tokens, w_key)
    v_pre = product(flat_tokens, w_value)
    q_norm, q_hat, q_factor = rms_forward(q_pre, q_gain)
    k_norm, k_hat, k_factor = rms_forward(k_pre, k_gain)
    q_low = rotate(q_norm, cos_table, sine_table, head_count, 1.0).astype(jnp.bfloat16)
    k_low = rotate(k_norm, cos_table, sine_table, group_count, 1.0).astype(jnp.bfloat16)
    v_low = v_pre.astype(jnp.bfloat16)
    q_blocks = q_low.reshape(micro_count, block_len, -1)
    k_blocks = k_low.reshape(micro_count, block_len, -1)
    v_blocks = v_low.reshape(micro_count, block_len, -1)
    key_all, value_all = (
        lax.all_gather(k_blocks, "seq", axis=1, tiled=True),
        lax.all_gather(v_blocks, "seq", axis=1, tiled=True),
    )

    def forward_block(pieces):
        return attend(pieces, score_scale, group_count, HD)

    attended, row_max, row_sum = lax.map(forward_block, (q_blocks, key_all, value_all, allowed))
    att_low = attended.reshape(micro_count * block_len, -1).astype(jnp.bfloat16)
    attn_proj = product(att_low, w_out)
    attn_normed, attn_hat, attn_factor = rms_forward(attn_proj, attn_gain)
    hidden = flat_tokens.astype(jnp.float32) + attn_normed
    hidden_low = hidden.astype(jnp.bfloat16)
    gate_pre = product(hidden_low, w_gate)
    up_pre = product(hidden_low, w_up)
    mixed_low = (jax.nn.silu(gate_pre) * up_pre).astype(jnp.bfloat16)
    down_pre = product(mixed_low, w_down)
    down_normed, down_hat, down_factor = rms_forward(down_pre, mlp_gain)
    layer_out = (hidden + down_normed).astype(jnp.bfloat16).reshape(tokens.shape)
    down_grad, grad_mlp_gain = rms_backward(out_grad, mlp_gain, down_hat, down_factor)
    down_grad = down_grad.astype(jnp.bfloat16)
    grad_w_down = weight_grad(mixed_low, down_grad)
    mixed_grad = back_product(down_grad, w_down)
    sigmoid_gate = jax.nn.sigmoid(gate_pre)
    gate_grad = (
        mixed_grad * up_pre * sigmoid_gate * (1.0 + gate_pre * (1.0 - sigmoid_gate))
    ).astype(jnp.bfloat16)
    up_grad = (mixed_grad * gate_pre * sigmoid_gate).astype(jnp.bfloat16)
    grad_w_gate = weight_grad(hidden_low, gate_grad)
    grad_w_up = weight_grad(hidden_low, up_grad)
    hidden_grad = out_grad + back_product(gate_grad, w_gate) + back_product(up_grad, w_up)
    proj_grad, grad_attn_gain = rms_backward(hidden_grad, attn_gain, attn_hat, attn_factor)
    proj_grad = proj_grad.astype(jnp.bfloat16)
    grad_w_out = weight_grad(att_low, proj_grad)
    att_grad = back_product(proj_grad, w_out).astype(jnp.bfloat16)
    grad_blocks = att_grad.reshape(micro_count, block_len, -1)
    key_back, value_back = (key_all, value_all)

    def query_pass(pieces):
        q_rows, grad_rows, key_rows, value_rows, mask_rows, max_rows, sum_rows = pieces

        def query_one_group(parts):
            q_group, grad_group, k_group, v_group, max_group, sum_group = parts
            prob_low, score_grad, unused = score_grads(
                q_group,
                grad_group,
                k_group,
                v_group,
                mask_rows,
                max_group,
                sum_group,
                None,
                score_scale,
            )
            q_grad = (
                jnp.einsum("rtu,ud->trd", score_grad, k_group, preferred_element_type=jnp.float32)
                * score_scale
            )
            key_terms = (
                jnp.einsum("rtu,trd->ud", score_grad, q_group, preferred_element_type=jnp.float32)
                * score_scale
            )
            value_terms = jnp.einsum(
                "rtu,trd->ud", prob_low, grad_group, preferred_element_type=jnp.float32
            )
            return (q_grad, key_terms, value_terms)

        q_grad, key_terms, value_terms = lax.map(
            query_one_group,
            (
                heads_first(q_rows, group_count, HD),
                heads_first(grad_rows, group_count, HD),
                kv_first(key_rows, group_count, HD),
                kv_first(value_rows, group_count, HD),
                max_rows,
                sum_rows,
            ),
        )
        q_grad = jnp.moveaxis(q_grad, 0, 1).reshape(block_len, -1)
        key_terms = jnp.moveaxis(key_terms, 0, 1).reshape(seq_length, -1)
        value_terms = jnp.moveaxis(value_terms, 0, 1).reshape(seq_length, -1)
        key_own, value_own = (
            lax.psum_scatter(key_terms, "seq", scatter_dimension=0, tiled=True),
            lax.psum_scatter(value_terms, "seq", scatter_dimension=0, tiled=True),
        )
        return (q_grad, key_own, value_own)

    q_rot_grad, k_rot_grad, value_grad = lax.map(
        query_pass, (q_blocks, grad_blocks, key_back, value_back, allowed, row_max, row_sum)
    )
    q_rot_grad = q_rot_grad.reshape(micro_count * block_len, -1)
    k_rot_grad = k_rot_grad.reshape(micro_count * block_len, -1)
    v_grad = value_grad.reshape(micro_count * block_len, -1).astype(jnp.bfloat16)
    q_norm_grad = rotate(q_rot_grad, cos_table, sine_table, head_count, -1.0)
    k_norm_grad = rotate(k_rot_grad, cos_table, sine_table, group_count, -1.0)
    q_grad, grad_q_gain = rms_backward(q_norm_grad, q_gain, q_hat, q_factor)
    k_grad, grad_k_gain = rms_backward(k_norm_grad, k_gain, k_hat, k_factor)
    q_grad = q_grad.astype(jnp.bfloat16)
    k_grad = k_grad.astype(jnp.bfloat16)
    grad_w_query = weight_grad(flat_tokens, q_grad)
    grad_w_key = weight_grad(flat_tokens, k_grad)
    grad_w_value = weight_grad(flat_tokens, v_grad)
    input_grad = (
        hidden_grad
        + back_product(q_grad, w_query)
        + back_product(k_grad, w_key)
        + back_product(v_grad, w_value)
    )
    input_grad = input_grad.reshape(tokens.shape)
    summed = (
        lax.psum_scatter(grad_w_query, ("dp", "seq"), scatter_dimension=0, tiled=True),
        lax.psum_scatter(grad_w_key, ("dp", "seq"), scatter_dimension=0, tiled=True),
        lax.psum_scatter(grad_w_value, ("dp", "seq"), scatter_dimension=0, tiled=True),
        lax.psum_scatter(grad_w_out, ("dp", "seq"), scatter_dimension=0, tiled=True),
        lax.psum_scatter(grad_q_gain, ("dp", "seq"), scatter_dimension=0, tiled=True),
        lax.psum_scatter(grad_k_gain, ("dp", "seq"), scatter_dimension=0, tiled=True),
        lax.psum_scatter(grad_attn_gain, ("dp", "seq"), scatter_dimension=0, tiled=True),
        lax.psum_scatter(grad_w_gate, ("dp", "seq"), scatter_dimension=0, tiled=True),
        lax.psum_scatter(grad_w_up, ("dp", "seq"), scatter_dimension=0, tiled=True),
        lax.psum_scatter(grad_w_down, ("dp", "seq"), scatter_dimension=0, tiled=True),
        lax.psum_scatter(grad_mlp_gain, ("dp", "seq"), scatter_dimension=0, tiled=True),
    )
    return (
        layer_out,
        input_grad,
        summed[0],
        summed[1],
        summed[2],
        summed[3],
        summed[4],
        summed[5],
        summed[6],
        summed[7],
        summed[8],
        summed[9],
        summed[10],
    )


def split_by_heads(
    tokens, cotangent, w_query, w_key, w_value, w_out, q_gain, k_gain, attn_gain,
    w_gate, w_up, w_down, mlp_gain, doc_lengths, block_order,
):
    rope = rope_constant(1024)
    q_gain_rows, k_gain_rows = q_gain.reshape(16, HD), k_gain.reshape(8, HD)
    own_tokens = tokens[:, 0]
    layer_out, in_grad, g_query, g_key, g_value, g_out, vec, gains, g_gate, g_up, g_down = whole_layer(
        own_tokens, cotangent[:, 0], attn_gain[None], mlp_gain[None], q_gain_rows, k_gain_rows,
        rope, w_out, w_gate, w_up, w_down, w_query, w_key, w_value, block_order, doc_lengths,
    )
    (
        layer_out, in_grad, g_query, g_key, g_value, g_out, g_gate, g_up, g_down,
        g_q_gain, g_k_gain, g_attn_gain, g_mlp_gain,
    ) = finish((layer_out, in_grad, g_query, g_key, g_value, g_out, g_gate, g_up, g_down), vec, gains)
    return (
        layer_out.reshape(tokens.shape),
        in_grad.reshape(tokens.shape),
        g_query,
        g_key,
        g_value,
        g_out,
        g_q_gain[0],
        g_k_gain[0],
        g_attn_gain[0],
        g_gate,
        g_up,
        g_down,
        g_mlp_gain[0],
    )


SPECS_IN = (
    P(None, "dp", "seq", None), P(None, "dp", "seq", None),
    P(), P(), P(), P(), P(), P(), P(), P(), P(), P(), P(),
    P(None, "dp", None), P(),
)
SPECS_OUT = (
    P(None, "dp", "seq", None), P(None, "dp", "seq", None),
    P(("dp", "seq"), None), P(("dp", "seq"), None), P(("dp", "seq"), None), P(("dp", "seq"), None),
    P(("dp", "seq")), P(("dp", "seq")), P(("dp", "seq")),
    P(("dp", "seq"), None), P(("dp", "seq"), None), P(("dp", "seq"), None),
    P(("dp", "seq")),
)


def solution(mesh):
    body = split_by_heads if mesh.shape["seq"] == 16 and mesh.shape["dp"] == 2 else on_device
    return jax.shard_map(body, mesh=mesh, in_specs=SPECS_IN, out_specs=SPECS_OUT, check_vma=False)
```
